32 devices in a mesh: rep: 4 (over y, x), shard: 8 (over z, core).
Axes of the slice: x: 2, y: 2, z: 4, core: 2. Of those that a mesh axis runs over, the one named last changes fastest.
Arguments:
- layer_in: bfloat16 [8, 1024, 1024], P('shard', 'rep'), may hold values from -6 to 6
- out_grad: bfloat16 [8, 1024, 1024], P('shard', 'rep'), may hold values from -6 to 6
- attn_norm: bfloat16 [1024], P('shard'), may hold values from 0.099609375 to 1.8984375
- query_weight: bfloat16 [1024, 2048], P('shard'), may hold values from -0.1875 to 0.1875
- key_projection: bfloat16 [1024, 1024], P('shard'), may hold values from -0.1875 to 0.1875
- value_projection: bfloat16 [1024, 1024], P('shard'), may hold values from -0.1875 to 0.1875
- query_norm: bfloat16 [128], P('shard'), may hold values from 1 to 2
- key_norm: bfloat16 [128], P('shard'), may hold values from 1 to 2
- out_weight: bfloat16 [2048, 1024], P('shard'), may hold values from -2 to 2
- mlp_norm: bfloat16 [1024], P('shard'), may hold values from 0.099609375 to 1.8984375
- gate_weight: bfloat16 [1024, 3072], P('shard'), may hold values from -0.1875 to 0.1875
- up_weight: bfloat16 [1024, 3072], P('shard'), may hold values from -0.1875 to 0.1875
- down_weight: bfloat16 [3072, 1024], P('shard'), may hold values from -0.109375 to 0.109375
- picture_starts: int32 [8, 3], P('shard'), may hold values from 0 to 768, as said below
- picture_count: int32 [8], P('shard'), may hold values from 1 to 3
Outputs:
- layer_out: bfloat16 [8, 1024, 1024], P('shard', 'rep')
- in_grad: bfloat16 [8, 1024, 1024], P('shard', 'rep')
- attn_norm_grad: float32 [1024], P('shard')
- query_weight_grad: float32 [1024, 2048], P('shard')
- key_weight_grad: float32 [1024, 1024], P('shard')
- value_weight_grad: float32 [1024, 1024], P('shard')
- query_norm_grad: float32 [128], P('shard')
- key_norm_grad: float32 [128], P('shard')
- out_weight_grad: float32 [2048, 1024], P('shard')
- mlp_norm_grad: float32 [1024], P('shard')
- gate_weight_grad: float32 [1024, 3072], P('shard')
- up_weight_grad: float32 [1024, 3072], P('shard')
- down_weight_grad: float32 [3072, 1024], P('shard')
The draws below stay inside these ranges and needn't reach their ends.
Inputs may be any that keep to these rules, and one draw needn't show every extreme that they name: `picture_starts`: in row b the entries 0 to picture_count[b] - 1 are distinct multiples of 256 in increasing order; the other entries are ignored.
All inputs are finite; a program needn't handle non-finite values.
Results may differ from the reference program's by a relative error of at most 0.023.
Values may be sent and summed in bfloat16 or wider, within the bound.
No kernel may reach another device: no remote copies, remote signals or barrier semaphores. Data moves between devices by JAX's collectives and lax.ppermute only.
A program may use at most 192 MiB of HBM per device.

```python
import jax
import jax.numpy as jnp
from jax import lax

MODEL_WIDTH = 1024
FF = 3072
QUERY_HEADS = 16
KEY_VALUE_HEADS = 8
HEAD_SIZE = 128
PIECE = 256
PIECES = 3
SEQUENCE_LENGTH = 1024
BATCH = 8


def picture_layout(key):
    key = jax.random.fold_in(key, 11)
    count_key, slot_key, pick_key = jax.random.split(key, 3)
    slot_total = SEQUENCE_LENGTH // PIECE
    counts = jax.random.randint(count_key, (BATCH,), 1, PIECES + 1)
    chosen = jax.random.randint(pick_key, (), 0, BATCH)
    counts = jnp.where(jnp.arange(BATCH) == chosen, PIECES, counts)
    row_keys = jax.random.split(slot_key, BATCH)
    orders = jax.vmap(lambda row_key: jax.random.permutation(row_key, slot_total))(row_keys)
    starts = jnp.sort(orders[:, :PIECES], axis=1) * PIECE
    return (starts.astype(jnp.int32), counts.astype(jnp.int32))


def draw_picture_starts(key, part):
    return picture_layout(key)[0]


def draw_picture_count(key, part):
    return picture_layout(key)[1]


def steps_of(own_key, shape, cuts, least, top_value):
    factor_of = 1.0
    for dim, blocks in cuts:
        steps = jax.random.uniform(jax.random.fold_in(jax.random.fold_in(own_key, 6), dim), (blocks,), jnp.float32, least / len(cuts), top_value / len(cuts))
        factor_of = factor_of * jnp.repeat(jnp.exp(steps), shape[dim] // blocks).reshape((-1,) + (1,) * (len(shape) - 1 - dim))
    return factor_of


def noise(key, extent, spread, most, cuts=(), kind=jnp.bfloat16):
    drawn = spread * jax.random.normal(key, extent, jnp.float32)
    if cuts:
        drawn = drawn * steps_of(key, extent, cuts, -0.22, 0.18)
    return jnp.clip(drawn, -most, most).astype(kind)


def setup_inputs(seed: int = 0) -> dict:
    streams_of = jax.random.split(jax.random.key(seed), 16)
    return {
        "layer_in": noise(streams_of[0], (BATCH, SEQUENCE_LENGTH, MODEL_WIDTH), 1.0, 6.0, ((0, 8), (1, 4))),
        "out_grad": noise(streams_of[1], (BATCH, SEQUENCE_LENGTH, MODEL_WIDTH), 1.0, 6.0, ((0, 8), (1, 4))),
        "attn_norm": jnp.clip(1.0 + 0.18 * jax.random.normal(streams_of[2], (MODEL_WIDTH,), jnp.float32), 0.099609375, 1.8984375).astype(jnp.bfloat16),
        "query_weight": noise(streams_of[3], (MODEL_WIDTH, QUERY_HEADS * HEAD_SIZE), MODEL_WIDTH ** -0.5, 0.1875, ((0, 8),)),
        "key_projection": noise(streams_of[4], (MODEL_WIDTH, KEY_VALUE_HEADS * HEAD_SIZE), MODEL_WIDTH ** -0.5, 0.1875, ((0, 8),)),
        "value_projection": noise(streams_of[5], (MODEL_WIDTH, KEY_VALUE_HEADS * HEAD_SIZE), MODEL_WIDTH ** -0.5, 0.1875, ((0, 8),)),
        "query_norm": jnp.clip(1.0 + 1.0 * jax.random.uniform(streams_of[6], (HEAD_SIZE,), jnp.float32) ** steps_of(streams_of[6], (HEAD_SIZE,), ((0, 8),), -0.2, 0.2), 1.0, 2.0).astype(jnp.bfloat16),
        "key_norm": jnp.clip(1.0 + 1.0 * jax.random.uniform(streams_of[7], (HEAD_SIZE,), jnp.float32) ** steps_of(streams_of[7], (HEAD_SIZE,), ((0, 8),), -0.2, 0.2), 1.0, 2.0).astype(jnp.bfloat16),
        "out_weight": noise(streams_of[8], (QUERY_HEADS * HEAD_SIZE, MODEL_WIDTH), (max(1, QUERY_HEADS * HEAD_SIZE * 4 // SEQUENCE_LENGTH)) ** -0.5, 2.0, ((0, 8),)),
        "mlp_norm": jnp.clip(1.0 + 0.18 * jax.random.normal(streams_of[9], (MODEL_WIDTH,), jnp.float32), 0.099609375, 1.8984375).astype(jnp.bfloat16),
        "gate_weight": noise(streams_of[10], (MODEL_WIDTH, FF), MODEL_WIDTH ** -0.5, 0.1875, ((0, 8),)),
        "up_weight": noise(streams_of[11], (MODEL_WIDTH, FF), MODEL_WIDTH ** -0.5, 0.1875, ((0, 8),)),
        "down_weight": noise(streams_of[12], (FF, MODEL_WIDTH), FF ** -0.5, 0.109375, ((0, 8),)),
        "picture_starts": draw_picture_starts(jax.random.fold_in(streams_of[15], 71), 0),
        "picture_count": draw_picture_count(jax.random.fold_in(streams_of[15], 71), 0),
    }


EPSILON = 1e-06
ROPE_BASE = 1000000.0

@jax.custom_vjp
def lowered_input(v):
    return lax.optimization_barrier(v.astype(jnp.bfloat16)).astype(jnp.float32)

@jax.custom_vjp
def lowered_backward(v):
    return v

def low_keep(v):
    return (lowered_input(v), None)

def low_pass(kept, grad):
    return (grad,)

def back_keep(v):
    return (v, None)

def back_low(kept, grad):
    return (lowered_input(grad),)
lowered_input.defvjp(low_keep, low_pass)
lowered_backward.defvjp(back_keep, back_low)

def root_mean_scale(values, gain_row):
    return values * lax.rsqrt(lax.optimization_barrier(jnp.mean(values * values, axis=-1, keepdims=True)) + EPSILON) * gain_row

def apply_rotary(values, token_positions):
    half_width = values.shape[-1] // 2
    inv_freq = ROPE_BASE ** (-2.0 * jnp.arange(half_width, dtype=jnp.float32) / values.shape[-1])
    angles = token_positions.astype(jnp.float32)[:, None] * inv_freq[None, :]
    cosine = jnp.cos(angles)[:, None, :]
    sine = jnp.sin(angles)[:, None, :]
    front_part = values[..., :half_width]
    back_part = values[..., half_width:]
    return jnp.concatenate([front_part * cosine - back_part * sine, back_part * cosine + front_part * sine], axis=-1)

def piece_ids(token_positions, picture_piece_starts, picture_piece_count):
    slot_ids = jnp.arange(picture_piece_starts.shape[0], dtype=jnp.int32)
    inside = (token_positions[:, None] >= picture_piece_starts[None, :]) & (token_positions[:, None] < picture_piece_starts[None, :] + PIECE) & (slot_ids[None, :] < picture_piece_count)
    return lax.optimization_barrier(jnp.sum(jnp.where(inside, slot_ids[None, :] + 1, 0), axis=1)).astype(jnp.int32)

def attention_layer(rotated_query, rotated_key, value_row_list, picture_piece_starts, picture_piece_count):
    token_positions = jnp.arange(SEQUENCE_LENGTH, dtype=jnp.int32)
    key_piece = piece_ids(token_positions, picture_piece_starts, picture_piece_count)
    head_keys = jnp.repeat(rotated_key, QUERY_HEADS // KEY_VALUE_HEADS, axis=1)
    head_values = jnp.repeat(value_row_list, QUERY_HEADS // KEY_VALUE_HEADS, axis=1)
    block_rows = min(SEQUENCE_LENGTH, 512)
    score_scale = HEAD_SIZE ** (-0.5)

    def one_block(block_index):
        first_row = (block_index * block_rows).astype(jnp.int32)
        query_rows = lax.dynamic_slice_in_dim(rotated_query, first_row, block_rows, 0)
        query_pos = first_row + jnp.arange(block_rows, dtype=jnp.int32)
        query_piece = lax.dynamic_slice_in_dim(key_piece, first_row, block_rows, 0)
        raw_scores = jnp.einsum('qhd,khd->hqk', query_rows, head_keys, precision=lax.Precision.HIGHEST)
        scores = lowered_backward(raw_scores) * score_scale
        allowed = (token_positions[None, :] <= query_pos[:, None]) | (query_piece[:, None] > 0) & (query_piece[:, None] == key_piece[None, :])
        scores = jnp.where(allowed[None], scores, -1e+30)
        probabilities = lowered_input(jax.nn.softmax(scores, axis=-1))
        return jnp.einsum('hqk,khd->qhd', probabilities, head_values, precision=lax.Precision.HIGHEST)
    blocks = lax.map(jax.checkpoint(one_block), jnp.arange(SEQUENCE_LENGTH // block_rows, dtype=jnp.int32))
    return blocks.reshape(SEQUENCE_LENGTH, QUERY_HEADS * HEAD_SIZE)

def layer_forward(tokens, attn_gain, query_matrix, key_matrix, value_matrix, query_gain, key_norm_scale, out_matrix, mlp_gain, gate_matrix, up_matrix, down_matrix, picture_piece_starts, picture_piece_count):
    highest = lax.Precision.HIGHEST
    token_positions = jnp.arange(SEQUENCE_LENGTH, dtype=jnp.int32)
    normed = lowered_input(root_mean_scale(tokens, attn_gain))
    query_raw = lowered_backward(jnp.dot(normed, query_matrix, precision=highest, preferred_element_type=jnp.float32))
    unrotated_key = lowered_backward(jnp.dot(normed, key_matrix, precision=highest, preferred_element_type=jnp.float32))
    value_row_list = lowered_input(lowered_backward(jnp.dot(normed, value_matrix, precision=highest, preferred_element_type=jnp.float32)))
    rotated_query = lowered_input(apply_rotary(root_mean_scale(query_raw.reshape(SEQUENCE_LENGTH, QUERY_HEADS, HEAD_SIZE), query_gain), token_positions))
    rotated_key = lowered_input(apply_rotary(root_mean_scale(unrotated_key.reshape(SEQUENCE_LENGTH, KEY_VALUE_HEADS, HEAD_SIZE), key_norm_scale), token_positions))
    mixed_head_rows = lowered_input(lowered_backward(attention_layer(rotated_query, rotated_key, value_row_list.reshape(SEQUENCE_LENGTH, KEY_VALUE_HEADS, HEAD_SIZE), picture_piece_starts, picture_piece_count)))
    after_attn = tokens + lowered_backward(jnp.dot(mixed_head_rows, out_matrix, precision=highest, preferred_element_type=jnp.float32))
    mlp_in = lowered_input(root_mean_scale(after_attn, mlp_gain))
    gate_act = lowered_backward(jnp.dot(mlp_in, gate_matrix, precision=highest, preferred_element_type=jnp.float32))
    up_act = lowered_backward(jnp.dot(mlp_in, up_matrix, precision=highest, preferred_element_type=jnp.float32))
    hidden = lowered_input(jax.nn.silu(gate_act) * up_act)
    return after_attn + lowered_backward(jnp.dot(hidden, down_matrix, precision=highest, preferred_element_type=jnp.float32))

def reference(layer_in, out_grad, attn_norm, query_weight, key_projection, value_projection, query_norm, key_norm, out_weight, mlp_norm, gate_weight, up_weight, down_weight, picture_starts, picture_count):
    weight_list = tuple((weight_arg.astype(jnp.float32) for weight_arg in (attn_norm, query_weight, key_projection, value_projection, query_norm, key_norm, out_weight, mlp_norm, gate_weight, up_weight, down_weight)))

    def one_sequence(totals, sequence_items):
        tokens, cotangent, picture_piece_starts, picture_piece_count = sequence_items

        def forward(token_value, *weight_args):
            return layer_forward(token_value, *weight_args, picture_piece_starts, picture_piece_count)
        result, pull_back = jax.vjp(forward, tokens.astype(jnp.float32), *weight_list)
        gradients = pull_back(cotangent.astype(jnp.float32))
        new_totals = tuple((total_grad + new_grad for total_grad, new_grad in zip(totals, gradients[1:])))
        return (new_totals, (result.astype(jnp.bfloat16), gradients[0].astype(jnp.bfloat16)))
    zero_grads = tuple((jnp.zeros(weight_arg.shape, jnp.float32) for weight_arg in weight_list))
    totals, outputs = lax.scan(one_sequence, zero_grads, (layer_in, out_grad, picture_starts, picture_count))
    return (outputs[0], outputs[1], totals[0], totals[1], totals[2], totals[3], totals[4], totals[5], totals[6], totals[7], totals[8], totals[9], totals[10])
```

```python
import jax
import jax.numpy as jnp
from jax import lax
from jax.experimental import pallas as pl
from jax.experimental.pallas import tpu as pltpu
from jax.sharding import PartitionSpec as P

MODEL_WIDTH = 1024
QUERY_HEADS = 16
KEY_VALUE_HEADS = 8
HEAD_SIZE = 128
GROUP = QUERY_HEADS // KEY_VALUE_HEADS
PIECE = 256

EPSILON = 1e-06
ROPE_BASE = 1000000.0
SCALE = HEAD_SIZE ** (-0.5)
LOG2E = 1.4426950408889634
BF = jnp.bfloat16
F32 = jnp.float32


def mm(a, b, dims=((1,), (0,))):
    return lax.dot_general(a, b, (dims, ((), ())), preferred_element_type=F32)


def flip(value, bit):
    count = lax.axis_size("rep")
    return lax.ppermute(value, "rep", [(i, i ^ bit) for i in range(count)])


def spread_blocks(value):
    count = lax.axis_size("rep")
    if count == 4:
        half = value.shape[0] // 2
        by_one, by_two = flip(value, 1), flip(value, 2)
        low, high = flip(by_one[:half], 2), flip(by_two[half:], 1)
        return jnp.stack([value, by_one, by_two, jnp.concatenate([low, high], axis=0)])
    blocks = value[None]
    bit = 1
    while bit < count:
        blocks = jnp.concatenate([blocks, flip(blocks, bit)], axis=0)
        bit *= 2
    return blocks


def sum_blocks(parts):
    count = lax.axis_size("rep")
    if count == 4:
        half = parts.shape[1] // 2
        a, b = parts[:, :half], parts[:, half:]
        a_in = flip(jnp.stack([a[1], a[3]]).astype(BF), 1).astype(F32)
        b_in = flip(jnp.stack([b[2], b[3]]).astype(BF), 2).astype(F32)
        a_last = flip((a[2] + a_in[1]).astype(BF), 2).astype(F32)
        b_last = flip((b[1] + b_in[1]).astype(BF), 1).astype(F32)
        return jnp.concatenate([a[0] + a_in[0] + a_last, b[0] + b_in[0] + b_last], axis=0)
    bit = count // 2
    while bit:
        parts = parts[:bit] + flip(parts[bit:].astype(BF), bit).astype(F32)
        bit //= 2
    return parts[0]


def ring_up(value):
    count = lax.axis_size("shard")
    return lax.ppermute(value, "shard", [(i, (i + 2) % count) for i in range(count)])


def other_core(value):
    count = lax.axis_size("shard")
    return lax.ppermute(value, "shard", [(i, i ^ 1) for i in range(count)])


def gather_rows(value):
    count = lax.axis_size("shard")
    chips = count // 2
    index = lax.axis_index("shard")
    chip, core = index // 2, index % 2
    full = jnp.zeros((count,) + value.shape, value.dtype)
    current = value
    for step in range(chips):
        if step:
            current = ring_up(current)
        place = 2 * ((chip + chips - step) % chips)
        full = lax.dynamic_update_index_in_dim(full, current, place + core, 0)
        full = lax.dynamic_update_index_in_dim(full, other_core(current), place + 1 - core, 0)
    return full, current


def scatter_rows(parts):
    count = lax.axis_size("shard")
    chips = count // 2
    index = lax.axis_index("shard")
    chip, core = index // 2, index % 2
    by_chip = parts.reshape((chips, 2) + parts.shape[1:])
    away = lax.dynamic_index_in_dim(by_chip, 1 - core, 1, keepdims=False).astype(BF)
    kept = lax.dynamic_index_in_dim(by_chip, core, 1, keepdims=False)
    paired = kept + other_core(away).astype(F32)

    def own(step):
        return lax.dynamic_index_in_dim(paired, (chip + 2 * chips - step) % chips, 0, keepdims=False)

    running = own(1)
    for step in range(1, chips):
        running = ring_up(running.astype(BF)).astype(F32) + own(step + 1)
    return running


def joint_move(value, pairs):
    shards = lax.axis_size("shard")
    joint = [
        (r0 * shards + 2 * z0 + c, r1 * shards + 2 * z1 + c)
        for (r0, z0), (r1, z1) in pairs
        for c in range(2)
    ]
    return lax.ppermute(value, ("rep", "shard"), joint)


def gather_heads(value):
    replicas, shards = lax.axis_size("rep"), lax.axis_size("shard")
    r, index = lax.axis_index("rep"), lax.axis_index("shard")
    if shards != 2 * replicas:
        full = lax.all_gather(value, "shard", axis=0, tiled=True)
        rows = full.shape[0] // replicas
        return lax.dynamic_slice_in_dim(full, r * rows, rows, 0)
    chip, core = index // 2, index % 2
    up = [((i, z), (i, z + 1)) for i in range(replicas) for z in range(i, replicas - 1)]
    down = [((i, z), (i, z - 1)) for i in range(replicas) for z in range(1, i + 1)]
    moved_up = joint_move(value, [p for p in up if p[0][1] == p[0][0]])
    moved_down = joint_move(value, [p for p in down if p[0][1] == p[0][0]])
    total = moved_up + moved_down
    result = jnp.where(chip == r, value, total)
    moved = total
    for hop in range(2, replicas):
        pairs = [p for p in up if p[0][1] - p[0][0] == hop - 1]
        pairs += [p for p in down if p[0][0] - p[0][1] == hop - 1]
        moved = joint_move(moved, pairs)
        result = result + moved
    other = other_core(result)
    first = jnp.where(core == 0, result, other)
    second = jnp.where(core == 0, other, result)
    return jnp.concatenate([first, second], axis=0)


def scatter_heads(parts):
    replicas, shards = lax.axis_size("rep"), lax.axis_size("shard")
    r, index = lax.axis_index("rep"), lax.axis_index("shard")
    if shards != 2 * replicas:
        rows = parts.shape[0]
        full = jnp.zeros((rows * replicas,) + parts.shape[1:], F32)
        full = lax.dynamic_update_slice_in_dim(full, parts, r * rows, 0)
        owned = lax.psum_scatter(full.astype(BF), "shard", scatter_dimension=0, tiled=True)
        return lax.psum(owned, "rep").astype(F32)
    chip, core = index // 2, index % 2
    halves = parts.reshape((2, -1) + parts.shape[1:])
    away = lax.dynamic_index_in_dim(halves, 1 - core, 0, keepdims=False).astype(BF)
    total = lax.dynamic_index_in_dim(halves, core, 0, keepdims=False) + other_core(away).astype(F32)
    low = total.astype(BF)
    for hop in range(1, replicas):
        pairs = [((i, (i + hop) % replicas), (i, i)) for i in range(replicas)]
        total = total + joint_move(low, pairs).astype(F32)
    low = total.astype(BF)
    if replicas == 4:
        half = low.shape[0] // 2
        one = joint_move(low, [((z, z), (z ^ 1, z)) for z in range(4)])
        two = joint_move(low, [((z, z), (z ^ 2, z)) for z in range(4)])
        top = joint_move(one[:half], [((z ^ 1, z), (z ^ 3, z)) for z in range(4)])
        bottom = joint_move(two[half:], [((z ^ 2, z), (z ^ 3, z)) for z in range(4)])
        rest = one + two + jnp.concatenate([top, bottom], axis=0)
    else:
        rest = jnp.zeros_like(low)
        for other in range(1, replicas):
            rest = rest + joint_move(low, [((z, z), ((z + other) % replicas, z)) for z in range(replicas)])
    return jnp.where(chip == r, low, rest).astype(F32)


def piece_mask(picture_flag, size, heads):
    key = lax.broadcasted_iota(jnp.int32, (size, size * heads), 0)
    query = lax.broadcasted_iota(jnp.int32, (size, size * heads), 1) % size
    return (key <= query) | (picture_flag > 0)


def attention_forward_kernel(info, q_ref, k_ref, v_ref, mixed_ref, lse_ref):
    blocks, size = k_ref.shape[0], k_ref.shape[1]
    own = info[0]
    for last in range(blocks):
        i = own ^ last
        query = jnp.concatenate(
            [q_ref[i, :, h * HEAD_SIZE : (h + 1) * HEAD_SIZE] for h in range(GROUP)], axis=0
        )
        total = jnp.zeros((1, GROUP * size), F32)
        mixed = jnp.zeros((HEAD_SIZE, GROUP * size), F32)
        for block in range(last + 1):
            j = own ^ block
            scores = mm(k_ref[j], query, ((1,), (1,)))
            weights = jnp.exp2(scores * (SCALE * LOG2E))
            if block == last:
                weights = jnp.where(piece_mask(info[1 + i], size, GROUP), weights, 0.0)
            total = total + jnp.sum(weights, axis=0, keepdims=True)
            mixed = mixed + mm(v_ref[j], weights.astype(BF), ((0,), (0,)))
        mixed = mixed * (1.0 / total)
        log_sum = jnp.log2(total)
        for h in range(GROUP):
            columns = slice(h * size, (h + 1) * size)
            mixed_ref[i, :, h * HEAD_SIZE : (h + 1) * HEAD_SIZE] = mixed[:, columns].T.astype(BF)
            lse_ref[i, h : h + 1, :] = log_sum[:, columns]


def attention_backward_kernel(
    info, q_ref, k_ref, v_ref, mixed_ref, lse_ref, grad_ref, dq_ref, dk_ref, dv_ref
):
    blocks, size = k_ref.shape[0], k_ref.shape[1]
    own = info[0]
    dk_ref[...] = jnp.zeros_like(dk_ref)
    dv_ref[...] = jnp.zeros_like(dv_ref)
    for last in range(blocks):
        i = own ^ last
        heads = [slice(h * HEAD_SIZE, (h + 1) * HEAD_SIZE) for h in range(GROUP)]
        query = jnp.concatenate([q_ref[i, :, h] for h in heads], axis=0)
        grad = jnp.concatenate([grad_ref[i, :, h] for h in heads], axis=0)
        mixed = jnp.concatenate([mixed_ref[i, :, h] for h in heads], axis=0)
        delta = jnp.sum((grad.astype(F32) * mixed.astype(F32)).T, axis=0, keepdims=True)
        log_sum = jnp.concatenate([lse_ref[i, h : h + 1, :] for h in range(GROUP)], axis=1)
        dquery = jnp.zeros((HEAD_SIZE, GROUP * size), F32)
        for block in range(last + 1):
            j = own ^ block
            scores = mm(k_ref[j], query, ((1,), (1,)))
            dprobs = mm(v_ref[j], grad, ((1,), (1,)))
            probs = jnp.exp2(scores * (SCALE * LOG2E) - log_sum)
            if block == last:
                probs = jnp.where(piece_mask(info[1 + i], size, GROUP), probs, 0.0)
            dscores = (probs * (dprobs - delta)).astype(BF)
            dv_ref[j] += mm(probs.astype(BF), grad)
            dk_ref[j] += mm(dscores, query)
            dquery = dquery + mm(k_ref[j], dscores, ((0,), (0,)))
        for h in range(GROUP):
            dq_ref[i, :, heads[h]] = dquery[:, h * size : (h + 1) * size].T * SCALE
    dk_ref[...] = dk_ref[...] * SCALE


def attention_specs(blocks, size):
    wide = pl.BlockSpec((blocks, size, GROUP * HEAD_SIZE), lambda g, info: (0, 0, g))
    thin = pl.BlockSpec((blocks, size, HEAD_SIZE), lambda g, info: (0, 0, g))
    rows = pl.BlockSpec((None, blocks, GROUP, size), lambda g, info: (g, 0, 0, 0))
    return wide, thin, rows


def attention_forward(info, query, key, value):
    blocks, size, width = key.shape
    groups = width // HEAD_SIZE
    wide, thin, rows = attention_specs(blocks, size)
    return pl.pallas_call(
        attention_forward_kernel,
        grid_spec=pltpu.PrefetchScalarGridSpec(
            num_scalar_prefetch=1,
            grid=(groups,),
            in_specs=[wide, thin, thin],
            out_specs=[wide, rows],
        ),
        out_shape=[
            jax.ShapeDtypeStruct(query.shape, BF),
            jax.ShapeDtypeStruct((groups, blocks, GROUP, size), F32),
        ],
        compiler_params=pltpu.CompilerParams(vmem_limit_bytes=48 << 20),
        name="attention_forward",
    )(info, query, key, value)


def attention_backward(info, query, key, value, mixed, lse, grad):
    blocks, size, width = key.shape
    groups = width // HEAD_SIZE
    wide, thin, rows = attention_specs(blocks, size)
    return pl.pallas_call(
        attention_backward_kernel,
        grid_spec=pltpu.PrefetchScalarGridSpec(
            num_scalar_prefetch=1,
            grid=(groups,),
            in_specs=[wide, thin, thin, wide, rows, wide],
            out_specs=[wide, thin, thin],
        ),
        out_shape=[
            jax.ShapeDtypeStruct(query.shape, F32),
            jax.ShapeDtypeStruct(key.shape, F32),
            jax.ShapeDtypeStruct(key.shape, F32),
        ],
        compiler_params=pltpu.CompilerParams(vmem_limit_bytes=48 << 20),
        name="attention_backward",
    )(info, query, key, value, mixed, lse, grad)


def inverse_root(values):
    return lax.rsqrt(jnp.mean(values * values, axis=-1, keepdims=True) + EPSILON)


def norm_back(values, inverse, gain, dy):
    weighted = dy * gain
    inner = jnp.mean(values * weighted, axis=-1, keepdims=True)
    return inverse * weighted - values * (inverse * inverse * inverse) * inner


def turn(values):
    return jnp.concatenate([values[..., HEAD_SIZE // 2 :], values[..., : HEAD_SIZE // 2]], axis=-1)


def per_device(
    layer_in,
    out_grad,
    attn_norm,
    query_weight,
    key_projection,
    value_projection,
    query_norm,
    key_norm,
    out_weight,
    mlp_norm,
    gate_weight,
    up_weight,
    down_weight,
    picture_starts,
    picture_count,
):
    replicas, shards = lax.axis_size("rep"), lax.axis_size("shard")
    r = lax.axis_index("rep")
    size = layer_in.shape[1]
    length = size * replicas
    rows = attn_norm.shape[0]
    q_width = QUERY_HEADS // replicas * HEAD_SIZE
    kv_width = KEY_VALUE_HEADS // replicas * HEAD_SIZE
    attn_width = q_width + 2 * kv_width
    ff_rows = down_weight.shape[0] // replicas
    ff = ff_rows * shards

    def columns_of(weight, width):
        return lax.dynamic_slice_in_dim(weight, r * width, width, 1)

    gains = jnp.concatenate([attn_norm, mlp_norm, query_norm, key_norm])
    head_rows = query_norm.shape[0]
    gain_rows = jnp.zeros((16, attn_width), BF).at[0, : gains.shape[0]].set(gains)
    attn_rows = jnp.concatenate(
        [
            jnp.concatenate(
                [
                    columns_of(query_weight, q_width),
                    columns_of(key_projection, kv_width),
                    columns_of(value_projection, kv_width),
                ],
                axis=1,
            ),
            gain_rows,
        ],
        axis=0,
    )

    def interleaved(weight):
        cut = weight.reshape(rows, shards, replicas, ff_rows)
        return lax.dynamic_index_in_dim(cut, r, 2, keepdims=False).reshape(rows, ff)

    gate_up_rows = jnp.concatenate([interleaved(gate_weight), interleaved(up_weight)], axis=1)
    down_rows = lax.dynamic_slice_in_dim(down_weight, r * ff_rows, ff_rows, 0)

    tokens = layer_in[0]
    all_tokens = spread_blocks(tokens)
    attn_all, attn_last = gather_rows(attn_rows)
    out_weight, _ = lax.optimization_barrier((out_weight, attn_last))
    out_matrix = gather_heads(out_weight)
    gate_up_rows, down_rows, _ = lax.optimization_barrier((gate_up_rows, down_rows, attn_last))
    gate_up_all, _ = gather_rows(gate_up_rows)
    down_all, _ = gather_rows(down_rows)
    cotangent_low, _ = lax.optimization_barrier((out_grad[0], all_tokens))
    all_cotangent = spread_blocks(cotangent_low).reshape(length, MODEL_WIDTH)

    attn_matrix = attn_all[:, :rows].reshape(MODEL_WIDTH, attn_width)
    gain_all = attn_all[:, rows].astype(F32)
    attn_gain = gain_all[:, :rows].reshape(MODEL_WIDTH)
    mlp_gain = gain_all[:, rows : 2 * rows].reshape(MODEL_WIDTH)
    query_gain = gain_all[:, 2 * rows : 2 * rows + head_rows].reshape(HEAD_SIZE)
    key_gain = gain_all[:, 2 * rows + head_rows : 2 * rows + 2 * head_rows].reshape(HEAD_SIZE)
    gate_up_matrix = gate_up_all.reshape(MODEL_WIDTH, 2 * ff)
    down_matrix = down_all.reshape(ff, MODEL_WIDTH)

    block_ids = r ^ jnp.arange(replicas, dtype=jnp.int32)
    positions = (block_ids[:, None] * size + jnp.arange(size, dtype=jnp.int32)[None, :]).reshape(-1)
    half = HEAD_SIZE // 2
    inv_freq = ROPE_BASE ** (-2.0 * jnp.arange(half, dtype=F32) / HEAD_SIZE)
    angles = positions.astype(F32)[:, None] * inv_freq[None, :]
    cosine, sine = jnp.cos(angles), jnp.sin(angles)
    cos_row = jnp.concatenate([cosine, cosine], axis=1)[:, None, :]
    sin_row = jnp.concatenate([-sine, sine], axis=1)[:, None, :]
    starts = picture_starts[0]
    held = (starts[None, :] == block_ids[:, None] * PIECE) & (
        jnp.arange(starts.shape[0], dtype=jnp.int32)[None, :] < picture_count[0]
    )
    info = jnp.concatenate([r[None].astype(jnp.int32), jnp.any(held, axis=1).astype(jnp.int32)])

    wide = all_tokens.reshape(length, MODEL_WIDTH).astype(F32)
    token_inverse = inverse_root(wide)
    normed = (wide * token_inverse * attn_gain).astype(BF)
    raw = mm(normed, attn_matrix)
    query_raw = raw[:, :q_width].reshape(length, -1, HEAD_SIZE)
    key_raw = raw[:, q_width : q_width + kv_width].reshape(length, -1, HEAD_SIZE)
    value = raw[:, q_width + kv_width :].astype(BF).reshape(replicas, size, kv_width)

    def rotated(values, gain):
        scaled = values * inverse_root(values) * gain
        return (scaled * cos_row + turn(scaled) * sin_row).astype(BF).reshape(replicas, size, -1)

    query, key = rotated(query_raw, query_gain), rotated(key_raw, key_gain)
    mixed, lse = attention_forward(info, query, key, value)
    mixed_rows = mixed.reshape(length, q_width)
    after_attn = tokens.astype(F32) + sum_blocks(
        mm(mixed_rows, out_matrix).reshape(replicas, size, MODEL_WIDTH)
    )
    after_inverse = inverse_root(after_attn)
    scaled_attn = after_attn * after_inverse
    mlp_in = spread_blocks((scaled_attn * mlp_gain).astype(BF)).reshape(length, MODEL_WIDTH)
    gate_up = mm(mlp_in, gate_up_matrix)
    gate_act, up_act = gate_up[:, :ff], gate_up[:, ff:]
    sigmoid = 1.0 / (1.0 + jnp.exp(-gate_act))
    silu = gate_act * sigmoid
    hidden = (silu * up_act).astype(BF)

    hidden_grad = mm(all_cotangent, down_matrix, ((1,), (1,)))
    gate_grad = (hidden_grad * up_act * sigmoid * (1.0 + gate_act * (1.0 - sigmoid))).astype(BF)
    up_grad = (hidden_grad * silu).astype(BF)
    gate_up_grad = jnp.concatenate([gate_grad, up_grad], axis=1)
    mlp_in_part = mm(gate_up_grad, gate_up_matrix, ((1,), (1,)))
    mlp_in_grad = sum_blocks(mlp_in_part.reshape(replicas, size, MODEL_WIDTH))
    residual_grad = out_grad[0].astype(F32) + norm_back(
        after_attn, after_inverse, mlp_gain, mlp_in_grad
    )
    mlp_gain_part = jnp.sum(mlp_in_grad * scaled_attn, axis=0)
    branch_grad = spread_blocks(residual_grad.astype(BF)).reshape(length, MODEL_WIDTH)

    layer_out = after_attn + sum_blocks(mm(hidden, down_matrix).reshape(replicas, size, MODEL_WIDTH))
    gate_up_w = scatter_rows(
        mm(mlp_in, gate_up_grad, ((0,), (0,))).reshape(shards, rows, 2 * ff)
    )
    down_w = scatter_rows(
        mm(hidden, all_cotangent, ((0,), (0,))).reshape(shards, ff_rows, MODEL_WIDTH)
    )

    out_w_grad = scatter_heads(mm(mixed_rows, branch_grad, ((0,), (0,))))
    mixed_grad = mm(branch_grad, out_matrix, ((1,), (1,))).astype(BF)
    dq, dk, dv = attention_backward(
        info, query, key, value, mixed, lse, mixed_grad.reshape(replicas, size, q_width)
    )

    def head_back(values, gain, dy):
        dy = dy.reshape(length, -1, HEAD_SIZE)
        dy = dy * cos_row - turn(dy) * sin_row
        inverse = inverse_root(values)
        gain_part = jnp.sum(dy * values * inverse, axis=(0, 1))
        return norm_back(values, inverse, gain, dy).astype(BF).reshape(length, -1), gain_part

    query_grad, query_gain_part = head_back(query_raw, query_gain, dq)
    key_grad, key_gain_part = head_back(key_raw, key_gain, dk)
    attn_grad = jnp.concatenate(
        [query_grad, key_grad, dv.reshape(length, kv_width).astype(BF)], axis=1
    )
    normed_part = mm(attn_grad, attn_matrix, ((1,), (1,)))
    normed_grad = sum_blocks(normed_part.reshape(replicas, size, MODEL_WIDTH))
    attn_gain_part = jnp.sum(normed_part * (wide * token_inverse), axis=0)
    own_tokens = tokens.astype(F32)
    in_grad = residual_grad + norm_back(own_tokens, inverse_root(own_tokens), attn_gain, normed_grad)

    gain_parts = jnp.concatenate(
        [
            attn_gain_part.reshape(shards, rows),
            mlp_gain_part.reshape(shards, rows),
            query_gain_part.reshape(shards, head_rows),
            key_gain_part.reshape(shards, head_rows),
        ],
        axis=1,
    )
    gain_block = jnp.zeros((shards, 16, attn_width), F32).at[:, 0, : gain_parts.shape[1]].set(gain_parts)
    attn_w_parts = mm(normed, attn_grad, ((0,), (0,))).reshape(shards, rows, attn_width)
    attn_w = scatter_rows(jnp.concatenate([attn_w_parts, gain_block], axis=1))

    def in_order(value):
        spread = spread_blocks(value.astype(BF))
        return jnp.stack(
            [lax.dynamic_index_in_dim(spread, r ^ a, 0, keepdims=False) for a in range(replicas)]
        ).astype(F32)

    attn_full = in_order(attn_w)
    gain_full = jnp.sum(attn_full[:, rows], axis=0)

    def beside(values):
        return jnp.concatenate([values[a] for a in range(replicas)], axis=1)

    query_w_grad = beside(attn_full[:, :rows, :q_width])
    key_w_grad = beside(attn_full[:, :rows, q_width : q_width + kv_width])
    value_w_grad = beside(attn_full[:, :rows, q_width + kv_width :])
    gate_up_full = in_order(gate_up_w)

    def woven(values):
        cut = values.reshape(replicas, rows, shards, ff_rows)
        return cut.transpose(1, 2, 0, 3).reshape(rows, shards * replicas * ff_rows)

    gate_w_grad = woven(gate_up_full[:, :, :ff])
    up_w_grad = woven(gate_up_full[:, :, ff:])
    down_w_grad = in_order(down_w).reshape(replicas * ff_rows, MODEL_WIDTH)

    return (
        layer_out.astype(BF)[None],
        in_grad.astype(BF)[None],
        gain_full[:rows],
        query_w_grad,
        key_w_grad,
        value_w_grad,
        gain_full[2 * rows : 2 * rows + head_rows],
        gain_full[2 * rows + head_rows : 2 * rows + 2 * head_rows],
        out_w_grad,
        gain_full[rows : 2 * rows],
        gate_w_grad,
        up_w_grad,
        down_w_grad,
    )


def solution(mesh):
    tokens, matrix, vector = P("shard", "rep", None), P("shard", None), P("shard")
    return jax.shard_map(
        per_device,
        mesh=mesh,
        in_specs=(tokens, tokens, vector, matrix, matrix, matrix, vector, vector, matrix, vector)
        + (matrix, matrix, matrix, matrix, vector),
        out_specs=(tokens, tokens, vector, matrix, matrix, matrix, vector, vector, matrix, vector)
        + (matrix, matrix, matrix),
        check_vma=False,
    )
```

```python
import jax
import jax.numpy as jnp
from jax import lax
from jax.experimental import pallas as pl
from jax.experimental.pallas import tpu as pltpu
from jax.sharding import PartitionSpec as P

MODEL_WIDTH = 1024
QUERY_HEADS = 16
KEY_VALUE_HEADS = 8
HEAD_SIZE = 128
GROUP = QUERY_HEADS // KEY_VALUE_HEADS
PIECE = 256

EPSILON = 1e-06
ROPE_BASE = 1000000.0
SCALE = HEAD_SIZE ** (-0.5)
LOG2E = 1.4426950408889634
BF = jnp.bfloat16
F32 = jnp.float32


def mm(a, b, dims=((1,), (0,))):
    return lax.dot_general(a, b, (dims, ((), ())), preferred_element_type=F32)


def flip(value, bit):
    count = lax.axis_size("rep")
    return lax.ppermute(value, "rep", [(i, i ^ bit) for i in range(count)])


def spread_blocks(value):
    count = lax.axis_size("rep")
    if count == 4:
        half = value.shape[0] // 2
        by_one, by_two = flip(value, 1), flip(value, 2)
        low, high = flip(by_one[:half], 2), flip(by_two[half:], 1)
        return jnp.stack([value, by_one, by_two, jnp.concatenate([low, high], axis=0)])
    blocks = value[None]
    bit = 1
    while bit < count:
        blocks = jnp.concatenate([blocks, flip(blocks, bit)], axis=0)
        bit *= 2
    return blocks


def sum_blocks(parts):
    count = lax.axis_size("rep")
    if count == 4:
        half = parts.shape[1] // 2
        a, b = parts[:, :half], parts[:, half:]
        a_in = flip(jnp.stack([a[1], a[3]]).astype(BF), 1).astype(F32)
        b_in = flip(jnp.stack([b[2], b[3]]).astype(BF), 2).astype(F32)
        a_last = flip((a[2] + a_in[1]).astype(BF), 2).astype(F32)
        b_last = flip((b[1] + b_in[1]).astype(BF), 1).astype(F32)
        return jnp.concatenate([a[0] + a_in[0] + a_last, b[0] + b_in[0] + b_last], axis=0)
    bit = count // 2
    while bit:
        parts = parts[:bit] + flip(parts[bit:].astype(BF), bit).astype(F32)
        bit //= 2
    return parts[0]


def ring_up(value):
    count = lax.axis_size("shard")
    return lax.ppermute(value, "shard", [(i, (i + 2) % count) for i in range(count)])


def other_core(value):
    count = lax.axis_size("shard")
    return lax.ppermute(value, "shard", [(i, i ^ 1) for i in range(count)])


def gather_rows(value):
    count = lax.axis_size("shard")
    chips = count // 2
    index = lax.axis_index("shard")
    chip, core = index // 2, index % 2
    full = jnp.zeros((count,) + value.shape, value.dtype)
    current = value
    for step in range(chips):
        if step:
            current = ring_up(current)
        place = 2 * ((chip + chips - step) % chips)
        full = lax.dynamic_update_index_in_dim(full, current, place + core, 0)
        full = lax.dynamic_update_index_in_dim(full, other_core(current), place + 1 - core, 0)
    return full, current


def scatter_rows(parts):
    count = lax.axis_size("shard")
    chips = count // 2
    index = lax.axis_index("shard")
    chip, core = index // 2, index % 2
    by_chip = parts.reshape((chips, 2) + parts.shape[1:])
    away = lax.dynamic_index_in_dim(by_chip, 1 - core, 1, keepdims=False).astype(BF)
    kept = lax.dynamic_index_in_dim(by_chip, core, 1, keepdims=False)
    paired = kept + other_core(away).astype(F32)

    def own(step):
        return lax.dynamic_index_in_dim(paired, (chip + 2 * chips - step) % chips, 0, keepdims=False)

    running = own(1)
    for step in range(1, chips):
        running = ring_up(running.astype(BF)).astype(F32) + own(step + 1)
    return running


def joint_move(value, pairs):
    shards = lax.axis_size("shard")
    joint = [
        (r0 * shards + 2 * z0 + c, r1 * shards + 2 * z1 + c)
        for (r0, z0), (r1, z1) in pairs
        for c in range(2)
    ]
    return lax.ppermute(value, ("rep", "shard"), joint)


def gather_heads(value):
    replicas, shards = lax.axis_size("rep"), lax.axis_size("shard")
    r, index = lax.axis_index("rep"), lax.axis_index("shard")
    if shards != 2 * replicas:
        full = lax.all_gather(value, "shard", axis=0, tiled=True)
        rows = full.shape[0] // replicas
        return lax.dynamic_slice_in_dim(full, r * rows, rows, 0)
    chip, core = index // 2, index % 2
    up = [((i, z), (i, z + 1)) for i in range(replicas) for z in range(i, replicas - 1)]
    down = [((i, z), (i, z - 1)) for i in range(replicas) for z in range(1, i + 1)]
    moved_up = joint_move(value, [p for p in up if p[0][1] == p[0][0]])
    moved_down = joint_move(value, [p for p in down if p[0][1] == p[0][0]])
    total = moved_up + moved_down
    result = jnp.where(chip == r, value, total)
    moved = total
    for hop in range(2, replicas):
        pairs = [p for p in up if p[0][1] - p[0][0] == hop - 1]
        pairs += [p for p in down if p[0][0] - p[0][1] == hop - 1]
        moved = joint_move(moved, pairs)
        result = result + moved
    other = other_core(result)
    first = jnp.where(core == 0, result, other)
    second = jnp.where(core == 0, other, result)
    return jnp.concatenate([first, second], axis=0)


def scatter_heads(parts):
    replicas, shards = lax.axis_size("rep"), lax.axis_size("shard")
    r, index = lax.axis_index("rep"), lax.axis_index("shard")
    if shards != 2 * replicas:
        rows = parts.shape[0]
        full = jnp.zeros((rows * replicas,) + parts.shape[1:], F32)
        full = lax.dynamic_update_slice_in_dim(full, parts, r * rows, 0)
        owned = lax.psum_scatter(full.astype(BF), "shard", scatter_dimension=0, tiled=True)
        return lax.psum(owned, "rep").astype(F32)
    chip, core = index // 2, index % 2
    halves = parts.reshape((2, -1) + parts.shape[1:])
    away = lax.dynamic_index_in_dim(halves, 1 - core, 0, keepdims=False).astype(BF)
    total = lax.dynamic_index_in_dim(halves, core, 0, keepdims=False) + other_core(away).astype(F32)
    low = total.astype(BF)
    for hop in range(1, replicas):
        pairs = [((i, (i + hop) % replicas), (i, i)) for i in range(replicas)]
        total = total + joint_move(low, pairs).astype(F32)
    low = total.astype(BF)
    if replicas == 4:
        half = low.shape[0] // 2
        one = joint_move(low, [((z, z), (z ^ 1, z)) for z in range(4)])
        two = joint_move(low, [((z, z), (z ^ 2, z)) for z in range(4)])
        top = joint_move(one[:half], [((z ^ 1, z), (z ^ 3, z)) for z in range(4)])
        bottom = joint_move(two[half:], [((z ^ 2, z), (z ^ 3, z)) for z in range(4)])
        rest = one + two + jnp.concatenate([top, bottom], axis=0)
    else:
        rest = jnp.zeros_like(low)
        for other in range(1, replicas):
            rest = rest + joint_move(low, [((z, z), ((z + other) % replicas, z)) for z in range(replicas)])
    return jnp.where(chip == r, low, rest).astype(F32)


def piece_mask(picture_flag, size, heads):
    key = lax.broadcasted_iota(jnp.int32, (size, size * heads), 0)
    query = lax.broadcasted_iota(jnp.int32, (size, size * heads), 1) % size
    return (key <= query) | (picture_flag > 0)


def attention_forward_kernel(info, q_ref, k_ref, v_ref, mixed_ref, lse_ref):
    blocks, size = k_ref.shape[0], k_ref.shape[1]
    own = info[0]
    for last in range(blocks):
        i = own ^ last
        query = jnp.concatenate(
            [q_ref[i, :, h * HEAD_SIZE : (h + 1) * HEAD_SIZE] for h in range(GROUP)], axis=0
        )
        total = jnp.zeros((1, GROUP * size), F32)
        mixed = jnp.zeros((HEAD_SIZE, GROUP * size), F32)
        for block in range(last + 1):
            j = own ^ block
            scores = mm(k_ref[j], query, ((1,), (1,)))
            weights = jnp.exp2(scores * (SCALE * LOG2E))
            if block == last:
                weights = jnp.where(piece_mask(info[1 + i], size, GROUP), weights, 0.0)
            total = total + jnp.sum(weights, axis=0, keepdims=True)
            mixed = mixed + mm(v_ref[j], weights.astype(BF), ((0,), (0,)))
        mixed = mixed * (1.0 / total)
        log_sum = jnp.log2(total)
        for h in range(GROUP):
            columns = slice(h * size, (h + 1) * size)
            mixed_ref[i, :, h * HEAD_SIZE : (h + 1) * HEAD_SIZE] = mixed[:, columns].T.astype(BF)
            lse_ref[i, h : h + 1, :] = log_sum[:, columns]


def attention_backward_kernel(
    info, q_ref, k_ref, v_ref, mixed_ref, lse_ref, grad_ref, dq_ref, dk_ref, dv_ref
):
    blocks, size = k_ref.shape[0], k_ref.shape[1]
    own = info[0]
    dk_ref[...] = jnp.zeros_like(dk_ref)
    dv_ref[...] = jnp.zeros_like(dv_ref)
    for last in range(blocks):
        i = own ^ last
        heads = [slice(h * HEAD_SIZE, (h + 1) * HEAD_SIZE) for h in range(GROUP)]
        query = jnp.concatenate([q_ref[i, :, h] for h in heads], axis=0)
        grad = jnp.concatenate([grad_ref[i, :, h] for h in heads], axis=0)
        mixed = jnp.concatenate([mixed_ref[i, :, h] for h in heads], axis=0)
        delta = jnp.sum((grad.astype(F32) * mixed.astype(F32)).T, axis=0, keepdims=True)
        log_sum = jnp.concatenate([lse_ref[i, h : h + 1, :] for h in range(GROUP)], axis=1)
        dquery = jnp.zeros((HEAD_SIZE, GROUP * size), F32)
        for block in range(last + 1):
            j = own ^ block
            scores = mm(k_ref[j], query, ((1,), (1,)))
            dprobs = mm(v_ref[j], grad, ((1,), (1,)))
            probs = jnp.exp2(scores * (SCALE * LOG2E) - log_sum)
            if block == last:
                probs = jnp.where(piece_mask(info[1 + i], size, GROUP), probs, 0.0)
            dscores = (probs * (dprobs - delta)).astype(BF)
            dv_ref[j] += mm(probs.astype(BF), grad)
            dk_ref[j] += mm(dscores, query)
            dquery = dquery + mm(k_ref[j], dscores, ((0,), (0,)))
        for h in range(GROUP):
            dq_ref[i, :, heads[h]] = dquery[:, h * size : (h + 1) * size].T * SCALE
    dk_ref[...] = dk_ref[...] * SCALE


def attention_specs(blocks, size):
    wide = pl.BlockSpec((blocks, size, GROUP * HEAD_SIZE), lambda g, info: (0, 0, g))
    thin = pl.BlockSpec((blocks, size, HEAD_SIZE), lambda g, info: (0, 0, g))
    rows = pl.BlockSpec((None, blocks, GROUP, size), lambda g, info: (g, 0, 0, 0))
    return wide, thin, rows


def attention_forward(info, query, key, value):
    blocks, size, width = key.shape
    groups = width // HEAD_SIZE
    wide, thin, rows = attention_specs(blocks, size)
    return pl.pallas_call(
        attention_forward_kernel,
        grid_spec=pltpu.PrefetchScalarGridSpec(
            num_scalar_prefetch=1,
            grid=(groups,),
            in_specs=[wide, thin, thin],
            out_specs=[wide, rows],
        ),
        out_shape=[
            jax.ShapeDtypeStruct(query.shape, BF),
            jax.ShapeDtypeStruct((groups, blocks, GROUP, size), F32),
        ],
        compiler_params=pltpu.CompilerParams(vmem_limit_bytes=48 << 20),
        name="attention_forward",
    )(info, query, key, value)


def attention_backward(info, query, key, value, mixed, lse, grad):
    blocks, size, width = key.shape
    groups = width // HEAD_SIZE
    wide, thin, rows = attention_specs(blocks, size)
    return pl.pallas_call(
        attention_backward_kernel,
        grid_spec=pltpu.PrefetchScalarGridSpec(
            num_scalar_prefetch=1,
            grid=(groups,),
            in_specs=[wide, thin, thin, wide, rows, wide],
            out_specs=[wide, thin, thin],
        ),
        out_shape=[
            jax.ShapeDtypeStruct(query.shape, F32),
            jax.ShapeDtypeStruct(key.shape, F32),
            jax.ShapeDtypeStruct(key.shape, F32),
        ],
        compiler_params=pltpu.CompilerParams(vmem_limit_bytes=48 << 20),
        name="attention_backward",
    )(info, query, key, value, mixed, lse, grad)


def inverse_root(values):
    return lax.rsqrt(jnp.mean(values * values, axis=-1, keepdims=True) + EPSILON)


def norm_back(values, inverse, gain, dy):
    weighted = dy * gain
    inner = jnp.mean(values * weighted, axis=-1, keepdims=True)
    return inverse * weighted - values * (inverse * inverse * inverse) * inner


def turn(values):
    return jnp.concatenate([values[..., HEAD_SIZE // 2 :], values[..., : HEAD_SIZE // 2]], axis=-1)


def per_device_any(
    layer_in,
    out_grad,
    attn_norm,
    query_weight,
    key_projection,
    value_projection,
    query_norm,
    key_norm,
    out_weight,
    mlp_norm,
    gate_weight,
    up_weight,
    down_weight,
    picture_starts,
    picture_count,
):
    replicas, shards = lax.axis_size("rep"), lax.axis_size("shard")
    r = lax.axis_index("rep")
    size = layer_in.shape[1]
    length = size * replicas
    rows = attn_norm.shape[0]
    q_width = QUERY_HEADS // replicas * HEAD_SIZE
    kv_width = KEY_VALUE_HEADS // replicas * HEAD_SIZE
    attn_width = q_width + 2 * kv_width
    ff_rows = down_weight.shape[0] // replicas
    ff = ff_rows * shards

    def columns_of(weight, width):
        return lax.dynamic_slice_in_dim(weight, r * width, width, 1)

    gains = jnp.concatenate([attn_norm, mlp_norm, query_norm, key_norm])
    head_rows = query_norm.shape[0]
    gain_rows = jnp.zeros((16, attn_width), BF).at[0, : gains.shape[0]].set(gains)
    attn_rows = jnp.concatenate(
        [
            jnp.concatenate(
                [
                    columns_of(query_weight, q_width),
                    columns_of(key_projection, kv_width),
                    columns_of(value_projection, kv_width),
                ],
                axis=1,
            ),
            gain_rows,
        ],
        axis=0,
    )

    def interleaved(weight):
        cut = weight.reshape(rows, shards, replicas, ff_rows)
        return lax.dynamic_index_in_dim(cut, r, 2, keepdims=False).reshape(rows, ff)

    gate_up_rows = jnp.concatenate([interleaved(gate_weight), interleaved(up_weight)], axis=1)
    down_rows = lax.dynamic_slice_in_dim(down_weight, r * ff_rows, ff_rows, 0)

    tokens = layer_in[0]
    all_tokens = spread_blocks(tokens)
    attn_all, attn_last = gather_rows(attn_rows)
    out_weight, _ = lax.optimization_barrier((out_weight, attn_last))
    out_matrix = gather_heads(out_weight)
    gate_up_rows, down_rows, _ = lax.optimization_barrier((gate_up_rows, down_rows, attn_last))
    gate_up_all, _ = gather_rows(gate_up_rows)
    down_all, _ = gather_rows(down_rows)
    cotangent_low, _ = lax.optimization_barrier((out_grad[0], all_tokens))
    all_cotangent = spread_blocks(cotangent_low).reshape(length, MODEL_WIDTH)

    attn_matrix = attn_all[:, :rows].reshape(MODEL_WIDTH, attn_width)
    gain_all = attn_all[:, rows].astype(F32)
    attn_gain = gain_all[:, :rows].reshape(MODEL_WIDTH)
    mlp_gain = gain_all[:, rows : 2 * rows].reshape(MODEL_WIDTH)
    query_gain = gain_all[:, 2 * rows : 2 * rows + head_rows].reshape(HEAD_SIZE)
    key_gain = gain_all[:, 2 * rows + head_rows : 2 * rows + 2 * head_rows].reshape(HEAD_SIZE)
    gate_up_matrix = gate_up_all.reshape(MODEL_WIDTH, 2 * ff)
    down_matrix = down_all.reshape(ff, MODEL_WIDTH)

    block_ids = r ^ jnp.arange(replicas, dtype=jnp.int32)
    positions = (block_ids[:, None] * size + jnp.arange(size, dtype=jnp.int32)[None, :]).reshape(-1)
    half = HEAD_SIZE // 2
    inv_freq = ROPE_BASE ** (-2.0 * jnp.arange(half, dtype=F32) / HEAD_SIZE)
    angles = positions.astype(F32)[:, None] * inv_freq[None, :]
    cosine, sine = jnp.cos(angles), jnp.sin(angles)
    cos_row = jnp.concatenate([cosine, cosine], axis=1)[:, None, :]
    sin_row = jnp.concatenate([-sine, sine], axis=1)[:, None, :]
    starts = picture_starts[0]
    held = (starts[None, :] == block_ids[:, None] * PIECE) & (
        jnp.arange(starts.shape[0], dtype=jnp.int32)[None, :] < picture_count[0]
    )
    info = jnp.concatenate([r[None].astype(jnp.int32), jnp.any(held, axis=1).astype(jnp.int32)])

    wide = all_tokens.reshape(length, MODEL_WIDTH).astype(F32)
    token_inverse = inverse_root(wide)
    normed = (wide * token_inverse * attn_gain).astype(BF)
    raw = mm(normed, attn_matrix)
    query_raw = raw[:, :q_width].reshape(length, -1, HEAD_SIZE)
    key_raw = raw[:, q_width : q_width + kv_width].reshape(length, -1, HEAD_SIZE)
    value = raw[:, q_width + kv_width :].astype(BF).reshape(replicas, size, kv_width)

    def rotated(values, gain):
        scaled = values * inverse_root(values) * gain
        return (scaled * cos_row + turn(scaled) * sin_row).astype(BF).reshape(replicas, size, -1)

    query, key = rotated(query_raw, query_gain), rotated(key_raw, key_gain)
    mixed, lse = attention_forward(info, query, key, value)
    mixed_rows = mixed.reshape(length, q_width)
    after_attn = tokens.astype(F32) + sum_blocks(
        mm(mixed_rows, out_matrix).reshape(replicas, size, MODEL_WIDTH)
    )
    after_inverse = inverse_root(after_attn)
    scaled_attn = after_attn * after_inverse
    mlp_in = spread_blocks((scaled_attn * mlp_gain).astype(BF)).reshape(length, MODEL_WIDTH)
    gate_up = mm(mlp_in, gate_up_matrix)
    gate_act, up_act = gate_up[:, :ff], gate_up[:, ff:]
    sigmoid = 1.0 / (1.0 + jnp.exp(-gate_act))
    silu = gate_act * sigmoid
    hidden = (silu * up_act).astype(BF)

    hidden_grad = mm(all_cotangent, down_matrix, ((1,), (1,)))
    gate_grad = (hidden_grad * up_act * sigmoid * (1.0 + gate_act * (1.0 - sigmoid))).astype(BF)
    up_grad = (hidden_grad * silu).astype(BF)
    gate_up_grad = jnp.concatenate([gate_grad, up_grad], axis=1)
    mlp_in_part = mm(gate_up_grad, gate_up_matrix, ((1,), (1,)))
    mlp_in_grad = sum_blocks(mlp_in_part.reshape(replicas, size, MODEL_WIDTH))
    residual_grad = out_grad[0].astype(F32) + norm_back(
        after_attn, after_inverse, mlp_gain, mlp_in_grad
    )
    mlp_gain_part = jnp.sum(mlp_in_grad * scaled_attn, axis=0)
    branch_grad = spread_blocks(residual_grad.astype(BF)).reshape(length, MODEL_WIDTH)

    layer_out = after_attn + sum_blocks(mm(hidden, down_matrix).reshape(replicas, size, MODEL_WIDTH))
    gate_up_w = scatter_rows(
        mm(mlp_in, gate_up_grad, ((0,), (0,))).reshape(shards, rows, 2 * ff)
    )
    down_w = scatter_rows(
        mm(hidden, all_cotangent, ((0,), (0,))).reshape(shards, ff_rows, MODEL_WIDTH)
    )

    out_w_grad = scatter_heads(mm(mixed_rows, branch_grad, ((0,), (0,))))
    mixed_grad = mm(branch_grad, out_matrix, ((1,), (1,))).astype(BF)
    dq, dk, dv = attention_backward(
        info, query, key, value, mixed, lse, mixed_grad.reshape(replicas, size, q_width)
    )

    def head_back(values, gain, dy):
        dy = dy.reshape(length, -1, HEAD_SIZE)
        dy = dy * cos_row - turn(dy) * sin_row
        inverse = inverse_root(values)
        gain_part = jnp.sum(dy * values * inverse, axis=(0, 1))
        return norm_back(values, inverse, gain, dy).astype(BF).reshape(length, -1), gain_part

    query_grad, query_gain_part = head_back(query_raw, query_gain, dq)
    key_grad, key_gain_part = head_back(key_raw, key_gain, dk)
    attn_grad = jnp.concatenate(
        [query_grad, key_grad, dv.reshape(length, kv_width).astype(BF)], axis=1
    )
    normed_part = mm(attn_grad, attn_matrix, ((1,), (1,)))
    normed_grad = sum_blocks(normed_part.reshape(replicas, size, MODEL_WIDTH))
    attn_gain_part = jnp.sum(normed_part * (wide * token_inverse), axis=0)
    own_tokens = tokens.astype(F32)
    in_grad = residual_grad + norm_back(own_tokens, inverse_root(own_tokens), attn_gain, normed_grad)

    gain_parts = jnp.concatenate(
        [
            attn_gain_part.reshape(shards, rows),
            mlp_gain_part.reshape(shards, rows),
            query_gain_part.reshape(shards, head_rows),
            key_gain_part.reshape(shards, head_rows),
        ],
        axis=1,
    )
    gain_block = jnp.zeros((shards, 16, attn_width), F32).at[:, 0, : gain_parts.shape[1]].set(gain_parts)
    attn_w_parts = mm(normed, attn_grad, ((0,), (0,))).reshape(shards, rows, attn_width)
    attn_w = scatter_rows(jnp.concatenate([attn_w_parts, gain_block], axis=1))

    def in_order(value):
        spread = spread_blocks(value.astype(BF))
        return jnp.stack(
            [lax.dynamic_index_in_dim(spread, r ^ a, 0, keepdims=False) for a in range(replicas)]
        ).astype(F32)

    attn_full = in_order(attn_w)
    gain_full = jnp.sum(attn_full[:, rows], axis=0)

    def beside(values):
        return jnp.concatenate([values[a] for a in range(replicas)], axis=1)

    query_w_grad = beside(attn_full[:, :rows, :q_width])
    key_w_grad = beside(attn_full[:, :rows, q_width : q_width + kv_width])
    value_w_grad = beside(attn_full[:, :rows, q_width + kv_width :])
    gate_up_full = in_order(gate_up_w)

    def woven(values):
        cut = values.reshape(replicas, rows, shards, ff_rows)
        return cut.transpose(1, 2, 0, 3).reshape(rows, shards * replicas * ff_rows)

    gate_w_grad = woven(gate_up_full[:, :, :ff])
    up_w_grad = woven(gate_up_full[:, :, ff:])
    down_w_grad = in_order(down_w).reshape(replicas * ff_rows, MODEL_WIDTH)

    return (
        layer_out.astype(BF)[None],
        in_grad.astype(BF)[None],
        gain_full[:rows],
        query_w_grad,
        key_w_grad,
        value_w_grad,
        gain_full[2 * rows : 2 * rows + head_rows],
        gain_full[2 * rows + head_rows : 2 * rows + 2 * head_rows],
        out_w_grad,
        gain_full[rows : 2 * rows],
        gate_w_grad,
        up_w_grad,
        down_w_grad,
    )


BLOCKS = 4
CHIPS = 4
ROWS = 128
SIZE = 256
HALF = SIZE // 2
Q_WIDTH = QUERY_HEADS // BLOCKS * HEAD_SIZE
KV_WIDTH = KEY_VALUE_HEADS // BLOCKS * HEAD_SIZE
QK_WIDTH = Q_WIDTH + KV_WIDTH
ATTN_WIDTH = Q_WIDTH + 2 * KV_WIDTH
FF_ROWS = 96
FF_PART = 768
OUT_ROWS = 64
PACKED = 3 * ROWS
TURN = HEAD_SIZE // 2


def shape(dims, dtype):
    return jax.ShapeDtypeStruct(dims, dtype)


def on_core(body, name, outs, scalars, args, flops=0, traffic=0):
    return pl.pallas_call(
        body,
        name=name,
        in_specs=[pl.BlockSpec(memory_space=pltpu.SMEM)] * len(scalars)
        + [pl.BlockSpec(memory_space=pltpu.VMEM)] * len(args),
        out_specs=[pl.BlockSpec(memory_space=pltpu.VMEM)] * len(outs),
        out_shape=outs,
        compiler_params=pltpu.CompilerParams(vmem_limit_bytes=50 << 20),
        cost_estimate=pl.CostEstimate(flops=flops, bytes_accessed=traffic, transcendentals=0),
    )(*scalars, *args)


def partial_shapes():
    return [
        shape((SIZE, MODEL_WIDTH), BF),
        shape((SIZE, MODEL_WIDTH), BF),
        shape((HALF, MODEL_WIDTH), F32),
        shape((HALF, MODEL_WIDTH), F32),
        shape((SIZE, MODEL_WIDTH), F32),
    ]


def put_partial(refs, j, part):
    by_one, by_two, keep_low, keep_high, keep = refs
    if j == 0:
        keep[...] = part
    if j == 1:
        by_one[:HALF] = part[:HALF].astype(BF)
        keep_high[...] = part[HALF:]
    if j == 2:
        by_two[:HALF] = part[HALF:].astype(BF)
        keep_low[...] = part[:HALF]
    if j == 3:
        by_one[HALF:] = part[:HALF].astype(BF)
        by_two[HALF:] = part[HALF:].astype(BF)


def move_partial(by_one, by_two, keep_low, keep_high, keep):
    one, two = flip(by_one, 1), flip(by_two, 2)
    low = flip((keep_low + one[HALF:].astype(F32)).astype(BF), 2)
    high = flip((keep_high + two[HALF:].astype(F32)).astype(BF), 1)
    return keep, one, two, low, high


def joined(keep, one, two, low, high):
    top = keep[:HALF] + one[:HALF].astype(F32) + low[...].astype(F32)
    bottom = keep[HALF:] + two[:HALF].astype(F32) + high[...].astype(F32)
    return jnp.concatenate([top, bottom], axis=0)


def spread(value):
    one, two = flip(value, 1), flip(value, 2)
    return value, one, two, flip(one[:HALF], 2), flip(two[HALF:], 1)


def spread_direct(value):
    return value, flip(value, 1), flip(value, 2), flip(value, 3)


def block_of(refs, j):
    if j < 3:
        return refs[j][...]
    return jnp.concatenate([ref[...] for ref in refs[3:]], axis=0)


def part_shard(info, t):
    chip = lax.rem(info[1] + CHIPS - t % CHIPS, CHIPS)
    return 2 * chip + (info[2] if t < CHIPS else 1 - info[2])


def project_kernel(info, *refs):
    tokens, (cos_ref, sin_ref), parts = refs[:5], refs[5:7], refs[7:15]
    normed_ref, raw_ref, q_ref, k_ref, v_ref, w_ref, gain_ref = refs[15:]
    gain_ref[...] = jnp.zeros_like(gain_ref)
    for t in range(2 * CHIPS):
        s = part_shard(info, t)
        columns = pl.ds(pl.multiple_of(s * ROWS, ROWS), ROWS)
        w_ref[columns, :] = parts[t][:ROWS]
        row = parts[t][ROWS : ROWS + 16, : 4 * ROWS].astype(F32)[:1]
        gain_ref[0:1, columns] = row[:, :ROWS]
        gain_ref[1:2, columns] = row[:, ROWS : 2 * ROWS]
        gain_ref[2:3, : 2 * HEAD_SIZE] += row[:, 2 * ROWS :]
    for j in range(BLOCKS):
        here = slice(j * SIZE, (j + 1) * SIZE)
        wide = block_of(tokens, j).astype(F32)
        normed = (wide * inverse_root(wide) * gain_ref[0:1, :]).astype(BF)
        normed_ref[here, :] = normed
        raw = mm(normed, w_ref[...])
        raw_ref[here, :] = raw[:, :QK_WIDTH]
        v_ref[j] = raw[:, QK_WIDTH:].astype(BF)
        cosine, sine = cos_ref[here, :], sin_ref[here, :]
        for h in range(QK_WIDTH // HEAD_SIZE):
            one = raw[:, h * HEAD_SIZE : (h + 1) * HEAD_SIZE]
            is_key = h * HEAD_SIZE >= Q_WIDTH
            gain = gain_ref[2:3, HEAD_SIZE : 2 * HEAD_SIZE] if is_key else gain_ref[2:3, :HEAD_SIZE]
            scaled = one * inverse_root(one) * gain
            rotated = (scaled * cosine + pltpu.roll(scaled, TURN, 1) * sine).astype(BF)
            at = h * HEAD_SIZE - (Q_WIDTH if is_key else 0)
            (k_ref if is_key else q_ref)[j, :, at : at + HEAD_SIZE] = rotated


def attend_kernel(info, q_ref, k_ref, v_ref, own_out, other_out, mixed_ref, lse_ref, out_ref, *partial):
    own = info[0]
    for core, rows in ((info[2], own_out), (1 - info[2], other_out)):
        for q in range(BLOCKS):
            at = pl.multiple_of(core * SIZE + (own ^ q) * OUT_ROWS, OUT_ROWS)
            out_ref[pl.ds(at, OUT_ROWS), :] = rows[q * OUT_ROWS : (q + 1) * OUT_ROWS]
    for last in range(BLOCKS - 1, -1, -1):
        i = own ^ last
        for g in range(KV_WIDTH // HEAD_SIZE):
            heads = [
                slice((g * GROUP + h) * HEAD_SIZE, (g * GROUP + h + 1) * HEAD_SIZE)
                for h in range(GROUP)
            ]
            kv = slice(g * HEAD_SIZE, (g + 1) * HEAD_SIZE)
            query = jnp.concatenate([q_ref[i, :, h] for h in heads], axis=0)
            total = jnp.zeros((1, GROUP * SIZE), F32)
            mixed = jnp.zeros((HEAD_SIZE, GROUP * SIZE), F32)
            for block in range(last + 1):
                j = own ^ block
                scores = mm(k_ref[j, :, kv], query, ((1,), (1,)))
                weights = jnp.exp2(scores * (SCALE * LOG2E))
                if block == last:
                    weights = jnp.where(piece_mask(info[3 + i], SIZE, GROUP), weights, 0.0)
                total = total + jnp.sum(weights, axis=0, keepdims=True)
                mixed = mixed + mm(v_ref[j, :, kv], weights.astype(BF), ((0,), (0,)))
            mixed = mixed * (1.0 / total)
            log_sum = jnp.log2(total)
            for h in range(GROUP):
                columns = slice(h * SIZE, (h + 1) * SIZE)
                mixed_ref[i, :, heads[h]] = mixed[:, columns].T.astype(BF)
                lse_ref[g, i, h : h + 1, :] = log_sum[:, columns]
    for j in (3, 1, 2, 0):
        put_partial(partial, j, mm(mixed_ref[j], out_ref[...]))


def after_kernel(tokens, gain_ref, *refs):
    after_ref, low_ref = refs[5:]
    after = tokens[...].astype(F32) + joined(*refs[:5])
    after_ref[...] = after
    low_ref[...] = (after * inverse_root(after) * gain_ref[1:2, :]).astype(BF)


def prepare_kernel(info, *refs):
    parts, cotangent = refs[:8], refs[8:12]
    gate_up_ref, down_ref = refs[12:14]
    grads = refs[14:]
    for t in range(2 * CHIPS):
        s = part_shard(info, t)
        at = pl.ds(pl.multiple_of(s * ROWS, ROWS), ROWS)
        gate_up_ref[at, :FF_PART] = parts[t][:ROWS]
        gate_up_ref[at, FF_PART:] = parts[t][ROWS : 2 * ROWS]
        at = pl.ds(pl.multiple_of(s * FF_ROWS, 32), FF_ROWS)
        down_ref[at, :FF_PART] = parts[t][2 * ROWS : 2 * ROWS + FF_ROWS]
        for i in range(3):
            at = pl.ds(pl.multiple_of(s * FF_ROWS + i * 32, 32), 32)
            down_ref[at, FF_PART:] = parts[t][2 * ROWS + FF_ROWS :, i * 256 : (i + 1) * 256]
    for j in range(BLOCKS):
        grads[j][...] = mm(cotangent[j][...], down_ref[...], ((1,), (1,)))


def feed_kernel(blocks, *refs):
    count = len(blocks)
    extra = 2 if blocks == (3,) else count
    inputs, hidden_grads = refs[:extra], refs[extra : extra + count]
    gate_up_ref = refs[extra + count]
    outs = refs[extra + count + 1 :]
    for n, j in enumerate(blocks):
        if j == 3:
            tokens = jnp.concatenate([inputs[0][...], inputs[1][...]], axis=0)
        else:
            tokens = inputs[n][...]
        hidden_ref, both_ref = outs[2 * n : 2 * n + 2]
        gate_up = mm(tokens, gate_up_ref[...])
        gate, up = gate_up[:, :FF_PART], gate_up[:, FF_PART:]
        sigmoid = 1.0 / (1.0 + jnp.exp(-gate))
        silu = gate * sigmoid
        hidden_ref[...] = (silu * up).astype(BF)
        grad = hidden_grads[n][...]
        both_ref[:, :FF_PART] = (grad * up * sigmoid * (1.0 + gate * (1.0 - sigmoid))).astype(BF)
        both_ref[:, FF_PART:] = (grad * silu).astype(BF)
        part = mm(both_ref[...], gate_up_ref[...], ((1,), (1,)))
        first, second = outs[2 * count + 2 * n : 2 * count + 2 * n + 2]
        first[...] = part[:HALF].astype(first.dtype)
        second[...] = part[HALF:].astype(second.dtype)


FEED_TYPES = {0: (F32, F32), 1: (BF, F32), 2: (F32, BF), 3: (BF, BF)}


def feed(blocks, inputs, hidden_grads, gate_up):
    outs = []
    for _ in blocks:
        outs += [shape((SIZE, FF_PART), BF), shape((SIZE, 2 * FF_PART), BF)]
    for j in blocks:
        outs += [shape((HALF, MODEL_WIDTH), dtype) for dtype in FEED_TYPES[j]]

    def body(*refs):
        feed_kernel(blocks, *refs)

    result = on_core(
        body,
        "feed",
        outs,
        (),
        (*inputs, *hidden_grads, gate_up),
        flops=len(blocks) * 4 * SIZE * MODEL_WIDTH * 2 * FF_PART,
    )
    count = len(blocks)
    hidden, both = result[0 : 2 * count : 2], result[1 : 2 * count : 2]
    return hidden, both, result[2 * count :]


def split_rows(info, kept, away, t, at, values):
    half = values.shape[0] // 2
    first, second = values[:half], values[half:]
    is_first = info[2] == 0
    kept[t, at : at + half, :] = jnp.where(is_first, first, second)
    away[t, at : at + half, :] = jnp.where(is_first, second, first).astype(BF)


def feed_weights_kernel(info, *refs):
    mlp_in, cotangent, hidden, both = refs[:5], refs[5:9], refs[9:13], refs[13:17]
    down_ref = refs[17]
    kept, away = refs[18:20]
    partial = refs[20:25]
    down_grad = refs[25]
    inputs = jnp.concatenate([block_of(mlp_in, j) for j in range(BLOCKS)], axis=0)
    stored = refs[26]
    stored[...] = inputs
    both_all = jnp.concatenate([ref[...] for ref in both], axis=0)
    hidden_all = jnp.concatenate([ref[...] for ref in hidden], axis=0)
    cotangent_all = jnp.concatenate([ref[...] for ref in cotangent], axis=0)
    down_grad[...] = mm(hidden_all, cotangent_all, ((0,), (0,)))
    for t in range(CHIPS):
        chip = lax.rem(info[1] + 2 * CHIPS - (t + 1), CHIPS)
        columns = stored[:, pl.ds(pl.multiple_of(chip * 2 * ROWS, 2 * ROWS), 2 * ROWS)]
        product = mm(columns, both_all, ((0,), (0,)))
        split_rows(info, kept, away, t, 0, product[:, :FF_PART])
        split_rows(info, kept, away, t, ROWS, product[:, FF_PART:])
        for core, target in ((info[2], kept), (1 - info[2], away)):
            at = pl.multiple_of((2 * chip + core) * FF_ROWS, 32)
            rows = down_grad[pl.ds(at, FF_ROWS), :].astype(target.dtype)
            target[t, 2 * ROWS : 2 * ROWS + FF_ROWS, :] = rows[:, :FF_PART]
            for i in range(3):
                target[t, 2 * ROWS + FF_ROWS :, i * 256 : (i + 1) * 256] = rows[
                    i * 32 : (i + 1) * 32, FF_PART:
                ]
    for j in (3, 1, 2, 0):
        put_partial(partial, j, mm(hidden[j][...], down_ref[...]))


def residual_kernel(cotangent, after_ref, gain_ref, *refs):
    grad_ref, low_ref, gain_part = refs[-3:]
    keep_a, keep_b, one_a, one_b, two_a, two_b, low, high = refs[:8]
    top = keep_a[...] + one_a[...].astype(F32) + low[...].astype(F32)
    bottom = keep_b[...] + two_a[...].astype(F32) + high[...].astype(F32)
    mlp_in_grad = jnp.concatenate([top, bottom], axis=0)
    after = after_ref[...]
    inverse = inverse_root(after)
    gain_part[...] = jnp.sum(mlp_in_grad * (after * inverse), axis=0, keepdims=True)
    grad = cotangent[...].astype(F32) + norm_back(after, inverse, gain_ref[1:2, :], mlp_in_grad)
    grad_ref[...] = grad
    low_ref[...] = grad.astype(BF)


def mixed_grad_kernel(info, mixed_ref, out_ref, *refs):
    branch, (grad_ref, kept, away, scratch) = refs[:5], refs[5:]
    own = info[0]
    for j in range(BLOCKS):
        grad_ref[j] = mm(block_of(branch, j), out_ref[...], ((1,), (1,))).astype(BF)
    branch_all = jnp.concatenate([block_of(branch, j) for j in range(BLOCKS)], axis=0)
    mixed_all = jnp.concatenate([mixed_ref[j] for j in range(BLOCKS)], axis=0)
    scratch[...] = mm(mixed_all, branch_all, ((0,), (0,)))
    for core, target in ((info[2], kept), (1 - info[2], away)):
        for q in range(BLOCKS):
            at = pl.multiple_of(core * SIZE + (own ^ q) * OUT_ROWS, OUT_ROWS)
            target[q] = scratch[pl.ds(at, OUT_ROWS), :].astype(target.dtype)


def head_back(grad, cosine, sine, raw, gain):
    dy = grad * cosine - pltpu.roll(grad, TURN, 1) * sine
    inverse = inverse_root(raw)
    gain_part = jnp.sum(dy * (raw * inverse), axis=0, keepdims=True)
    return norm_back(raw, inverse, gain, dy).astype(BF), gain_part


def attend_back_kernel(
    info, q_ref, k_ref, v_ref, mixed_ref, lse_ref, grad_ref, raw_ref, cos_ref, sin_ref, gain_ref,
    out_ref, gain_part, dk_ref, dv_ref,
):
    own = info[0]
    query_part = jnp.zeros((1, HEAD_SIZE), F32)
    key_part = jnp.zeros((1, HEAD_SIZE), F32)
    for g in range(KV_WIDTH // HEAD_SIZE):
        dk_ref[...] = jnp.zeros_like(dk_ref)
        dv_ref[...] = jnp.zeros_like(dv_ref)
        heads = [
            slice((g * GROUP + h) * HEAD_SIZE, (g * GROUP + h + 1) * HEAD_SIZE) for h in range(GROUP)
        ]
        kv = slice(g * HEAD_SIZE, (g + 1) * HEAD_SIZE)
        for last in range(BLOCKS):
            i = own ^ last
            rows = pl.ds(pl.multiple_of(i * SIZE, SIZE), SIZE)
            query = jnp.concatenate([q_ref[i, :, h] for h in heads], axis=0)
            grad = jnp.concatenate([grad_ref[i, :, h] for h in heads], axis=0)
            mixed = jnp.concatenate([mixed_ref[i, :, h] for h in heads], axis=0)
            delta = jnp.sum((grad.astype(F32) * mixed.astype(F32)).T, axis=0, keepdims=True)
            log_sum = jnp.concatenate([lse_ref[g, i, h : h + 1, :] for h in range(GROUP)], axis=1)
            dquery = jnp.zeros((HEAD_SIZE, GROUP * SIZE), F32)
            for block in range(last + 1):
                j = own ^ block
                scores = mm(k_ref[j, :, kv], query, ((1,), (1,)))
                dprobs = mm(v_ref[j, :, kv], grad, ((1,), (1,)))
                probs = jnp.exp2(scores * (SCALE * LOG2E) - log_sum)
                if block == last:
                    probs = jnp.where(piece_mask(info[3 + i], SIZE, GROUP), probs, 0.0)
                dscores = (probs * (dprobs - delta)).astype(BF)
                dv_ref[j] += mm(probs.astype(BF), grad)
                dk_ref[j] += mm(dscores, query)
                dquery = dquery + mm(k_ref[j, :, kv], dscores, ((0,), (0,)))
            for h in range(GROUP):
                back, part = head_back(
                    dquery[:, h * SIZE : (h + 1) * SIZE].T * SCALE,
                    cos_ref[rows, :],
                    sin_ref[rows, :],
                    raw_ref[rows, heads[h]],
                    gain_ref[2:3, :HEAD_SIZE],
                )
                out_ref[rows, heads[h]] = back
                query_part = query_part + part
        for j in range(BLOCKS):
            rows = slice(j * SIZE, (j + 1) * SIZE)
            at = Q_WIDTH + g * HEAD_SIZE
            back, part = head_back(
                dk_ref[j] * SCALE,
                cos_ref[rows, :],
                sin_ref[rows, :],
                raw_ref[rows, at : at + HEAD_SIZE],
                gain_ref[2:3, HEAD_SIZE : 2 * HEAD_SIZE],
            )
            out_ref[rows, at : at + HEAD_SIZE] = back
            key_part = key_part + part
            at += KV_WIDTH
            out_ref[rows, at : at + HEAD_SIZE] = dv_ref[j].astype(BF)
    gain_part[...] = jnp.concatenate([query_part, key_part], axis=1)


def attend_weights_kernel(info, normed_ref, grad_ref, w_ref, mlp_part, head_part, *refs):
    tokens, (kept, away), partial = refs[:5], refs[5:7], refs[7:12]
    gain_part = jnp.zeros((1, MODEL_WIDTH), F32)
    for j in (3, 1, 2, 0):
        part = mm(grad_ref[j * SIZE : (j + 1) * SIZE, :], w_ref[...], ((1,), (1,)))
        put_partial(partial, j, part)
        wide = block_of(tokens, j).astype(F32)
        gain_part = gain_part + jnp.sum(part * (wide * inverse_root(wide)), axis=0, keepdims=True)
    heads = jnp.concatenate([head_part[...], jnp.zeros((1, MODEL_WIDTH - 2 * HEAD_SIZE), F32)], axis=1)
    row = lax.broadcasted_iota(jnp.int32, (16, MODEL_WIDTH), 0)
    gains = jnp.where(row == 0, gain_part, jnp.where(row == 1, mlp_part[...], jnp.where(row == 2, heads, 0.0)))
    for t in range(CHIPS):
        chip = lax.rem(info[1] + 2 * CHIPS - (t + 1), CHIPS)
        columns = normed_ref[:, pl.ds(pl.multiple_of(chip * 2 * ROWS, 2 * ROWS), 2 * ROWS)]
        split_rows(info, kept, away, t, 0, mm(columns, grad_ref[...], ((0,), (0,))))
        kept[t, ROWS:, :] = gains
        away[t, ROWS:, :] = gains.astype(BF)


def final_kernel(tokens, gain_ref, residual, *refs):
    grad_ref = refs[5]
    wide = tokens[...].astype(F32)
    dy = joined(*refs[:5])
    back = norm_back(wide, inverse_root(wide), gain_ref[0:1, :], dy)
    grad_ref[...] = (residual[...] + back).astype(BF)


def output_kernel(after_ref, *refs):
    refs[5][...] = (after_ref[...] + joined(*refs[:5])).astype(BF)


def ring_parts(value):
    own, other = [value], [other_core(value)]
    for _ in range(CHIPS - 1):
        own.append(ring_up(own[-1]))
        other.append(other_core(own[-1]))
    return own, other


def ring_sum(kept, away):
    crossed = other_core(away)
    running = (kept[0] + crossed[0].astype(F32)).astype(BF)
    for t in range(1, CHIPS):
        running = (ring_up(running).astype(F32) + kept[t] + crossed[t].astype(F32)).astype(BF)
    return running


def per_device(
    layer_in,
    out_grad,
    attn_norm,
    query_weight,
    key_projection,
    value_projection,
    query_norm,
    key_norm,
    out_weight,
    mlp_norm,
    gate_weight,
    up_weight,
    down_weight,
    picture_starts,
    picture_count,
):
    r, index = lax.axis_index("rep"), lax.axis_index("shard")
    chip, core = index // 2, index % 2
    length = BLOCKS * SIZE
    tokens, cotangent_own = layer_in[0], out_grad[0]

    def columns_of(weight, width):
        return lax.dynamic_slice_in_dim(weight, r * width, width, 1)

    def placed(gain):
        return lax.dynamic_update_slice_in_dim(
            jnp.zeros((HEAD_SIZE,), BF), gain, index * gain.shape[0], 0
        )

    gains = jnp.concatenate([attn_norm, mlp_norm, placed(query_norm), placed(key_norm)])
    attn_rows = jnp.concatenate(
        [
            jnp.concatenate(
                [
                    columns_of(query_weight, Q_WIDTH),
                    columns_of(key_projection, KV_WIDTH),
                    columns_of(value_projection, KV_WIDTH),
                ],
                axis=1,
            ),
            jnp.pad(gains[None, :], ((0, 15), (0, ATTN_WIDTH - gains.shape[0]))),
            lax.dynamic_slice_in_dim(out_weight, r * OUT_ROWS, OUT_ROWS, 0),
        ],
        axis=0,
    )
    attn_own, attn_other = ring_parts(attn_rows)
    token_pieces = spread(tokens)

    out_pieces = jnp.stack([part[ROWS + 16 :] for part in attn_own])

    def out_piece(j):
        step = (chip + CHIPS - (r ^ j)) % CHIPS
        return lax.dynamic_index_in_dim(out_pieces, step, 0, keepdims=False)

    out_own = jnp.concatenate([out_piece(0)] + [flip(out_piece(j), j) for j in (1, 2, 3)], axis=0)
    out_other = other_core(out_own)

    def interleaved(weight):
        cut = weight.reshape(ROWS, 2 * CHIPS, BLOCKS, FF_ROWS)
        return lax.dynamic_index_in_dim(cut, r, 2, keepdims=False).reshape(ROWS, FF_PART)

    down_rows = lax.dynamic_slice_in_dim(down_weight, r * FF_ROWS, FF_ROWS, 0)
    rest = down_rows[:, FF_PART:]
    feed_rows = jnp.concatenate(
        [
            interleaved(gate_weight),
            interleaved(up_weight),
            down_rows[:, :FF_PART],
            jnp.concatenate([rest[i * 32 : (i + 1) * 32] for i in range(3)], axis=1),
        ],
        axis=0,
    )
    feed_rows, _ = lax.optimization_barrier((feed_rows, attn_own[-1]))
    feed_parts = sum(ring_parts(feed_rows), [])
    cotangent_own, _ = lax.optimization_barrier((cotangent_own, out_own))
    cotangent = spread_direct(cotangent_own)

    block_ids = r ^ jnp.arange(BLOCKS, dtype=jnp.int32)
    positions = (block_ids[:, None] * SIZE + jnp.arange(SIZE, dtype=jnp.int32)[None, :]).reshape(-1)
    inv_freq = ROPE_BASE ** (-2.0 * jnp.arange(TURN, dtype=F32) / HEAD_SIZE)
    angles = positions.astype(F32)[:, None] * inv_freq[None, :]
    cosine, sine = jnp.cos(angles), jnp.sin(angles)
    cos_rows = jnp.concatenate([cosine, cosine], axis=1)
    sin_rows = jnp.concatenate([-sine, sine], axis=1)
    starts = picture_starts[0]
    held = (starts[None, :] == block_ids[:, None] * PIECE) & (
        jnp.arange(starts.shape[0], dtype=jnp.int32)[None, :] < picture_count[0]
    )
    info = jnp.concatenate(
        [jnp.stack([r, chip, core]).astype(jnp.int32), jnp.any(held, axis=1).astype(jnp.int32)]
    )

    normed, raw, query, key, value, attn_matrix, gain_rows = on_core(
        project_kernel,
        "project",
        [
            shape((length, MODEL_WIDTH), BF),
            shape((length, QK_WIDTH), F32),
            shape((BLOCKS, SIZE, Q_WIDTH), BF),
            shape((BLOCKS, SIZE, KV_WIDTH), BF),
            shape((BLOCKS, SIZE, KV_WIDTH), BF),
            shape((MODEL_WIDTH, ATTN_WIDTH), BF),
            shape((8, MODEL_WIDTH), F32),
        ],
        (info,),
        (*token_pieces, cos_rows, sin_rows, *attn_own, *attn_other),
        flops=2 * length * MODEL_WIDTH * ATTN_WIDTH,
    )
    mixed, lse, out_matrix, *partial = on_core(
        attend_kernel,
        "attend",
        [
            shape((BLOCKS, SIZE, Q_WIDTH), BF),
            shape((KV_WIDTH // HEAD_SIZE, BLOCKS, GROUP, SIZE), F32),
            shape((Q_WIDTH, MODEL_WIDTH), BF),
        ]
        + partial_shapes(),
        (info,),
        (query, key, value, out_own, out_other),
        flops=4 * length * MODEL_WIDTH * Q_WIDTH,
    )
    after_attn, mlp_own = on_core(
        after_kernel,
        "after",
        [shape((SIZE, MODEL_WIDTH), F32), shape((SIZE, MODEL_WIDTH), BF)],
        (),
        (tokens, gain_rows, *move_partial(*partial)),
    )
    mlp_in = spread(mlp_own)
    gate_up, down, *hidden_grads = on_core(
        prepare_kernel,
        "prepare",
        [shape((MODEL_WIDTH, 2 * FF_PART), BF), shape((FF_PART, MODEL_WIDTH), BF)]
        + [shape((SIZE, FF_PART), F32)] * BLOCKS,
        (info,),
        (*feed_parts, *cotangent),
        flops=2 * length * MODEL_WIDTH * FF_PART,
    )
    hidden_0, both_0, keep = feed((0,), mlp_in[:1], hidden_grads[:1], gate_up)
    hidden_12, both_12, (one_a, keep_high, keep_low, two_a) = feed(
        (1, 2), mlp_in[1:3], hidden_grads[1:3], gate_up
    )
    hidden_3, both_3, (one_b, two_b) = feed((3,), mlp_in[3:], hidden_grads[3:], gate_up)
    hidden = [*hidden_0, *hidden_12, *hidden_3]
    both = [*both_0, *both_12, *both_3]

    one_b, two_b = flip(one_b, 1), flip(two_b, 2)
    one_a, two_a = flip(one_a, 1), flip(two_a, 2)
    low = flip((keep_low + one_b.astype(F32)).astype(BF), 2)
    high = flip((keep_high + two_b.astype(F32)).astype(BF), 1)
    residual_grad, branch_own, mlp_gain_part = on_core(
        residual_kernel,
        "residual",
        [
            shape((SIZE, MODEL_WIDTH), F32),
            shape((SIZE, MODEL_WIDTH), BF),
            shape((1, MODEL_WIDTH), F32),
        ],
        (),
        (out_grad[0], after_attn, gain_rows, *keep, one_a, one_b, two_a, two_b, low, high),
    )
    branch = spread(branch_own)

    feed_kept, feed_away, *partial = pl.pallas_call(
        feed_weights_kernel,
        name="feed_weights",
        in_specs=[pl.BlockSpec(memory_space=pltpu.SMEM)]
        + [pl.BlockSpec(memory_space=pltpu.VMEM)] * 18,
        out_specs=[pl.BlockSpec(memory_space=pltpu.VMEM)] * 7,
        out_shape=[
            shape((CHIPS, PACKED, FF_PART), F32),
            shape((CHIPS, PACKED, FF_PART), BF),
        ]
        + partial_shapes(),
        scratch_shapes=[
            pltpu.VMEM((FF_PART, MODEL_WIDTH), F32),
            pltpu.VMEM((length, MODEL_WIDTH), BF),
        ],
        compiler_params=pltpu.CompilerParams(vmem_limit_bytes=56 << 20),
        cost_estimate=pl.CostEstimate(
            flops=8 * length * MODEL_WIDTH * FF_PART, bytes_accessed=0, transcendentals=0
        ),
    )(info, *mlp_in, *cotangent, *hidden, *both, down)
    (layer_out,) = on_core(
        output_kernel,
        "output",
        [shape((SIZE, MODEL_WIDTH), BF)],
        (),
        (after_attn, *move_partial(*partial)),
    )
    feed_sum = ring_sum(feed_kept, feed_away)

    mixed_grad, out_kept, out_away = pl.pallas_call(
        mixed_grad_kernel,
        name="mixed_grad",
        in_specs=[pl.BlockSpec(memory_space=pltpu.SMEM)]
        + [pl.BlockSpec(memory_space=pltpu.VMEM)] * 7,
        out_specs=[pl.BlockSpec(memory_space=pltpu.VMEM)] * 3,
        out_shape=[
            shape((BLOCKS, SIZE, Q_WIDTH), BF),
            shape((BLOCKS, OUT_ROWS, MODEL_WIDTH), F32),
            shape((BLOCKS, OUT_ROWS, MODEL_WIDTH), BF),
        ],
        scratch_shapes=[pltpu.VMEM((Q_WIDTH, MODEL_WIDTH), F32)],
        compiler_params=pltpu.CompilerParams(vmem_limit_bytes=50 << 20),
        cost_estimate=pl.CostEstimate(
            flops=4 * length * MODEL_WIDTH * Q_WIDTH, bytes_accessed=0, transcendentals=0
        ),
    )(info, mixed, out_matrix, *branch)
    out_pair = (out_kept + other_core(out_away).astype(F32)).astype(BF)
    out_blocks = jnp.stack([out_pair[0]] + [flip(out_pair[j], j) for j in (1, 2, 3)])

    def out_step(t):
        return lax.dynamic_index_in_dim(
            out_blocks, r ^ ((chip + 2 * CHIPS - t) % CHIPS), 0, keepdims=False
        )

    out_sum = out_step(1)
    for t in range(1, CHIPS):
        out_sum = (ring_up(out_sum).astype(F32) + out_step(t + 1).astype(F32)).astype(BF)

    attn_grad, head_part = pl.pallas_call(
        attend_back_kernel,
        name="attend_back",
        in_specs=[pl.BlockSpec(memory_space=pltpu.SMEM)]
        + [pl.BlockSpec(memory_space=pltpu.VMEM)] * 10,
        out_specs=[pl.BlockSpec(memory_space=pltpu.VMEM)] * 2,
        out_shape=[shape((length, ATTN_WIDTH), BF), shape((1, 2 * HEAD_SIZE), F32)],
        scratch_shapes=[pltpu.VMEM((BLOCKS, SIZE, HEAD_SIZE), F32)] * 2,
        compiler_params=pltpu.CompilerParams(vmem_limit_bytes=50 << 20),
        cost_estimate=pl.CostEstimate(
            flops=20 * length * length * Q_WIDTH, bytes_accessed=0, transcendentals=0
        ),
    )(info, query, key, value, mixed, lse, mixed_grad, raw, cos_rows, sin_rows, gain_rows)
    attn_kept, attn_away, *partial = on_core(
        attend_weights_kernel,
        "attend_weights",
        [
            shape((CHIPS, ROWS + 16, ATTN_WIDTH), F32),
            shape((CHIPS, ROWS + 16, ATTN_WIDTH), BF),
        ]
        + partial_shapes(),
        (info,),
        (normed, attn_grad, attn_matrix, mlp_gain_part, head_part, *token_pieces),
        flops=4 * length * MODEL_WIDTH * ATTN_WIDTH,
    )
    attn_sum = ring_sum(attn_kept, attn_away)
    (in_grad,) = on_core(
        final_kernel,
        "final",
        [shape((SIZE, MODEL_WIDTH), BF)],
        (),
        (tokens, gain_rows, residual_grad, *move_partial(*partial)),
    )

    def in_order(value):
        pieces = jnp.stack(spread_direct(value))
        return [lax.dynamic_index_in_dim(pieces, r ^ a, 0, keepdims=False) for a in range(BLOCKS)]

    out_w_grad = jnp.concatenate(in_order(out_sum), axis=0).astype(F32)
    attn_full = in_order(attn_sum)

    def beside(start, stop):
        return jnp.concatenate([one[:ROWS, start:stop] for one in attn_full], axis=1).astype(F32)

    gain_full = sum(one[ROWS : ROWS + 3].astype(F32) for one in attn_full)

    def slice_of(row, width, start=0):
        return lax.dynamic_slice_in_dim(gain_full[row], start + index * width, width, 0)

    feed_full = in_order(feed_sum)

    def woven(first):
        cut = jnp.stack([one[first : first + ROWS] for one in feed_full])
        cut = cut.reshape(BLOCKS, ROWS, 2 * CHIPS, FF_ROWS).transpose(1, 2, 0, 3)
        return cut.reshape(ROWS, 2 * CHIPS * BLOCKS * FF_ROWS).astype(F32)

    def unpacked(one):
        rest = one[2 * ROWS + FF_ROWS :]
        side = jnp.concatenate([rest[:, i * 256 : (i + 1) * 256] for i in range(3)], axis=0)
        return jnp.concatenate([one[2 * ROWS : 2 * ROWS + FF_ROWS], side], axis=1)

    head_rows = query_norm.shape[0]
    return (
        layer_out[None],
        in_grad[None],
        slice_of(0, ROWS),
        beside(0, Q_WIDTH),
        beside(Q_WIDTH, QK_WIDTH),
        beside(QK_WIDTH, ATTN_WIDTH),
        slice_of(2, head_rows),
        slice_of(2, head_rows, HEAD_SIZE),
        out_w_grad,
        slice_of(1, ROWS),
        woven(0),
        woven(ROWS),
        jnp.concatenate([unpacked(one) for one in feed_full], axis=0).astype(F32),
    )


def solution(mesh):
    tokens, matrix, vector = P("shard", "rep", None), P("shard", None), P("shard")
    return jax.shard_map(
        per_device if dict(mesh.shape) == {"rep": 4, "shard": 8} else per_device_any,
        mesh=mesh,
        in_specs=(tokens, tokens, vector, matrix, matrix, matrix, vector, vector, matrix, vector)
        + (matrix, matrix, matrix, matrix, vector),
        out_specs=(tokens, tokens, vector, matrix, matrix, matrix, vector, vector, matrix, vector)
        + (matrix, matrix, matrix),
        check_vma=False,
    )
```

```python
import jax
import jax.numpy as jnp
from jax import lax
from jax.experimental import pallas as pl
from jax.experimental.pallas import tpu as pltpu
from jax.sharding import PartitionSpec as P

MODEL_WIDTH = 1024
QUERY_HEADS = 16
KEY_VALUE_HEADS = 8
HEAD_SIZE = 128
GROUP = QUERY_HEADS // KEY_VALUE_HEADS
PIECE = 256

EPSILON = 1e-06
ROPE_BASE = 1000000.0
SCALE = HEAD_SIZE ** (-0.5)
LOG2E = 1.4426950408889634
BF = jnp.bfloat16
F32 = jnp.float32


def mm(a, b, dims=((1,), (0,))):
    return lax.dot_general(a, b, (dims, ((), ())), preferred_element_type=F32)


def flip(value, bit):
    count = lax.axis_size("rep")
    return lax.ppermute(value, "rep", [(i, i ^ bit) for i in range(count)])


def spread_blocks(value):
    count = lax.axis_size("rep")
    if count == 4:
        half = value.shape[0] // 2
        by_one, by_two = flip(value, 1), flip(value, 2)
        low, high = flip(by_one[:half], 2), flip(by_two[half:], 1)
        return jnp.stack([value, by_one, by_two, jnp.concatenate([low, high], axis=0)])
    blocks = value[None]
    bit = 1
    while bit < count:
        blocks = jnp.concatenate([blocks, flip(blocks, bit)], axis=0)
        bit *= 2
    return blocks


def sum_blocks(parts):
    count = lax.axis_size("rep")
    if count == 4:
        half = parts.shape[1] // 2
        a, b = parts[:, :half], parts[:, half:]
        a_in = flip(jnp.stack([a[1], a[3]]).astype(BF), 1).astype(F32)
        b_in = flip(jnp.stack([b[2], b[3]]).astype(BF), 2).astype(F32)
        a_last = flip((a[2] + a_in[1]).astype(BF), 2).astype(F32)
        b_last = flip((b[1] + b_in[1]).astype(BF), 1).astype(F32)
        return jnp.concatenate([a[0] + a_in[0] + a_last, b[0] + b_in[0] + b_last], axis=0)
    bit = count // 2
    while bit:
        parts = parts[:bit] + flip(parts[bit:].astype(BF), bit).astype(F32)
        bit //= 2
    return parts[0]


def ring_up(value):
    count = lax.axis_size("shard")
    return lax.ppermute(value, "shard", [(i, (i + 2) % count) for i in range(count)])


def other_core(value):
    count = lax.axis_size("shard")
    return lax.ppermute(value, "shard", [(i, i ^ 1) for i in range(count)])


def gather_rows(value):
    count = lax.axis_size("shard")
    chips = count // 2
    index = lax.axis_index("shard")
    chip, core = index // 2, index % 2
    full = jnp.zeros((count,) + value.shape, value.dtype)
    current = value
    for step in range(chips):
        if step:
            current = ring_up(current)
        place = 2 * ((chip + chips - step) % chips)
        full = lax.dynamic_update_index_in_dim(full, current, place + core, 0)
        full = lax.dynamic_update_index_in_dim(full, other_core(current), place + 1 - core, 0)
    return full, current


def scatter_rows(parts):
    count = lax.axis_size("shard")
    chips = count // 2
    index = lax.axis_index("shard")
    chip, core = index // 2, index % 2
    by_chip = parts.reshape((chips, 2) + parts.shape[1:])
    away = lax.dynamic_index_in_dim(by_chip, 1 - core, 1, keepdims=False).astype(BF)
    kept = lax.dynamic_index_in_dim(by_chip, core, 1, keepdims=False)
    paired = kept + other_core(away).astype(F32)

    def own(step):
        return lax.dynamic_index_in_dim(paired, (chip + 2 * chips - step) % chips, 0, keepdims=False)

    running = own(1)
    for step in range(1, chips):
        running = ring_up(running.astype(BF)).astype(F32) + own(step + 1)
    return running


def joint_move(value, pairs):
    shards = lax.axis_size("shard")
    joint = [
        (r0 * shards + 2 * z0 + c, r1 * shards + 2 * z1 + c)
        for (r0, z0), (r1, z1) in pairs
        for c in range(2)
    ]
    return lax.ppermute(value, ("rep", "shard"), joint)


def gather_heads(value):
    replicas, shards = lax.axis_size("rep"), lax.axis_size("shard")
    r, index = lax.axis_index("rep"), lax.axis_index("shard")
    if shards != 2 * replicas:
        full = lax.all_gather(value, "shard", axis=0, tiled=True)
        rows = full.shape[0] // replicas
        return lax.dynamic_slice_in_dim(full, r * rows, rows, 0)
    chip, core = index // 2, index % 2
    up = [((i, z), (i, z + 1)) for i in range(replicas) for z in range(i, replicas - 1)]
    down = [((i, z), (i, z - 1)) for i in range(replicas) for z in range(1, i + 1)]
    moved_up = joint_move(value, [p for p in up if p[0][1] == p[0][0]])
    moved_down = joint_move(value, [p for p in down if p[0][1] == p[0][0]])
    total = moved_up + moved_down
    result = jnp.where(chip == r, value, total)
    moved = total
    for hop in range(2, replicas):
        pairs = [p for p in up if p[0][1] - p[0][0] == hop - 1]
        pairs += [p for p in down if p[0][0] - p[0][1] == hop - 1]
        moved = joint_move(moved, pairs)
        result = result + moved
    other = other_core(result)
    first = jnp.where(core == 0, result, other)
    second = jnp.where(core == 0, other, result)
    return jnp.concatenate([first, second], axis=0)


def scatter_heads(parts):
    replicas, shards = lax.axis_size("rep"), lax.axis_size("shard")
    r, index = lax.axis_index("rep"), lax.axis_index("shard")
    if shards != 2 * replicas:
        rows = parts.shape[0]
        full = jnp.zeros((rows * replicas,) + parts.shape[1:], F32)
        full = lax.dynamic_update_slice_in_dim(full, parts, r * rows, 0)
        owned = lax.psum_scatter(full.astype(BF), "shard", scatter_dimension=0, tiled=True)
        return lax.psum(owned, "rep").astype(F32)
    chip, core = index // 2, index % 2
    halves = parts.reshape((2, -1) + parts.shape[1:])
    away = lax.dynamic_index_in_dim(halves, 1 - core, 0, keepdims=False).astype(BF)
    total = lax.dynamic_index_in_dim(halves, core, 0, keepdims=False) + other_core(away).astype(F32)
    low = total.astype(BF)
    for hop in range(1, replicas):
        pairs = [((i, (i + hop) % replicas), (i, i)) for i in range(replicas)]
        total = total + joint_move(low, pairs).astype(F32)
    low = total.astype(BF)
    if replicas == 4:
        half = low.shape[0] // 2
        one = joint_move(low, [((z, z), (z ^ 1, z)) for z in range(4)])
        two = joint_move(low, [((z, z), (z ^ 2, z)) for z in range(4)])
        top = joint_move(one[:half], [((z ^ 1, z), (z ^ 3, z)) for z in range(4)])
        bottom = joint_move(two[half:], [((z ^ 2, z), (z ^ 3, z)) for z in range(4)])
        rest = one + two + jnp.concatenate([top, bottom], axis=0)
    else:
        rest = jnp.zeros_like(low)
        for other in range(1, replicas):
            rest = rest + joint_move(low, [((z, z), ((z + other) % replicas, z)) for z in range(replicas)])
    return jnp.where(chip == r, low, rest).astype(F32)


def piece_mask(picture_flag, size, heads):
    key = lax.broadcasted_iota(jnp.int32, (size, size * heads), 0)
    query = lax.broadcasted_iota(jnp.int32, (size, size * heads), 1) % size
    return (key <= query) | (picture_flag > 0)


def attention_forward_kernel(info, q_ref, k_ref, v_ref, mixed_ref, lse_ref):
    blocks, size = k_ref.shape[0], k_ref.shape[1]
    own = info[0]
    for last in range(blocks):
        i = own ^ last
        query = jnp.concatenate(
            [q_ref[i, :, h * HEAD_SIZE : (h + 1) * HEAD_SIZE] for h in range(GROUP)], axis=0
        )
        total = jnp.zeros((1, GROUP * size), F32)
        mixed = jnp.zeros((HEAD_SIZE, GROUP * size), F32)
        for block in range(last + 1):
            j = own ^ block
            scores = mm(k_ref[j], query, ((1,), (1,)))
            weights = jnp.exp2(scores * (SCALE * LOG2E))
            if block == last:
                weights = jnp.where(piece_mask(info[1 + i], size, GROUP), weights, 0.0)
            total = total + jnp.sum(weights, axis=0, keepdims=True)
            mixed = mixed + mm(v_ref[j], weights.astype(BF), ((0,), (0,)))
        mixed = mixed * (1.0 / total)
        log_sum = jnp.log2(total)
        for h in range(GROUP):
            columns = slice(h * size, (h + 1) * size)
            mixed_ref[i, :, h * HEAD_SIZE : (h + 1) * HEAD_SIZE] = mixed[:, columns].T.astype(BF)
            lse_ref[i, h : h + 1, :] = log_sum[:, columns]


def attention_backward_kernel(
    info, q_ref, k_ref, v_ref, mixed_ref, lse_ref, grad_ref, dq_ref, dk_ref, dv_ref
):
    blocks, size = k_ref.shape[0], k_ref.shape[1]
    own = info[0]
    dk_ref[...] = jnp.zeros_like(dk_ref)
    dv_ref[...] = jnp.zeros_like(dv_ref)
    for last in range(blocks):
        i = own ^ last
        heads = [slice(h * HEAD_SIZE, (h + 1) * HEAD_SIZE) for h in range(GROUP)]
        query = jnp.concatenate([q_ref[i, :, h] for h in heads], axis=0)
        grad = jnp.concatenate([grad_ref[i, :, h] for h in heads], axis=0)
        mixed = jnp.concatenate([mixed_ref[i, :, h] for h in heads], axis=0)
        delta = jnp.sum((grad.astype(F32) * mixed.astype(F32)).T, axis=0, keepdims=True)
        log_sum = jnp.concatenate([lse_ref[i, h : h + 1, :] for h in range(GROUP)], axis=1)
        dquery = jnp.zeros((HEAD_SIZE, GROUP * size), F32)
        for block in range(last + 1):
            j = own ^ block
            scores = mm(k_ref[j], query, ((1,), (1,)))
            dprobs = mm(v_ref[j], grad, ((1,), (1,)))
            probs = jnp.exp2(scores * (SCALE * LOG2E) - log_sum)
            if block == last:
                probs = jnp.where(piece_mask(info[1 + i], size, GROUP), probs, 0.0)
            dscores = (probs * (dprobs - delta)).astype(BF)
            dv_ref[j] += mm(probs.astype(BF), grad)
            dk_ref[j] += mm(dscores, query)
            dquery = dquery + mm(k_ref[j], dscores, ((0,), (0,)))
        for h in range(GROUP):
            dq_ref[i, :, heads[h]] = dquery[:, h * size : (h + 1) * size].T * SCALE
    dk_ref[...] = dk_ref[...] * SCALE


def attention_specs(blocks, size):
    wide = pl.BlockSpec((blocks, size, GROUP * HEAD_SIZE), lambda g, info: (0, 0, g))
    thin = pl.BlockSpec((blocks, size, HEAD_SIZE), lambda g, info: (0, 0, g))
    rows = pl.BlockSpec((None, blocks, GROUP, size), lambda g, info: (g, 0, 0, 0))
    return wide, thin, rows


def attention_forward(info, query, key, value):
    blocks, size, width = key.shape
    groups = width // HEAD_SIZE
    wide, thin, rows = attention_specs(blocks, size)
    return pl.pallas_call(
        attention_forward_kernel,
        grid_spec=pltpu.PrefetchScalarGridSpec(
            num_scalar_prefetch=1,
            grid=(groups,),
            in_specs=[wide, thin, thin],
            out_specs=[wide, rows],
        ),
        out_shape=[
            jax.ShapeDtypeStruct(query.shape, BF),
            jax.ShapeDtypeStruct((groups, blocks, GROUP, size), F32),
        ],
        compiler_params=pltpu.CompilerParams(vmem_limit_bytes=48 << 20),
        name="attention_forward",
    )(info, query, key, value)


def attention_backward(info, query, key, value, mixed, lse, grad):
    blocks, size, width = key.shape
    groups = width // HEAD_SIZE
    wide, thin, rows = attention_specs(blocks, size)
    return pl.pallas_call(
        attention_backward_kernel,
        grid_spec=pltpu.PrefetchScalarGridSpec(
            num_scalar_prefetch=1,
            grid=(groups,),
            in_specs=[wide, thin, thin, wide, rows, wide],
            out_specs=[wide, thin, thin],
        ),
        out_shape=[
            jax.ShapeDtypeStruct(query.shape, F32),
            jax.ShapeDtypeStruct(key.shape, F32),
            jax.ShapeDtypeStruct(key.shape, F32),
        ],
        compiler_params=pltpu.CompilerParams(vmem_limit_bytes=48 << 20),
        name="attention_backward",
    )(info, query, key, value, mixed, lse, grad)


def inverse_root(values):
    return lax.rsqrt(jnp.mean(values * values, axis=-1, keepdims=True) + EPSILON)


def norm_back(values, inverse, gain, dy):
    weighted = dy * gain
    inner = jnp.mean(values * weighted, axis=-1, keepdims=True)
    return inverse * weighted - values * (inverse * inverse * inverse) * inner


def turn(values):
    return jnp.concatenate([values[..., HEAD_SIZE // 2 :], values[..., : HEAD_SIZE // 2]], axis=-1)


def per_device_any(
    layer_in,
    out_grad,
    attn_norm,
    query_weight,
    key_projection,
    value_projection,
    query_norm,
    key_norm,
    out_weight,
    mlp_norm,
    gate_weight,
    up_weight,
    down_weight,
    picture_starts,
    picture_count,
):
    replicas, shards = lax.axis_size("rep"), lax.axis_size("shard")
    r = lax.axis_index("rep")
    size = layer_in.shape[1]
    length = size * replicas
    rows = attn_norm.shape[0]
    q_width = QUERY_HEADS // replicas * HEAD_SIZE
    kv_width = KEY_VALUE_HEADS // replicas * HEAD_SIZE
    attn_width = q_width + 2 * kv_width
    ff_rows = down_weight.shape[0] // replicas
    ff = ff_rows * shards

    def columns_of(weight, width):
        return lax.dynamic_slice_in_dim(weight, r * width, width, 1)

    gains = jnp.concatenate([attn_norm, mlp_norm, query_norm, key_norm])
    head_rows = query_norm.shape[0]
    gain_rows = jnp.zeros((16, attn_width), BF).at[0, : gains.shape[0]].set(gains)
    attn_rows = jnp.concatenate(
        [
            jnp.concatenate(
                [
                    columns_of(query_weight, q_width),
                    columns_of(key_projection, kv_width),
                    columns_of(value_projection, kv_width),
                ],
                axis=1,
            ),
            gain_rows,
        ],
        axis=0,
    )

    def interleaved(weight):
        cut = weight.reshape(rows, shards, replicas, ff_rows)
        return lax.dynamic_index_in_dim(cut, r, 2, keepdims=False).reshape(rows, ff)

    gate_up_rows = jnp.concatenate([interleaved(gate_weight), interleaved(up_weight)], axis=1)
    down_rows = lax.dynamic_slice_in_dim(down_weight, r * ff_rows, ff_rows, 0)

    tokens = layer_in[0]
    all_tokens = spread_blocks(tokens)
    attn_all, attn_last = gather_rows(attn_rows)
    out_weight, _ = lax.optimization_barrier((out_weight, attn_last))
    out_matrix = gather_heads(out_weight)
    gate_up_rows, down_rows, _ = lax.optimization_barrier((gate_up_rows, down_rows, attn_last))
    gate_up_all, _ = gather_rows(gate_up_rows)
    down_all, _ = gather_rows(down_rows)
    cotangent_low, _ = lax.optimization_barrier((out_grad[0], all_tokens))
    all_cotangent = spread_blocks(cotangent_low).reshape(length, MODEL_WIDTH)

    attn_matrix = attn_all[:, :rows].reshape(MODEL_WIDTH, attn_width)
    gain_all = attn_all[:, rows].astype(F32)
    attn_gain = gain_all[:, :rows].reshape(MODEL_WIDTH)
    mlp_gain = gain_all[:, rows : 2 * rows].reshape(MODEL_WIDTH)
    query_gain = gain_all[:, 2 * rows : 2 * rows + head_rows].reshape(HEAD_SIZE)
    key_gain = gain_all[:, 2 * rows + head_rows : 2 * rows + 2 * head_rows].reshape(HEAD_SIZE)
    gate_up_matrix = gate_up_all.reshape(MODEL_WIDTH, 2 * ff)
    down_matrix = down_all.reshape(ff, MODEL_WIDTH)

    block_ids = r ^ jnp.arange(replicas, dtype=jnp.int32)
    positions = (block_ids[:, None] * size + jnp.arange(size, dtype=jnp.int32)[None, :]).reshape(-1)
    half = HEAD_SIZE // 2
    inv_freq = ROPE_BASE ** (-2.0 * jnp.arange(half, dtype=F32) / HEAD_SIZE)
    angles = positions.astype(F32)[:, None] * inv_freq[None, :]
    cosine, sine = jnp.cos(angles), jnp.sin(angles)
    cos_row = jnp.concatenate([cosine, cosine], axis=1)[:, None, :]
    sin_row = jnp.concatenate([-sine, sine], axis=1)[:, None, :]
    starts = picture_starts[0]
    held = (starts[None, :] == block_ids[:, None] * PIECE) & (
        jnp.arange(starts.shape[0], dtype=jnp.int32)[None, :] < picture_count[0]
    )
    info = jnp.concatenate([r[None].astype(jnp.int32), jnp.any(held, axis=1).astype(jnp.int32)])

    wide = all_tokens.reshape(length, MODEL_WIDTH).astype(F32)
    token_inverse = inverse_root(wide)
    normed = (wide * token_inverse * attn_gain).astype(BF)
    raw = mm(normed, attn_matrix)
    query_raw = raw[:, :q_width].reshape(length, -1, HEAD_SIZE)
    key_raw = raw[:, q_width : q_width + kv_width].reshape(length, -1, HEAD_SIZE)
    value = raw[:, q_width + kv_width :].astype(BF).reshape(replicas, size, kv_width)

    def rotated(values, gain):
        scaled = values * inverse_root(values) * gain
        return (scaled * cos_row + turn(scaled) * sin_row).astype(BF).reshape(replicas, size, -1)

    query, key = rotated(query_raw, query_gain), rotated(key_raw, key_gain)
    mixed, lse = attention_forward(info, query, key, value)
    mixed_rows = mixed.reshape(length, q_width)
    after_attn = tokens.astype(F32) + sum_blocks(
        mm(mixed_rows, out_matrix).reshape(replicas, size, MODEL_WIDTH)
    )
    after_inverse = inverse_root(after_attn)
    scaled_attn = after_attn * after_inverse
    mlp_in = spread_blocks((scaled_attn * mlp_gain).astype(BF)).reshape(length, MODEL_WIDTH)
    gate_up = mm(mlp_in, gate_up_matrix)
    gate_act, up_act = gate_up[:, :ff], gate_up[:, ff:]
    sigmoid = 1.0 / (1.0 + jnp.exp(-gate_act))
    silu = gate_act * sigmoid
    hidden = (silu * up_act).astype(BF)

    hidden_grad = mm(all_cotangent, down_matrix, ((1,), (1,)))
    gate_grad = (hidden_grad * up_act * sigmoid * (1.0 + gate_act * (1.0 - sigmoid))).astype(BF)
    up_grad = (hidden_grad * silu).astype(BF)
    gate_up_grad = jnp.concatenate([gate_grad, up_grad], axis=1)
    mlp_in_part = mm(gate_up_grad, gate_up_matrix, ((1,), (1,)))
    mlp_in_grad = sum_blocks(mlp_in_part.reshape(replicas, size, MODEL_WIDTH))
    residual_grad = out_grad[0].astype(F32) + norm_back(
        after_attn, after_inverse, mlp_gain, mlp_in_grad
    )
    mlp_gain_part = jnp.sum(mlp_in_grad * scaled_attn, axis=0)
    branch_grad = spread_blocks(residual_grad.astype(BF)).reshape(length, MODEL_WIDTH)

    layer_out = after_attn + sum_blocks(mm(hidden, down_matrix).reshape(replicas, size, MODEL_WIDTH))
    gate_up_w = scatter_rows(
        mm(mlp_in, gate_up_grad, ((0,), (0,))).reshape(shards, rows, 2 * ff)
    )
    down_w = scatter_rows(
        mm(hidden, all_cotangent, ((0,), (0,))).reshape(shards, ff_rows, MODEL_WIDTH)
    )

    out_w_grad = scatter_heads(mm(mixed_rows, branch_grad, ((0,), (0,))))
    mixed_grad = mm(branch_grad, out_matrix, ((1,), (1,))).astype(BF)
    dq, dk, dv = attention_backward(
        info, query, key, value, mixed, lse, mixed_grad.reshape(replicas, size, q_width)
    )

    def head_back(values, gain, dy):
        dy = dy.reshape(length, -1, HEAD_SIZE)
        dy = dy * cos_row - turn(dy) * sin_row
        inverse = inverse_root(values)
        gain_part = jnp.sum(dy * values * inverse, axis=(0, 1))
        return norm_back(values, inverse, gain, dy).astype(BF).reshape(length, -1), gain_part

    query_grad, query_gain_part = head_back(query_raw, query_gain, dq)
    key_grad, key_gain_part = head_back(key_raw, key_gain, dk)
    attn_grad = jnp.concatenate(
        [query_grad, key_grad, dv.reshape(length, kv_width).astype(BF)], axis=1
    )
    normed_part = mm(attn_grad, attn_matrix, ((1,), (1,)))
    normed_grad = sum_blocks(normed_part.reshape(replicas, size, MODEL_WIDTH))
    attn_gain_part = jnp.sum(normed_part * (wide * token_inverse), axis=0)
    own_tokens = tokens.astype(F32)
    in_grad = residual_grad + norm_back(own_tokens, inverse_root(own_tokens), attn_gain, normed_grad)

    gain_parts = jnp.concatenate(
        [
            attn_gain_part.reshape(shards, rows),
            mlp_gain_part.reshape(shards, rows),
            query_gain_part.reshape(shards, head_rows),
            key_gain_part.reshape(shards, head_rows),
        ],
        axis=1,
    )
    gain_block = jnp.zeros((shards, 16, attn_width), F32).at[:, 0, : gain_parts.shape[1]].set(gain_parts)
    attn_w_parts = mm(normed, attn_grad, ((0,), (0,))).reshape(shards, rows, attn_width)
    attn_w = scatter_rows(jnp.concatenate([attn_w_parts, gain_block], axis=1))

    def in_order(value):
        spread = spread_blocks(value.astype(BF))
        return jnp.stack(
            [lax.dynamic_index_in_dim(spread, r ^ a, 0, keepdims=False) for a in range(replicas)]
        ).astype(F32)

    attn_full = in_order(attn_w)
    gain_full = jnp.sum(attn_full[:, rows], axis=0)

    def beside(values):
        return jnp.concatenate([values[a] for a in range(replicas)], axis=1)

    query_w_grad = beside(attn_full[:, :rows, :q_width])
    key_w_grad = beside(attn_full[:, :rows, q_width : q_width + kv_width])
    value_w_grad = beside(attn_full[:, :rows, q_width + kv_width :])
    gate_up_full = in_order(gate_up_w)

    def woven(values):
        cut = values.reshape(replicas, rows, shards, ff_rows)
        return cut.transpose(1, 2, 0, 3).reshape(rows, shards * replicas * ff_rows)

    gate_w_grad = woven(gate_up_full[:, :, :ff])
    up_w_grad = woven(gate_up_full[:, :, ff:])
    down_w_grad = in_order(down_w).reshape(replicas * ff_rows, MODEL_WIDTH)

    return (
        layer_out.astype(BF)[None],
        in_grad.astype(BF)[None],
        gain_full[:rows],
        query_w_grad,
        key_w_grad,
        value_w_grad,
        gain_full[2 * rows : 2 * rows + head_rows],
        gain_full[2 * rows + head_rows : 2 * rows + 2 * head_rows],
        out_w_grad,
        gain_full[rows : 2 * rows],
        gate_w_grad,
        up_w_grad,
        down_w_grad,
    )


BLOCKS = 4
CHIPS = 4
ROWS = 128
SIZE = 256
HALF = SIZE // 2
Q_WIDTH = QUERY_HEADS // BLOCKS * HEAD_SIZE
KV_WIDTH = KEY_VALUE_HEADS // BLOCKS * HEAD_SIZE
ATTN_WIDTH = Q_WIDTH + 2 * KV_WIDTH
GROUPS = KV_WIDTH // HEAD_SIZE
GROUP_Q = GROUP * HEAD_SIZE
GROUP_WIDTH = GROUP_Q + 2 * HEAD_SIZE
FF_ROWS = 96
FF_PART = 768
OUT_ROWS = 64
PACKED = 3 * ROWS
TURN = HEAD_SIZE // 2


def shape(dims, dtype):
    return jax.ShapeDtypeStruct(dims, dtype)


def on_core(body, name, outs, scalars, args, far=(), scratch=(), limit=16):
    return pl.pallas_call(
        body,
        name=name,
        in_specs=[pl.BlockSpec(memory_space=pltpu.SMEM)] * len(scalars)
        + [pl.BlockSpec(memory_space=pltpu.VMEM)] * len(args)
        + [pl.BlockSpec(memory_space=pl.ANY)] * len(far),
        out_specs=[pl.BlockSpec(memory_space=pltpu.VMEM)] * len(outs),
        out_shape=outs,
        scratch_shapes=list(scratch),
        compiler_params=pltpu.CompilerParams(vmem_limit_bytes=limit << 20),
    )(*scalars, *args, *far)


class Loads:
    def __init__(self, semaphores):
        self.semaphores, self.used = semaphores, 0

    def __call__(self, source, target):
        copy = pltpu.make_async_copy(source, target, self.semaphores.at[self.used])
        self.used += 1
        copy.start()
        return copy


def partial_shapes():
    return [
        shape((SIZE, MODEL_WIDTH), BF),
        shape((SIZE, MODEL_WIDTH), BF),
        shape((HALF, MODEL_WIDTH), F32),
        shape((HALF, MODEL_WIDTH), F32),
        shape((SIZE, MODEL_WIDTH), F32),
    ]


def put_partial(refs, j, part):
    by_one, by_two, keep_low, keep_high, keep = refs
    if j == 0:
        keep[...] = part
    if j == 1:
        by_one[:HALF] = part[:HALF].astype(BF)
        keep_high[...] = part[HALF:]
    if j == 2:
        by_two[:HALF] = part[HALF:].astype(BF)
        keep_low[...] = part[:HALF]
    if j == 3:
        by_one[HALF:] = part[:HALF].astype(BF)
        by_two[HALF:] = part[HALF:].astype(BF)


def move_partial(by_one, by_two, keep_low, keep_high, keep):
    one, two = flip(by_one, 1), flip(by_two, 2)
    low = flip((keep_low + one[HALF:].astype(F32)).astype(BF), 2)
    high = flip((keep_high + two[HALF:].astype(F32)).astype(BF), 1)
    return keep, one, two, low, high


def joined(keep, one, two, low, high):
    top = keep[:HALF] + one[:HALF].astype(F32) + low[...].astype(F32)
    bottom = keep[HALF:] + two[:HALF].astype(F32) + high[...].astype(F32)
    return jnp.concatenate([top, bottom], axis=0)


def spread(value):
    half = value.shape[0] // 2
    one, two = flip(value, 1), flip(value, 2)
    return value, one, two, flip(one[:half], 2), flip(two[half:], 1)


def spread_direct(value):
    return value, flip(value, 1), flip(value, 2), flip(value, 3)


def tie(values, *others):
    return lax.optimization_barrier((values, others))[0]


def block_of(refs, j):
    if j < 3 or len(refs) == 4:
        return refs[j][...]
    return jnp.concatenate([ref[...] for ref in refs[3:]], axis=0)


def load_paired(loads, refs, which, target):
    at = slice(which * HALF, (which + 1) * HALF)
    return [
        loads(refs[n].at[at, :], target.at[n * HALF : (n + 1) * HALF, :]) for n in range(2 * BLOCKS)
    ]


def part_shard(info, t):
    chip = lax.rem(info[1] + CHIPS - t % CHIPS, CHIPS)
    return 2 * chip + (info[2] if t < CHIPS else 1 - info[2])


def pack_kernel(info, wq, wk, wv, wo, attn_gain, mlp_gain, query_gain, key_gain, out):
    for g in range(GROUPS):
        at = g * GROUP_WIDTH
        head = info[0] * GROUPS + g
        out[:ROWS, at : at + GROUP_Q] = wq[:, pl.ds(pl.multiple_of(head * GROUP_Q, GROUP_Q), GROUP_Q)]
        for weight, start in ((wk, at + GROUP_Q), (wv, at + GROUP_Q + HEAD_SIZE)):
            columns = pl.ds(pl.multiple_of(head * HEAD_SIZE, HEAD_SIZE), HEAD_SIZE)
            out[:ROWS, start : start + HEAD_SIZE] = weight[:, columns]
    tile = slice(ROWS, ROWS + 16)
    out[tile, :] = jnp.zeros((16, ATTN_WIDTH), BF)
    out[tile, :ROWS] = jnp.broadcast_to(attn_gain[...], (16, ROWS))
    out[tile, ROWS : 2 * ROWS] = jnp.broadcast_to(mlp_gain[...], (16, ROWS))
    out[tile, 2 * ROWS : 2 * ROWS + 16] = jnp.broadcast_to(query_gain[...], (16, 16))
    out[tile, 3 * ROWS : 3 * ROWS + 16] = jnp.broadcast_to(key_gain[...], (16, 16))
    out[ROWS + 16 :, :] = wo[pl.ds(pl.multiple_of(info[0] * OUT_ROWS, OUT_ROWS), OUT_ROWS), :]


def pack_feed_kernel(info, gate, up, down, out):
    for a in range(BLOCKS):

        @pl.when(info[0] == a)
        def _():
            for weight, first in ((gate, 0), (up, ROWS)):
                cut = []
                for s in range(2 * CHIPS):
                    start = (s * BLOCKS + a) * FF_ROWS
                    cut.append(weight[:, start : start + FF_ROWS])
                out[first : first + ROWS, :] = jnp.concatenate(cut, axis=1)
            rows = slice(a * FF_ROWS, (a + 1) * FF_ROWS)
            out[2 * ROWS : 2 * ROWS + FF_ROWS, :] = down[rows, :FF_PART]
            for i in range(3):
                rows = slice(a * FF_ROWS + i * 32, a * FF_ROWS + (i + 1) * 32)
                out[2 * ROWS + FF_ROWS :, i * 256 : (i + 1) * 256] = down[rows, FF_PART:]


def pick_kernel(info, *refs):
    parts, outs, semaphores = refs[:CHIPS], refs[CHIPS:-1], refs[-1]
    for j in range(BLOCKS):
        step = lax.rem(info[1] + CHIPS - (info[0] ^ j), CHIPS)
        for t in range(CHIPS):

            @pl.when(step == t)
            def _():
                pltpu.make_async_copy(
                    parts[t].at[ROWS + 16 :, :], outs[j], semaphores.at[j]
                ).start()

    for j in range(BLOCKS):
        pltpu.make_async_copy(parts[0].at[ROWS + 16 :, :], outs[j], semaphores.at[j]).wait()


def project_kernel(info, cos_ref, sin_ref, *refs):
    parts, tokens = refs[:8], refs[8:16]
    normed_ref, raw_ref, q_ref, k_ref, v_ref, w_ref, gain_ref = refs[16:23]
    all_tokens, gain_rows, semaphores = refs[23:]
    loads = Loads(semaphores)
    gain_loads, part_loads = [], []
    shards = [part_shard(info, t) for t in range(2 * CHIPS)]
    for t in range(2 * CHIPS):
        gain_loads.append(loads(parts[t].at[ROWS : ROWS + 16, :], gain_rows.at[t]))
    token_loads = load_paired(loads, tokens, 0, all_tokens)
    for t in range(2 * CHIPS):
        at = pl.ds(pl.multiple_of(shards[t] * ROWS, ROWS), ROWS)
        part_loads.append(loads(parts[t].at[:ROWS, :], w_ref.at[at, :]))
    gain_ref[...] = jnp.zeros_like(gain_ref)
    low_lane = lax.broadcasted_iota(jnp.int32, (8, HEAD_SIZE), 1) < 16
    for t in range(2 * CHIPS):
        gain_loads[t].wait()
        columns = pl.ds(pl.multiple_of(shards[t] * ROWS, ROWS), ROWS)
        row = gain_rows[t, :, : 4 * ROWS].astype(F32)[:8]
        gain_ref[0:1, columns] = row[:1, :ROWS]
        gain_ref[1:2, columns] = row[:1, ROWS : 2 * ROWS]
        for start in (0, HEAD_SIZE):
            mine = jnp.where(low_lane, row[:, 2 * ROWS + start : 3 * ROWS + start], 0.0)
            gain_ref[2:3, start : start + HEAD_SIZE] += pltpu.roll(mine, shards[t] * 16, 1)[:1]
    for j in range(BLOCKS):
        here = slice(j * SIZE, (j + 1) * SIZE)
        for copy in token_loads[2 * j : 2 * j + 2]:
            copy.wait()
        wide = all_tokens[here, :].astype(F32)
        normed = (wide * inverse_root(wide) * gain_ref[0:1, :]).astype(BF)
        normed_ref[here, :] = normed
    for copy in part_loads:
        copy.wait()
    for j in range(BLOCKS):
        here = slice(j * SIZE, (j + 1) * SIZE)
        raw = mm(normed_ref[here, :], w_ref[...])
        cosine, sine = cos_ref[here, :], sin_ref[here, :]
        for g in range(GROUPS):
            for h in range(GROUP + 1):
                at = g * GROUP_WIDTH + h * HEAD_SIZE
                one = raw[:, at : at + HEAD_SIZE]
                raw_ref[g, here, h * HEAD_SIZE : (h + 1) * HEAD_SIZE] = one
                gain_at = HEAD_SIZE if h == GROUP else 0
                scaled = one * inverse_root(one) * gain_ref[2:3, gain_at : gain_at + HEAD_SIZE]
                rotated = (scaled * cosine + pltpu.roll(scaled, TURN, 1) * sine).astype(BF)
                if h == GROUP:
                    k_ref[g, j] = rotated
                else:
                    q_ref[g, j, h * SIZE : (h + 1) * SIZE, :] = rotated
            v_ref[g, j] = raw[:, (g + 1) * GROUP_WIDTH - HEAD_SIZE : (g + 1) * GROUP_WIDTH].astype(BF)


def attend_kernel(info, q_ref, k_ref, v_ref, mixed_ref, lse_ref):
    own = info[0]
    for last in range(BLOCKS - 1, -1, -1):
        i = own ^ last
        for g in range(GROUPS):
            query = q_ref[g, i]
            total = jnp.zeros((1, GROUP * SIZE), F32)
            mixed = jnp.zeros((HEAD_SIZE, GROUP * SIZE), F32)
            for block in range(last + 1):
                j = own ^ block
                scores = mm(k_ref[g, j], query, ((1,), (1,)))
                weights = jnp.exp2(scores * (SCALE * LOG2E))
                if block == last:
                    weights = jnp.where(piece_mask(info[3 + i], SIZE, GROUP), weights, 0.0)
                total = total + jnp.sum(weights, axis=0, keepdims=True)
                mixed = mixed + mm(v_ref[g, j], weights.astype(BF), ((0,), (0,)))
            mixed = mixed * (1.0 / total)
            for h in range(GROUP):
                columns = slice(h * SIZE, (h + 1) * SIZE)
                at = (g * GROUP + h) * HEAD_SIZE
                mixed_ref[i, :, at : at + HEAD_SIZE] = mixed[:, columns].T.astype(BF)
            lse_ref[g, i] = jnp.log2(total)


def out_kernel(info, mixed_ref, *refs):
    own_pieces, other_pieces, out_ref, partial = refs[:4], refs[4:8], refs[8], refs[9:]
    own = info[0]
    for core, rows in ((info[2], own_pieces), (1 - info[2], other_pieces)):
        for q in range(BLOCKS):
            at = pl.multiple_of(core * SIZE + (own ^ q) * OUT_ROWS, OUT_ROWS)
            out_ref[pl.ds(at, OUT_ROWS), :] = rows[q][...]
    for j in (3, 1, 2, 0):
        put_partial(partial, j, mm(mixed_ref[j], out_ref[...]))


def after_kernel(tokens, gain_ref, *refs):
    after_ref, low_ref = refs[5:]
    after = tokens[...].astype(F32) + joined(*refs[:5])
    after_ref[...] = after
    low_ref[...] = (after * inverse_root(after) * gain_ref[1:2, :]).astype(BF)


def prepare_kernel(info, *refs):
    parts, pieces = refs[:8], refs[8:16]
    gate_up_ref, down_ref, cotangent = refs[16:19]
    grads, semaphores = refs[19:23], refs[23]
    loads = Loads(semaphores)
    down_loads, gate_loads = [], []
    cotangent_loads = load_paired(loads, pieces, 1, cotangent)
    for t in range(2 * CHIPS):
        s = part_shard(info, t)
        at = pl.ds(pl.multiple_of(s * FF_ROWS, 32), FF_ROWS)
        rows = slice(2 * ROWS, 2 * ROWS + FF_ROWS)
        down_loads.append(loads(parts[t].at[rows, :], down_ref.at[at, :FF_PART]))
        for i in range(3):
            at = pl.ds(pl.multiple_of(s * FF_ROWS + i * 32, 32), 32)
            rest = parts[t].at[2 * ROWS + FF_ROWS :, i * 256 : (i + 1) * 256]
            down_loads.append(loads(rest, down_ref.at[at, FF_PART:]))
    for t in range(2 * CHIPS):
        at = pl.ds(pl.multiple_of(part_shard(info, t) * ROWS, ROWS), ROWS)
        gate_loads.append(loads(parts[t].at[:ROWS, :], gate_up_ref.at[at, :FF_PART]))
        gate_loads.append(loads(parts[t].at[ROWS : 2 * ROWS, :], gate_up_ref.at[at, FF_PART:]))
    for copy in cotangent_loads + down_loads:
        copy.wait()
    for j in range(BLOCKS):
        here = slice(j * SIZE, (j + 1) * SIZE)
        grads[j][...] = mm(cotangent[here, :], down_ref[...], ((1,), (1,)))
    for copy in gate_loads:
        copy.wait()


def feed_kernel(blocks, *refs):
    count = len(blocks)
    last = blocks == (3,)
    extra = 2 if last else count
    inputs, hidden_grads = refs[:extra], refs[extra : extra + count]
    gate_up_ref = refs[extra + count]
    if last:
        first_a, second_b = refs[extra + count + 1 : extra + count + 3]
    outs = refs[extra + count + (3 if last else 1) :]
    for n, j in enumerate(blocks):
        tokens = jnp.concatenate([inputs[0][...], inputs[1][...]], axis=0) if last else inputs[n][...]
        hidden_ref, both_ref = outs[2 * n : 2 * n + 2]
        gate_up = mm(tokens, gate_up_ref[...])
        gate, up = gate_up[:, :FF_PART], gate_up[:, FF_PART:]
        sigmoid = 1.0 / (1.0 + jnp.exp(-gate))
        silu = gate * sigmoid
        hidden_ref[...] = (silu * up).astype(BF)
        grad = hidden_grads[n][...]
        both_ref[:, :FF_PART] = (grad * up * sigmoid * (1.0 + gate * (1.0 - sigmoid))).astype(BF)
        both_ref[:, FF_PART:] = (grad * silu).astype(BF)
        part = mm(both_ref[...], gate_up_ref[...], ((1,), (1,)))
        first, second = outs[2 * count + 2 * n : 2 * count + 2 * n + 2]
        if last:
            first[:HALF] = first_a[...]
            first[HALF:] = part[:HALF].astype(BF)
            second[:HALF] = second_b[...]
            second[HALF:] = part[HALF:].astype(BF)
        else:
            first[...] = part[:HALF].astype(first.dtype)
            second[...] = part[HALF:].astype(second.dtype)


FEED_TYPES = {0: (F32, F32), 1: (BF, F32), 2: (F32, BF), 3: (BF, BF)}


def feed(blocks, inputs, hidden_grads, gate_up, earlier=()):
    outs = []
    for _ in blocks:
        outs += [shape((SIZE, FF_PART), BF), shape((SIZE, 2 * FF_PART), BF)]
    for j in blocks:
        outs += [shape((SIZE if j == 3 else HALF, MODEL_WIDTH), dtype) for dtype in FEED_TYPES[j]]

    def body(*refs):
        feed_kernel(blocks, *refs)

    args = (*inputs, *hidden_grads, gate_up, *earlier)
    result = on_core(body, "feed", outs, (), args)
    count = len(blocks)
    hidden, both = result[0 : 2 * count : 2], result[1 : 2 * count : 2]
    return hidden, both, result[2 * count :]


def split_rows(info, kept, away, t, at, values):
    half = values.shape[0] // 2
    first, second = values[:half], values[half:]
    is_first = info[2] == 0
    kept[t, at : at + half, :] = jnp.where(is_first, first, second)
    away[t, at : at + half, :] = jnp.where(is_first, second, first).astype(BF)


def feed_weights_kernel(info, cotangent, *refs):
    hidden, both, mlp_in = refs[:4], refs[4:8], refs[8:13]
    kept, away, down_grad, stored, semaphores = refs[13:]
    loads = Loads(semaphores)
    copies = [loads(mlp_in[j], stored.at[j * SIZE : (j + 1) * SIZE, :]) for j in range(3)]
    copies += [
        loads(mlp_in[3 + n], stored.at[3 * SIZE + n * HALF : 3 * SIZE + (n + 1) * HALF, :])
        for n in range(2)
    ]
    both_all = jnp.concatenate([ref[...] for ref in both], axis=0)
    hidden_all = jnp.concatenate([ref[...] for ref in hidden], axis=0)
    down_grad[...] = mm(hidden_all, cotangent[...], ((0,), (0,)))
    for copy in copies:
        copy.wait()
    for t in range(CHIPS):
        chip = lax.rem(info[1] + 2 * CHIPS - (t + 1), CHIPS)
        columns = stored[:, pl.ds(pl.multiple_of(chip * 2 * ROWS, 2 * ROWS), 2 * ROWS)]
        product = mm(columns, both_all, ((0,), (0,)))
        split_rows(info, kept, away, t, 0, product[:, :FF_PART])
        split_rows(info, kept, away, t, ROWS, product[:, FF_PART:])
        for core, target in ((info[2], kept), (1 - info[2], away)):
            at = pl.multiple_of((2 * chip + core) * FF_ROWS, 32)
            rows = down_grad[pl.ds(at, FF_ROWS), :].astype(target.dtype)
            target[t, 2 * ROWS : 2 * ROWS + FF_ROWS, :] = rows[:, :FF_PART]
            for i in range(3):
                target[t, 2 * ROWS + FF_ROWS :, i * 256 : (i + 1) * 256] = rows[
                    i * 32 : (i + 1) * 32, FF_PART:
                ]


def down_kernel(down_ref, *refs):
    hidden, partial = refs[:4], refs[4:]
    for j in (3, 1, 2, 0):
        put_partial(partial, j, mm(hidden[j][...], down_ref[...]))


def residual_kernel(cotangent, after_ref, gain_ref, *refs):
    grad_ref, low_ref, gain_part = refs[-3:]
    keep_a, keep_b, one, two, low, high = refs[:6]
    top = keep_a[...] + one[:HALF].astype(F32) + low[...].astype(F32)
    bottom = keep_b[...] + two[:HALF].astype(F32) + high[...].astype(F32)
    mlp_in_grad = jnp.concatenate([top, bottom], axis=0)
    after = after_ref[...]
    inverse = inverse_root(after)
    gain_part[...] = jnp.sum(mlp_in_grad * (after * inverse), axis=0, keepdims=True)
    grad = cotangent[...].astype(F32) + norm_back(after, inverse, gain_ref[1:2, :], mlp_in_grad)
    grad_ref[...] = grad
    low_ref[...] = grad.astype(BF)


def mixed_grad_kernel(info, mixed_ref, out_ref, *refs):
    branch, (grad_ref, kept, away, scratch) = refs[:5], refs[5:]
    own = info[0]
    for j in range(BLOCKS):
        grad_ref[j] = mm(block_of(branch, j), out_ref[...], ((1,), (1,))).astype(BF)
    branch_all = jnp.concatenate([block_of(branch, j) for j in range(BLOCKS)], axis=0)
    mixed_all = jnp.concatenate([mixed_ref[j] for j in range(BLOCKS)], axis=0)
    scratch[...] = mm(mixed_all, branch_all, ((0,), (0,)))
    for core, target in ((info[2], kept), (1 - info[2], away)):
        for q in range(BLOCKS):
            at = pl.multiple_of(core * SIZE + (own ^ q) * OUT_ROWS, OUT_ROWS)
            target[q] = scratch[pl.ds(at, OUT_ROWS), :].astype(target.dtype)


def head_back(grad, cosine, sine, raw, gain):
    dy = grad * cosine - pltpu.roll(grad, TURN, 1) * sine
    inverse = inverse_root(raw)
    gain_part = jnp.sum(dy * (raw * inverse), axis=0, keepdims=True)
    return norm_back(raw, inverse, gain, dy).astype(BF), gain_part


def attend_back_kernel(g, info, lse_ref, mixed_ref, grad_ref, mlp_part, gain_ref, *refs):
    far, (out_ref, kept, away) = refs[:8], refs[8:11]
    dk_ref, dv_ref, q_ref, k_ref, v_ref, raw_ref, cos_ref, sin_ref, normed_ref, w_ref, semaphores = refs[11:]
    loads = Loads(semaphores)
    width = slice(g * GROUP_WIDTH, (g + 1) * GROUP_WIDTH)
    first = [loads(far[n].at[g], near) for n, near in enumerate((q_ref, k_ref, v_ref))]
    second = [loads(far[3].at[g], raw_ref), loads(far[4], cos_ref), loads(far[5], sin_ref)]
    third = [loads(far[6], normed_ref), loads(far[7].at[:, width], w_ref)]
    own = info[0]
    query_part = jnp.zeros((1, HEAD_SIZE), F32)
    key_part = jnp.zeros((1, HEAD_SIZE), F32)
    dk_ref[...] = jnp.zeros_like(dk_ref)
    dv_ref[...] = jnp.zeros_like(dv_ref)
    for copy in first:
        copy.wait()
    for last in range(BLOCKS):
        i = own ^ last
        rows = pl.ds(pl.multiple_of(i * SIZE, SIZE), SIZE)
        heads = [slice((g * GROUP + h) * HEAD_SIZE, (g * GROUP + h + 1) * HEAD_SIZE) for h in range(GROUP)]
        query = q_ref[i]
        grad = jnp.concatenate([grad_ref[i, :, h] for h in heads], axis=0)
        mixed = jnp.concatenate([mixed_ref[i, :, h] for h in heads], axis=0)
        delta = jnp.sum((grad.astype(F32) * mixed.astype(F32)).T, axis=0, keepdims=True)
        log_sum = lse_ref[g, i]
        dquery = jnp.zeros((HEAD_SIZE, GROUP * SIZE), F32)
        for block in range(last + 1):
            j = own ^ block
            scores = mm(k_ref[j], query, ((1,), (1,)))
            dprobs = mm(v_ref[j], grad, ((1,), (1,)))
            probs = jnp.exp2(scores * (SCALE * LOG2E) - log_sum)
            if block == last:
                probs = jnp.where(piece_mask(info[3 + i], SIZE, GROUP), probs, 0.0)
            dscores = (probs * (dprobs - delta)).astype(BF)
            dv_ref[j] += mm(probs.astype(BF), grad)
            dk_ref[j] += mm(dscores, query)
            dquery = dquery + mm(k_ref[j], dscores, ((0,), (0,)))
        if last == 0:
            for copy in second:
                copy.wait()
        for h in range(GROUP):
            at = slice(h * HEAD_SIZE, (h + 1) * HEAD_SIZE)
            back, part = head_back(
                dquery[:, h * SIZE : (h + 1) * SIZE].T * SCALE,
                cos_ref[rows, :],
                sin_ref[rows, :],
                raw_ref[rows, at],
                gain_ref[2:3, :HEAD_SIZE],
            )
            out_ref[rows, at] = back
            query_part = query_part + part
    for j in range(BLOCKS):
        rows = slice(j * SIZE, (j + 1) * SIZE)
        at = slice(GROUP_Q, GROUP_Q + HEAD_SIZE)
        back, part = head_back(
            dk_ref[j] * SCALE,
            cos_ref[rows, :],
            sin_ref[rows, :],
            raw_ref[rows, at],
            gain_ref[2:3, HEAD_SIZE : 2 * HEAD_SIZE],
        )
        out_ref[rows, at] = back
        key_part = key_part + part
        out_ref[rows, GROUP_Q + HEAD_SIZE :] = dv_ref[j].astype(BF)
    for copy in third:
        copy.wait()
    row = lax.broadcasted_iota(jnp.int32, (16, GROUP_WIDTH), 0)
    for t in range(CHIPS):
        chip = lax.rem(info[1] + 2 * CHIPS - (t + 1), CHIPS)
        at = pl.ds(pl.multiple_of(chip * 2 * ROWS, 2 * ROWS), 2 * ROWS)
        product = mm(normed_ref[:, at], out_ref[...], ((0,), (0,)))
        split_rows(info, kept, away, t, 0, product)
        inner = jnp.sum(product * w_ref[at, :].astype(F32), axis=1, keepdims=True)
        inner = jnp.broadcast_to(inner, (2 * ROWS, ROWS)).T[0:1] / gain_ref[0:1, at]
        mlp = mlp_part[0:1, at] if g == 0 else jnp.zeros_like(inner)
        for is_first, half in ((True, slice(0, ROWS)), (False, slice(ROWS, 2 * ROWS))):
            values = jnp.concatenate([inner[:, half], mlp[:, half], query_part, key_part], axis=1)
            values = jnp.where(row == 0, values, 0.0)

            @pl.when((info[2] == 0) == is_first)
            def _():
                kept[t, ROWS:, :] = values

            @pl.when((info[2] == 0) != is_first)
            def _():
                away[t, ROWS:, :] = values.astype(BF)


def normed_grad_kernel(w_ref, *refs):
    grads, partial = refs[:GROUPS], refs[GROUPS:]
    for j in (3, 1, 2, 0):
        here = slice(j * SIZE, (j + 1) * SIZE)
        grad = jnp.concatenate([ref[here, :] for ref in grads], axis=1)
        put_partial(partial, j, mm(grad, w_ref[...], ((1,), (1,))))


def final_kernel(tokens, gain_ref, residual, *refs):
    grad_ref = refs[5]
    wide = tokens[...].astype(F32)
    dy = joined(*refs[:5])
    back = norm_back(wide, inverse_root(wide), gain_ref[0:1, :], dy)
    grad_ref[...] = (residual[...] + back).astype(BF)


def output_kernel(after_ref, *refs):
    refs[5][...] = (after_ref[...] + joined(*refs[:5])).astype(BF)


def unpack_feed_kernel(info, *refs):
    pieces, (gate_ref, up_ref, down_ref, scratch) = refs[:5], refs[5:]
    for j in range(BLOCKS):
        scratch[info[0] ^ j] = block_of(pieces, j).astype(F32)
    for first, target in ((0, gate_ref), (ROWS, up_ref)):
        for s in range(0, 2 * CHIPS):
            columns = slice(s * FF_ROWS, (s + 1) * FF_ROWS)
            cut = [scratch[a, first : first + ROWS, columns] for a in range(BLOCKS)]
            target[:, s * BLOCKS * FF_ROWS : (s + 1) * BLOCKS * FF_ROWS] = jnp.concatenate(cut, axis=1)
    for a in range(BLOCKS):
        at = slice(a * FF_ROWS, (a + 1) * FF_ROWS)
        down_ref[at, :FF_PART] = scratch[a, 2 * ROWS : 2 * ROWS + FF_ROWS, :]
        for i in range(3):
            at = slice(a * FF_ROWS + i * 32, a * FF_ROWS + (i + 1) * 32)
            down_ref[at, FF_PART:] = scratch[a, 2 * ROWS + FF_ROWS :, i * 256 : (i + 1) * 256]


def unpack_attend_kernel(info, *refs):
    pieces, (query_ref, key_ref, value_ref, out_ref, gain_ref) = (refs[:4], refs[4:8]), refs[8:]
    gains = jnp.zeros((8, GROUP_WIDTH), F32)
    for g in range(GROUPS):
        for j in range(BLOCKS):
            piece = pieces[g][j]
            head = (info[0] ^ j) * GROUPS + g
            values = piece[:ROWS, :].astype(F32)
            wide = pl.ds(pl.multiple_of(head * GROUP_Q, GROUP_Q), GROUP_Q)
            thin = pl.ds(pl.multiple_of(head * HEAD_SIZE, HEAD_SIZE), HEAD_SIZE)
            query_ref[:, wide] = values[:, :GROUP_Q]
            key_ref[:, thin] = values[:, GROUP_Q : GROUP_Q + HEAD_SIZE]
            value_ref[:, thin] = values[:, GROUP_Q + HEAD_SIZE :]
            gains = gains + piece[ROWS : ROWS + 16, :].astype(F32)[:8]
            if g == 0:
                rows = pl.ds(pl.multiple_of((info[0] ^ j) * OUT_ROWS, OUT_ROWS), OUT_ROWS)
                top = piece[ROWS + 16 : ROWS + 16 + OUT_ROWS, :].astype(F32)
                out_ref[rows, :GROUP_WIDTH] = top
                out_ref[rows, GROUP_WIDTH:] = piece[ROWS + 16 + OUT_ROWS :, :].astype(F32)
    gain_ref[...] = gains


def ring_parts(value, then):
    own, other = [value], [other_core(value)]
    for t in range(1, CHIPS):
        ready = then.get(t, ())
        if t > 1:
            ready = (ready, other[t - 2])
        own.append(ring_up(tie(own[-1], ready)))
        other.append(other_core(own[-1]))
    return own, other


def ring_sum(kept, away, then, beside=None):
    crossed = other_core(away)

    def term(t, moved):
        value = kept[t] + crossed[t].astype(F32)
        count = value.shape[0]
        if moved is not None:
            value = value + moved[:count].astype(F32)
        value = value.astype(BF)
        if beside is not None:
            extra = beside(t + 1)
            if moved is not None:
                extra = (moved[count:].astype(F32) + extra.astype(F32)).astype(BF)
            value = jnp.concatenate([value, extra], axis=0)
        return value

    running = [term(0, None)]
    for t in range(1, CHIPS):
        running.append(term(t, ring_up(tie(running[-1], then.get(t, ())))))
    return running


def per_device(
    layer_in,
    out_grad,
    attn_norm,
    query_weight,
    key_projection,
    value_projection,
    query_norm,
    key_norm,
    out_weight,
    mlp_norm,
    gate_weight,
    up_weight,
    down_weight,
    picture_starts,
    picture_count,
):
    r, index = lax.axis_index("rep"), lax.axis_index("shard")
    chip, core = index // 2, index % 2
    length = BLOCKS * SIZE
    tokens, cotangent_own = layer_in[0], out_grad[0]

    block_ids = r ^ jnp.arange(BLOCKS, dtype=jnp.int32)
    starts = picture_starts[0]
    held = (starts[None, :] == block_ids[:, None] * PIECE) & (
        jnp.arange(starts.shape[0], dtype=jnp.int32)[None, :] < picture_count[0]
    )
    place = jnp.stack([r, chip, core]).astype(jnp.int32)
    info = jnp.concatenate([place, jnp.any(held, axis=1).astype(jnp.int32)])

    (attn_rows,) = on_core(
        pack_kernel,
        "pack",
        [shape((ROWS + 16 + OUT_ROWS, ATTN_WIDTH), BF)],
        (place,),
        (query_weight, key_projection, value_projection, out_weight)
        + tuple(gain.reshape(1, -1) for gain in (attn_norm, mlp_norm, query_norm, key_norm)),
    )
    low_half, high_half = tie(
        tuple(jnp.concatenate([tokens[at], cotangent_own[at]]) for at in (slice(0, HALF), slice(HALF, SIZE))),
        attn_rows,
    )
    one = flip(low_half, 1), flip(high_half, 1)
    two = flip(low_half, 2), flip(high_half, 2)
    pieces = (low_half, high_half, *one, *two, flip(one[0], 2), flip(two[1], 1))
    (feed_rows,) = on_core(
        pack_feed_kernel,
        "pack_feed",
        [shape((PACKED, FF_PART), BF)],
        (place,),
        tie((gate_weight, up_weight, down_weight), attn_rows),
    )

    positions = (block_ids[:, None] * SIZE + jnp.arange(SIZE, dtype=jnp.int32)[None, :]).reshape(-1)
    inv_freq = ROPE_BASE ** (-2.0 * jnp.arange(TURN, dtype=F32) / HEAD_SIZE)
    angles = positions.astype(F32)[:, None] * inv_freq[None, :]
    cosine, sine = jnp.cos(angles), jnp.sin(angles)
    cos_rows = jnp.concatenate([cosine, cosine], axis=1)
    sin_rows = jnp.concatenate([-sine, sine], axis=1)

    attn_own, attn_other = ring_parts(
        attn_rows, {2: (feed_rows, info), 3: (one, two, cos_rows, sin_rows)}
    )

    picked = on_core(
        pick_kernel,
        "pick",
        [shape((OUT_ROWS, MODEL_WIDTH), BF)] * BLOCKS,
        (place,),
        (),
        attn_own,
        [pltpu.SemaphoreType.DMA((BLOCKS,))],
    )
    out_own = [picked[0]] + [flip(picked[j], j) for j in (1, 2, 3)]

    normed, raw, query, key, value, attn_matrix, gain_rows = on_core(
        project_kernel,
        "project",
        [
            shape((length, MODEL_WIDTH), BF),
            shape((GROUPS, length, GROUP_Q + HEAD_SIZE), F32),
            shape((GROUPS, BLOCKS, GROUP * SIZE, HEAD_SIZE), BF),
            shape((GROUPS, BLOCKS, SIZE, HEAD_SIZE), BF),
            shape((GROUPS, BLOCKS, SIZE, HEAD_SIZE), BF),
            shape((MODEL_WIDTH, ATTN_WIDTH), BF),
            shape((8, MODEL_WIDTH), F32),
        ],
        (info,),
        (cos_rows, sin_rows),
        (*attn_own, *attn_other, *pieces),
        [
            pltpu.VMEM((length, MODEL_WIDTH), BF),
            pltpu.VMEM((2 * CHIPS, 16, ATTN_WIDTH), BF),
            pltpu.SemaphoreType.DMA((6 * CHIPS,)),
        ],
    )
    mixed, lse = on_core(
        attend_kernel,
        "attend",
        [
            shape((BLOCKS, SIZE, Q_WIDTH), BF),
            shape((GROUPS, BLOCKS, 1, GROUP * SIZE), F32),
        ],
        (info,),
        (query, key, value),
    )
    out_own = tie(out_own, query)
    out_other = other_core(jnp.concatenate(out_own, axis=0))
    out_other = [out_other[j * OUT_ROWS : (j + 1) * OUT_ROWS] for j in range(BLOCKS)]
    out_matrix, *partial = on_core(
        out_kernel,
        "out",
        [shape((Q_WIDTH, MODEL_WIDTH), BF)] + partial_shapes(),
        (info,),
        (mixed, *out_own, *out_other),
    )
    feed_own, feed_other = ring_parts(tie(feed_rows, attn_own[-1]), {2: mixed, 3: partial[0]})
    partial = move_partial(*partial)
    after_attn, mlp_own = on_core(
        after_kernel,
        "after",
        [shape((SIZE, MODEL_WIDTH), F32), shape((SIZE, MODEL_WIDTH), BF)],
        (),
        (tokens, gain_rows, *partial),
    )
    mlp_in = spread(mlp_own)
    gate_up, down, cotangent, *hidden_grads = on_core(
        prepare_kernel,
        "prepare",
        [
            shape((MODEL_WIDTH, 2 * FF_PART), BF),
            shape((FF_PART, MODEL_WIDTH), BF),
            shape((length, MODEL_WIDTH), BF),
        ]
        + [shape((SIZE, FF_PART), F32)] * BLOCKS,
        (info,),
        (),
        (*tie((*feed_own, *feed_other), mlp_own), *pieces),
        [pltpu.SemaphoreType.DMA((14 * CHIPS,))],
    )
    hidden_0, both_0, keep = feed((0,), mlp_in[:1], hidden_grads[:1], gate_up)
    hidden_12, both_12, (one_a, keep_high, keep_low, two_a) = feed(
        (1, 2), tie(mlp_in[1:3], both_0), hidden_grads[1:3], gate_up
    )
    hidden_3, both_3, (one, two) = feed(
        (3,), tie(mlp_in[3:], both_12), hidden_grads[3:], gate_up, (one_a, two_a)
    )
    hidden = [*hidden_0, *hidden_12, *hidden_3]
    both = [*both_0, *both_12, *both_3]

    feed_kept, feed_away = on_core(
        feed_weights_kernel,
        "feed_weights",
        [
            shape((CHIPS, PACKED, FF_PART), F32),
            shape((CHIPS, PACKED, FF_PART), BF),
        ],
        (info,),
        (cotangent, *hidden, *both),
        mlp_in,
        [
            pltpu.VMEM((FF_PART, MODEL_WIDTH), F32),
            pltpu.VMEM((length, MODEL_WIDTH), BF),
            pltpu.SemaphoreType.DMA((5,)),
        ],
        24,
    )
    feed_ring = ring_sum(feed_kept, feed_away, {})
    one, two = tie((flip(one, 1), flip(two, 2)), feed_kept)
    low = flip((keep_low + one[HALF:].astype(F32)).astype(BF), 2)
    high = flip((keep_high + two[HALF:].astype(F32)).astype(BF), 1)
    residual_grad, branch_own, mlp_gain_part = on_core(
        residual_kernel,
        "residual",
        [
            shape((SIZE, MODEL_WIDTH), F32),
            shape((SIZE, MODEL_WIDTH), BF),
            shape((1, MODEL_WIDTH), F32),
        ],
        (),
        (cotangent_own, after_attn, gain_rows, *tie((*keep, one, two, low, high), feed_ring[0])),
    )
    branch = spread(branch_own)
    layer_partial = on_core(
        down_kernel, "down", partial_shapes(), (), tie((down, *hidden), branch_own)
    )

    mixed_grad, out_kept, out_away = on_core(
        mixed_grad_kernel,
        "mixed_grad",
        [
            shape((BLOCKS, SIZE, Q_WIDTH), BF),
            shape((BLOCKS, OUT_ROWS, MODEL_WIDTH), F32),
            shape((BLOCKS, OUT_ROWS, MODEL_WIDTH), BF),
        ],
        (info,),
        (mixed, out_matrix, *tie(branch, layer_partial, feed_ring[1])),
        (),
        [pltpu.VMEM((Q_WIDTH, MODEL_WIDTH), F32)],
    )
    out_pair = (out_kept + other_core(out_away).astype(F32)).astype(BF)
    out_pair = [out_pair[j] for j in range(BLOCKS)]
    out_moved = [out_pair[0]] + [flip(out_pair[j], j) for j in (1, 2, 3)]

    def back(g, grad):
        def body(*refs):
            attend_back_kernel(g, *refs)

        return on_core(
            body,
            "attend_back",
            [
                shape((length, GROUP_WIDTH), BF),
                shape((CHIPS, ROWS + 16, GROUP_WIDTH), F32),
                shape((CHIPS, ROWS + 16, GROUP_WIDTH), BF),
            ],
            (info,),
            (lse, mixed, grad, mlp_gain_part, gain_rows),
            (query, key, value, raw, cos_rows, sin_rows, normed, attn_matrix),
            [
                pltpu.VMEM((BLOCKS, SIZE, HEAD_SIZE), F32),
                pltpu.VMEM((BLOCKS, SIZE, HEAD_SIZE), F32),
                pltpu.VMEM((BLOCKS, GROUP * SIZE, HEAD_SIZE), BF),
                pltpu.VMEM((BLOCKS, SIZE, HEAD_SIZE), BF),
                pltpu.VMEM((BLOCKS, SIZE, HEAD_SIZE), BF),
                pltpu.VMEM((length, GROUP_Q + HEAD_SIZE), F32),
                pltpu.VMEM((length, HEAD_SIZE), F32),
                pltpu.VMEM((length, HEAD_SIZE), F32),
                pltpu.VMEM((length, MODEL_WIDTH), BF),
                pltpu.VMEM((MODEL_WIDTH, GROUP_WIDTH), BF),
                pltpu.SemaphoreType.DMA((8,)),
            ],
        )

    grad_0, kept_0, away_0 = back(0, tie(mixed_grad, out_pair))
    out_blocks = jnp.stack(tie(out_moved, grad_0))

    def out_step(t):
        block = lax.dynamic_index_in_dim(
            out_blocks, r ^ ((chip + 2 * CHIPS - t) % CHIPS), 0, keepdims=False
        )
        return jnp.concatenate([block[:, :GROUP_WIDTH], block[:, GROUP_WIDTH:]], axis=0)

    layer_pieces = move_partial(*tie(layer_partial, grad_0))
    attn_first = ring_sum(kept_0, away_0, {}, out_step)
    grad_1, kept_1, away_1 = back(1, tie(mixed_grad, attn_first[0], feed_ring[2]))
    attn_second = ring_sum(kept_1, away_1, {})
    partial = on_core(
        normed_grad_kernel,
        "normed_grad",
        partial_shapes(),
        (),
        (attn_matrix, *tie((grad_0, grad_1), attn_second[0])),
    )
    (layer_out,) = on_core(
        output_kernel,
        "output",
        [shape((SIZE, MODEL_WIDTH), BF)],
        (),
        (after_attn, *layer_pieces),
    )
    (in_grad,) = on_core(
        final_kernel,
        "final",
        [shape((SIZE, MODEL_WIDTH), BF)],
        (),
        (tokens, gain_rows, residual_grad, *move_partial(*partial)),
    )

    gate_w_grad, up_w_grad, down_w_grad = on_core(
        unpack_feed_kernel,
        "unpack_feed",
        [
            shape((ROWS, 2 * CHIPS * BLOCKS * FF_ROWS), F32),
            shape((ROWS, 2 * CHIPS * BLOCKS * FF_ROWS), F32),
            shape((BLOCKS * FF_ROWS, MODEL_WIDTH), F32),
        ],
        (place,),
        spread(feed_ring[-1]),
        (),
        [pltpu.VMEM((BLOCKS, PACKED, FF_PART), F32)],
    )
    query_w_grad, key_w_grad, value_w_grad, out_w_grad, gain_full = on_core(
        unpack_attend_kernel,
        "unpack_attend",
        [
            shape((ROWS, QUERY_HEADS * HEAD_SIZE), F32),
            shape((ROWS, KEY_VALUE_HEADS * HEAD_SIZE), F32),
            shape((ROWS, KEY_VALUE_HEADS * HEAD_SIZE), F32),
            shape((SIZE, MODEL_WIDTH), F32),
            shape((8, GROUP_WIDTH), F32),
        ],
        (place,),
        (*spread_direct(attn_first[-1]), *spread_direct(attn_second[-1])),
    )
    gains = gain_full[0]
    head_rows = query_norm.shape[0]

    def slice_of(start, width):
        return lax.dynamic_slice_in_dim(gains, start + index * width, width, 0)

    return (
        layer_out[None],
        in_grad[None],
        gains[:ROWS],
        query_w_grad,
        key_w_grad,
        value_w_grad,
        slice_of(2 * ROWS, head_rows),
        slice_of(2 * ROWS + HEAD_SIZE, head_rows),
        out_w_grad,
        gains[ROWS : 2 * ROWS],
        gate_w_grad,
        up_w_grad,
        down_w_grad,
    )


def solution(mesh):
    tokens, matrix, vector = P("shard", "rep", None), P("shard", None), P("shard")
    return jax.shard_map(
        per_device if dict(mesh.shape) == {"rep": 4, "shard": 8} else per_device_any,
        mesh=mesh,
        in_specs=(tokens, tokens, vector, matrix, matrix, matrix, vector, vector, matrix, vector)
        + (matrix, matrix, matrix, matrix, vector),
        out_specs=(tokens, tokens, vector, matrix, matrix, matrix, vector, vector, matrix, vector)
        + (matrix, matrix, matrix),
        check_vma=False,
    )
```

```python
import jax
import jax.numpy as jnp
from jax import lax
from jax.experimental import pallas as pl
from jax.experimental.pallas import tpu as pltpu
from jax.sharding import PartitionSpec as P

MODEL_WIDTH = 1024
QUERY_HEADS = 16
KEY_VALUE_HEADS = 8
HEAD_SIZE = 128
GROUP = QUERY_HEADS // KEY_VALUE_HEADS
PIECE = 256

EPSILON = 1e-06
ROPE_BASE = 1000000.0
SCALE = HEAD_SIZE ** (-0.5)
LOG2E = 1.4426950408889634
BF = jnp.bfloat16
F32 = jnp.float32


def mm(a, b, dims=((1,), (0,))):
    return lax.dot_general(a, b, (dims, ((), ())), preferred_element_type=F32)


def flip(value, bit):
    count = lax.axis_size("rep")
    return lax.ppermute(value, "rep", [(i, i ^ bit) for i in range(count)])


def spread_blocks(value):
    count = lax.axis_size("rep")
    if count == 4:
        half = value.shape[0] // 2
        by_one, by_two = flip(value, 1), flip(value, 2)
        low, high = flip(by_one[:half], 2), flip(by_two[half:], 1)
        return jnp.stack([value, by_one, by_two, jnp.concatenate([low, high], axis=0)])
    blocks = value[None]
    bit = 1
    while bit < count:
        blocks = jnp.concatenate([blocks, flip(blocks, bit)], axis=0)
        bit *= 2
    return blocks


def sum_blocks(parts):
    count = lax.axis_size("rep")
    if count == 4:
        half = parts.shape[1] // 2
        a, b = parts[:, :half], parts[:, half:]
        a_in = flip(jnp.stack([a[1], a[3]]).astype(BF), 1).astype(F32)
        b_in = flip(jnp.stack([b[2], b[3]]).astype(BF), 2).astype(F32)
        a_last = flip((a[2] + a_in[1]).astype(BF), 2).astype(F32)
        b_last = flip((b[1] + b_in[1]).astype(BF), 1).astype(F32)
        return jnp.concatenate([a[0] + a_in[0] + a_last, b[0] + b_in[0] + b_last], axis=0)
    bit = count // 2
    while bit:
        parts = parts[:bit] + flip(parts[bit:].astype(BF), bit).astype(F32)
        bit //= 2
    return parts[0]


def ring_up(value):
    count = lax.axis_size("shard")
    return lax.ppermute(value, "shard", [(i, (i + 2) % count) for i in range(count)])


def other_core(value):
    count = lax.axis_size("shard")
    return lax.ppermute(value, "shard", [(i, i ^ 1) for i in range(count)])


def gather_rows(value):
    count = lax.axis_size("shard")
    chips = count // 2
    index = lax.axis_index("shard")
    chip, core = index // 2, index % 2
    full = jnp.zeros((count,) + value.shape, value.dtype)
    current = value
    for step in range(chips):
        if step:
            current = ring_up(current)
        place = 2 * ((chip + chips - step) % chips)
        full = lax.dynamic_update_index_in_dim(full, current, place + core, 0)
        full = lax.dynamic_update_index_in_dim(full, other_core(current), place + 1 - core, 0)
    return full, current


def scatter_rows(parts):
    count = lax.axis_size("shard")
    chips = count // 2
    index = lax.axis_index("shard")
    chip, core = index // 2, index % 2
    by_chip = parts.reshape((chips, 2) + parts.shape[1:])
    away = lax.dynamic_index_in_dim(by_chip, 1 - core, 1, keepdims=False).astype(BF)
    kept = lax.dynamic_index_in_dim(by_chip, core, 1, keepdims=False)
    paired = kept + other_core(away).astype(F32)

    def own(step):
        return lax.dynamic_index_in_dim(paired, (chip + 2 * chips - step) % chips, 0, keepdims=False)

    running = own(1)
    for step in range(1, chips):
        running = ring_up(running.astype(BF)).astype(F32) + own(step + 1)
    return running


def joint_move(value, pairs):
    shards = lax.axis_size("shard")
    joint = [
        (r0 * shards + 2 * z0 + c, r1 * shards + 2 * z1 + c)
        for (r0, z0), (r1, z1) in pairs
        for c in range(2)
    ]
    return lax.ppermute(value, ("rep", "shard"), joint)


def gather_heads(value):
    replicas, shards = lax.axis_size("rep"), lax.axis_size("shard")
    r, index = lax.axis_index("rep"), lax.axis_index("shard")
    if shards != 2 * replicas:
        full = lax.all_gather(value, "shard", axis=0, tiled=True)
        rows = full.shape[0] // replicas
        return lax.dynamic_slice_in_dim(full, r * rows, rows, 0)
    chip, core = index // 2, index % 2
    up = [((i, z), (i, z + 1)) for i in range(replicas) for z in range(i, replicas - 1)]
    down = [((i, z), (i, z - 1)) for i in range(replicas) for z in range(1, i + 1)]
    moved_up = joint_move(value, [p for p in up if p[0][1] == p[0][0]])
    moved_down = joint_move(value, [p for p in down if p[0][1] == p[0][0]])
    total = moved_up + moved_down
    result = jnp.where(chip == r, value, total)
    moved = total
    for hop in range(2, replicas):
        pairs = [p for p in up if p[0][1] - p[0][0] == hop - 1]
        pairs += [p for p in down if p[0][0] - p[0][1] == hop - 1]
        moved = joint_move(moved, pairs)
        result = result + moved
    other = other_core(result)
    first = jnp.where(core == 0, result, other)
    second = jnp.where(core == 0, other, result)
    return jnp.concatenate([first, second], axis=0)


def scatter_heads(parts):
    replicas, shards = lax.axis_size("rep"), lax.axis_size("shard")
    r, index = lax.axis_index("rep"), lax.axis_index("shard")
    if shards != 2 * replicas:
        rows = parts.shape[0]
        full = jnp.zeros((rows * replicas,) + parts.shape[1:], F32)
        full = lax.dynamic_update_slice_in_dim(full, parts, r * rows, 0)
        owned = lax.psum_scatter(full.astype(BF), "shard", scatter_dimension=0, tiled=True)
        return lax.psum(owned, "rep").astype(F32)
    chip, core = index // 2, index % 2
    halves = parts.reshape((2, -1) + parts.shape[1:])
    away = lax.dynamic_index_in_dim(halves, 1 - core, 0, keepdims=False).astype(BF)
    total = lax.dynamic_index_in_dim(halves, core, 0, keepdims=False) + other_core(away).astype(F32)
    low = total.astype(BF)
    for hop in range(1, replicas):
        pairs = [((i, (i + hop) % replicas), (i, i)) for i in range(replicas)]
        total = total + joint_move(low, pairs).astype(F32)
    low = total.astype(BF)
    if replicas == 4:
        half = low.shape[0] // 2
        one = joint_move(low, [((z, z), (z ^ 1, z)) for z in range(4)])
        two = joint_move(low, [((z, z), (z ^ 2, z)) for z in range(4)])
        top = joint_move(one[:half], [((z ^ 1, z), (z ^ 3, z)) for z in range(4)])
        bottom = joint_move(two[half:], [((z ^ 2, z), (z ^ 3, z)) for z in range(4)])
        rest = one + two + jnp.concatenate([top, bottom], axis=0)
    else:
        rest = jnp.zeros_like(low)
        for other in range(1, replicas):
            rest = rest + joint_move(low, [((z, z), ((z + other) % replicas, z)) for z in range(replicas)])
    return jnp.where(chip == r, low, rest).astype(F32)


def piece_mask(picture_flag, size, heads):
    key = lax.broadcasted_iota(jnp.int32, (size, size * heads), 0)
    query = lax.broadcasted_iota(jnp.int32, (size, size * heads), 1) % size
    return (key <= query) | (picture_flag > 0)


def attention_forward_kernel(info, q_ref, k_ref, v_ref, mixed_ref, lse_ref):
    blocks, size = k_ref.shape[0], k_ref.shape[1]
    own = info[0]
    for last in range(blocks):
        i = own ^ last
        query = jnp.concatenate(
            [q_ref[i, :, h * HEAD_SIZE : (h + 1) * HEAD_SIZE] for h in range(GROUP)], axis=0
        )
        total = jnp.zeros((1, GROUP * size), F32)
        mixed = jnp.zeros((HEAD_SIZE, GROUP * size), F32)
        for block in range(last + 1):
            j = own ^ block
            scores = mm(k_ref[j], query, ((1,), (1,)))
            weights = jnp.exp2(scores * (SCALE * LOG2E))
            if block == last:
                weights = jnp.where(piece_mask(info[1 + i], size, GROUP), weights, 0.0)
            total = total + jnp.sum(weights, axis=0, keepdims=True)
            mixed = mixed + mm(v_ref[j], weights.astype(BF), ((0,), (0,)))
        mixed = mixed * (1.0 / total)
        log_sum = jnp.log2(total)
        for h in range(GROUP):
            columns = slice(h * size, (h + 1) * size)
            mixed_ref[i, :, h * HEAD_SIZE : (h + 1) * HEAD_SIZE] = mixed[:, columns].T.astype(BF)
            lse_ref[i, h : h + 1, :] = log_sum[:, columns]


def attention_backward_kernel(
    info, q_ref, k_ref, v_ref, mixed_ref, lse_ref, grad_ref, dq_ref, dk_ref, dv_ref
):
    blocks, size = k_ref.shape[0], k_ref.shape[1]
    own = info[0]
    dk_ref[...] = jnp.zeros_like(dk_ref)
    dv_ref[...] = jnp.zeros_like(dv_ref)
    for last in range(blocks):
        i = own ^ last
        heads = [slice(h * HEAD_SIZE, (h + 1) * HEAD_SIZE) for h in range(GROUP)]
        query = jnp.concatenate([q_ref[i, :, h] for h in heads], axis=0)
        grad = jnp.concatenate([grad_ref[i, :, h] for h in heads], axis=0)
        mixed = jnp.concatenate([mixed_ref[i, :, h] for h in heads], axis=0)
        delta = jnp.sum((grad.astype(F32) * mixed.astype(F32)).T, axis=0, keepdims=True)
        log_sum = jnp.concatenate([lse_ref[i, h : h + 1, :] for h in range(GROUP)], axis=1)
        dquery = jnp.zeros((HEAD_SIZE, GROUP * size), F32)
        for block in range(last + 1):
            j = own ^ block
            scores = mm(k_ref[j], query, ((1,), (1,)))
            dprobs = mm(v_ref[j], grad, ((1,), (1,)))
            probs = jnp.exp2(scores * (SCALE * LOG2E) - log_sum)
            if block == last:
                probs = jnp.where(piece_mask(info[1 + i], size, GROUP), probs, 0.0)
            dscores = (probs * (dprobs - delta)).astype(BF)
            dv_ref[j] += mm(probs.astype(BF), grad)
            dk_ref[j] += mm(dscores, query)
            dquery = dquery + mm(k_ref[j], dscores, ((0,), (0,)))
        for h in range(GROUP):
            dq_ref[i, :, heads[h]] = dquery[:, h * size : (h + 1) * size].T * SCALE
    dk_ref[...] = dk_ref[...] * SCALE


def attention_specs(blocks, size):
    wide = pl.BlockSpec((blocks, size, GROUP * HEAD_SIZE), lambda g, info: (0, 0, g))
    thin = pl.BlockSpec((blocks, size, HEAD_SIZE), lambda g, info: (0, 0, g))
    rows = pl.BlockSpec((None, blocks, GROUP, size), lambda g, info: (g, 0, 0, 0))
    return wide, thin, rows


def attention_forward(info, query, key, value):
    blocks, size, width = key.shape
    groups = width // HEAD_SIZE
    wide, thin, rows = attention_specs(blocks, size)
    return pl.pallas_call(
        attention_forward_kernel,
        grid_spec=pltpu.PrefetchScalarGridSpec(
            num_scalar_prefetch=1,
            grid=(groups,),
            in_specs=[wide, thin, thin],
            out_specs=[wide, rows],
        ),
        out_shape=[
            jax.ShapeDtypeStruct(query.shape, BF),
            jax.ShapeDtypeStruct((groups, blocks, GROUP, size), F32),
        ],
        compiler_params=pltpu.CompilerParams(vmem_limit_bytes=48 << 20),
        name="attention_forward",
    )(info, query, key, value)


def attention_backward(info, query, key, value, mixed, lse, grad):
    blocks, size, width = key.shape
    groups = width // HEAD_SIZE
    wide, thin, rows = attention_specs(blocks, size)
    return pl.pallas_call(
        attention_backward_kernel,
        grid_spec=pltpu.PrefetchScalarGridSpec(
            num_scalar_prefetch=1,
            grid=(groups,),
            in_specs=[wide, thin, thin, wide, rows, wide],
            out_specs=[wide, thin, thin],
        ),
        out_shape=[
            jax.ShapeDtypeStruct(query.shape, F32),
            jax.ShapeDtypeStruct(key.shape, F32),
            jax.ShapeDtypeStruct(key.shape, F32),
        ],
        compiler_params=pltpu.CompilerParams(vmem_limit_bytes=48 << 20),
        name="attention_backward",
    )(info, query, key, value, mixed, lse, grad)


def inverse_root(values):
    return lax.rsqrt(jnp.mean(values * values, axis=-1, keepdims=True) + EPSILON)


def norm_back(values, inverse, gain, dy):
    weighted = dy * gain
    inner = jnp.mean(values * weighted, axis=-1, keepdims=True)
    return inverse * weighted - values * (inverse * inverse * inverse) * inner


def turn(values):
    return jnp.concatenate([values[..., HEAD_SIZE // 2 :], values[..., : HEAD_SIZE // 2]], axis=-1)


def per_device_any(
    layer_in,
    out_grad,
    attn_norm,
    query_weight,
    key_projection,
    value_projection,
    query_norm,
    key_norm,
    out_weight,
    mlp_norm,
    gate_weight,
    up_weight,
    down_weight,
    picture_starts,
    picture_count,
):
    replicas, shards = lax.axis_size("rep"), lax.axis_size("shard")
    r = lax.axis_index("rep")
    size = layer_in.shape[1]
    length = size * replicas
    rows = attn_norm.shape[0]
    q_width = QUERY_HEADS // replicas * HEAD_SIZE
    kv_width = KEY_VALUE_HEADS // replicas * HEAD_SIZE
    attn_width = q_width + 2 * kv_width
    ff_rows = down_weight.shape[0] // replicas
    ff = ff_rows * shards

    def columns_of(weight, width):
        return lax.dynamic_slice_in_dim(weight, r * width, width, 1)

    gains = jnp.concatenate([attn_norm, mlp_norm, query_norm, key_norm])
    head_rows = query_norm.shape[0]
    gain_rows = jnp.zeros((16, attn_width), BF).at[0, : gains.shape[0]].set(gains)
    attn_rows = jnp.concatenate(
        [
            jnp.concatenate(
                [
                    columns_of(query_weight, q_width),
                    columns_of(key_projection, kv_width),
                    columns_of(value_projection, kv_width),
                ],
                axis=1,
            ),
            gain_rows,
        ],
        axis=0,
    )

    def interleaved(weight):
        cut = weight.reshape(rows, shards, replicas, ff_rows)
        return lax.dynamic_index_in_dim(cut, r, 2, keepdims=False).reshape(rows, ff)

    gate_up_rows = jnp.concatenate([interleaved(gate_weight), interleaved(up_weight)], axis=1)
    down_rows = lax.dynamic_slice_in_dim(down_weight, r * ff_rows, ff_rows, 0)

    tokens = layer_in[0]
    all_tokens = spread_blocks(tokens)
    attn_all, attn_last = gather_rows(attn_rows)
    out_weight, _ = lax.optimization_barrier((out_weight, attn_last))
    out_matrix = gather_heads(out_weight)
    gate_up_rows, down_rows, _ = lax.optimization_barrier((gate_up_rows, down_rows, attn_last))
    gate_up_all, _ = gather_rows(gate_up_rows)
    down_all, _ = gather_rows(down_rows)
    cotangent_low, _ = lax.optimization_barrier((out_grad[0], all_tokens))
    all_cotangent = spread_blocks(cotangent_low).reshape(length, MODEL_WIDTH)

    attn_matrix = attn_all[:, :rows].reshape(MODEL_WIDTH, attn_width)
    gain_all = attn_all[:, rows].astype(F32)
    attn_gain = gain_all[:, :rows].reshape(MODEL_WIDTH)
    mlp_gain = gain_all[:, rows : 2 * rows].reshape(MODEL_WIDTH)
    query_gain = gain_all[:, 2 * rows : 2 * rows + head_rows].reshape(HEAD_SIZE)
    key_gain = gain_all[:, 2 * rows + head_rows : 2 * rows + 2 * head_rows].reshape(HEAD_SIZE)
    gate_up_matrix = gate_up_all.reshape(MODEL_WIDTH, 2 * ff)
    down_matrix = down_all.reshape(ff, MODEL_WIDTH)

    block_ids = r ^ jnp.arange(replicas, dtype=jnp.int32)
    positions = (block_ids[:, None] * size + jnp.arange(size, dtype=jnp.int32)[None, :]).reshape(-1)
    half = HEAD_SIZE // 2
    inv_freq = ROPE_BASE ** (-2.0 * jnp.arange(half, dtype=F32) / HEAD_SIZE)
    angles = positions.astype(F32)[:, None] * inv_freq[None, :]
    cosine, sine = jnp.cos(angles), jnp.sin(angles)
    cos_row = jnp.concatenate([cosine, cosine], axis=1)[:, None, :]
    sin_row = jnp.concatenate([-sine, sine], axis=1)[:, None, :]
    starts = picture_starts[0]
    held = (starts[None, :] == block_ids[:, None] * PIECE) & (
        jnp.arange(starts.shape[0], dtype=jnp.int32)[None, :] < picture_count[0]
    )
    info = jnp.concatenate([r[None].astype(jnp.int32), jnp.any(held, axis=1).astype(jnp.int32)])

    wide = all_tokens.reshape(length, MODEL_WIDTH).astype(F32)
    token_inverse = inverse_root(wide)
    normed = (wide * token_inverse * attn_gain).astype(BF)
    raw = mm(normed, attn_matrix)
    query_raw = raw[:, :q_width].reshape(length, -1, HEAD_SIZE)
    key_raw = raw[:, q_width : q_width + kv_width].reshape(length, -1, HEAD_SIZE)
    value = raw[:, q_width + kv_width :].astype(BF).reshape(replicas, size, kv_width)

    def rotated(values, gain):
        scaled = values * inverse_root(values) * gain
        return (scaled * cos_row + turn(scaled) * sin_row).astype(BF).reshape(replicas, size, -1)

    query, key = rotated(query_raw, query_gain), rotated(key_raw, key_gain)
    mixed, lse = attention_forward(info, query, key, value)
    mixed_rows = mixed.reshape(length, q_width)
    after_attn = tokens.astype(F32) + sum_blocks(
        mm(mixed_rows, out_matrix).reshape(replicas, size, MODEL_WIDTH)
    )
    after_inverse = inverse_root(after_attn)
    scaled_attn = after_attn * after_inverse
    mlp_in = spread_blocks((scaled_attn * mlp_gain).astype(BF)).reshape(length, MODEL_WIDTH)
    gate_up = mm(mlp_in, gate_up_matrix)
    gate_act, up_act = gate_up[:, :ff], gate_up[:, ff:]
    sigmoid = 1.0 / (1.0 + jnp.exp(-gate_act))
    silu = gate_act * sigmoid
    hidden = (silu * up_act).astype(BF)

    hidden_grad = mm(all_cotangent, down_matrix, ((1,), (1,)))
    gate_grad = (hidden_grad * up_act * sigmoid * (1.0 + gate_act * (1.0 - sigmoid))).astype(BF)
    up_grad = (hidden_grad * silu).astype(BF)
    gate_up_grad = jnp.concatenate([gate_grad, up_grad], axis=1)
    mlp_in_part = mm(gate_up_grad, gate_up_matrix, ((1,), (1,)))
    mlp_in_grad = sum_blocks(mlp_in_part.reshape(replicas, size, MODEL_WIDTH))
    residual_grad = out_grad[0].astype(F32) + norm_back(
        after_attn, after_inverse, mlp_gain, mlp_in_grad
    )
    mlp_gain_part = jnp.sum(mlp_in_grad * scaled_attn, axis=0)
    branch_grad = spread_blocks(residual_grad.astype(BF)).reshape(length, MODEL_WIDTH)

    layer_out = after_attn + sum_blocks(mm(hidden, down_matrix).reshape(replicas, size, MODEL_WIDTH))
    gate_up_w = scatter_rows(
        mm(mlp_in, gate_up_grad, ((0,), (0,))).reshape(shards, rows, 2 * ff)
    )
    down_w = scatter_rows(
        mm(hidden, all_cotangent, ((0,), (0,))).reshape(shards, ff_rows, MODEL_WIDTH)
    )

    out_w_grad = scatter_heads(mm(mixed_rows, branch_grad, ((0,), (0,))))
    mixed_grad = mm(branch_grad, out_matrix, ((1,), (1,))).astype(BF)
    dq, dk, dv = attention_backward(
        info, query, key, value, mixed, lse, mixed_grad.reshape(replicas, size, q_width)
    )

    def head_back(values, gain, dy):
        dy = dy.reshape(length, -1, HEAD_SIZE)
        dy = dy * cos_row - turn(dy) * sin_row
        inverse = inverse_root(values)
        gain_part = jnp.sum(dy * values * inverse, axis=(0, 1))
        return norm_back(values, inverse, gain, dy).astype(BF).reshape(length, -1), gain_part

    query_grad, query_gain_part = head_back(query_raw, query_gain, dq)
    key_grad, key_gain_part = head_back(key_raw, key_gain, dk)
    attn_grad = jnp.concatenate(
        [query_grad, key_grad, dv.reshape(length, kv_width).astype(BF)], axis=1
    )
    normed_part = mm(attn_grad, attn_matrix, ((1,), (1,)))
    normed_grad = sum_blocks(normed_part.reshape(replicas, size, MODEL_WIDTH))
    attn_gain_part = jnp.sum(normed_part * (wide * token_inverse), axis=0)
    own_tokens = tokens.astype(F32)
    in_grad = residual_grad + norm_back(own_tokens, inverse_root(own_tokens), attn_gain, normed_grad)

    gain_parts = jnp.concatenate(
        [
            attn_gain_part.reshape(shards, rows),
            mlp_gain_part.reshape(shards, rows),
            query_gain_part.reshape(shards, head_rows),
            key_gain_part.reshape(shards, head_rows),
        ],
        axis=1,
    )
    gain_block = jnp.zeros((shards, 16, attn_width), F32).at[:, 0, : gain_parts.shape[1]].set(gain_parts)
    attn_w_parts = mm(normed, attn_grad, ((0,), (0,))).reshape(shards, rows, attn_width)
    attn_w = scatter_rows(jnp.concatenate([attn_w_parts, gain_block], axis=1))

    def in_order(value):
        spread = spread_blocks(value.astype(BF))
        return jnp.stack(
            [lax.dynamic_index_in_dim(spread, r ^ a, 0, keepdims=False) for a in range(replicas)]
        ).astype(F32)

    attn_full = in_order(attn_w)
    gain_full = jnp.sum(attn_full[:, rows], axis=0)

    def beside(values):
        return jnp.concatenate([values[a] for a in range(replicas)], axis=1)

    query_w_grad = beside(attn_full[:, :rows, :q_width])
    key_w_grad = beside(attn_full[:, :rows, q_width : q_width + kv_width])
    value_w_grad = beside(attn_full[:, :rows, q_width + kv_width :])
    gate_up_full = in_order(gate_up_w)

    def woven(values):
        cut = values.reshape(replicas, rows, shards, ff_rows)
        return cut.transpose(1, 2, 0, 3).reshape(rows, shards * replicas * ff_rows)

    gate_w_grad = woven(gate_up_full[:, :, :ff])
    up_w_grad = woven(gate_up_full[:, :, ff:])
    down_w_grad = in_order(down_w).reshape(replicas * ff_rows, MODEL_WIDTH)

    return (
        layer_out.astype(BF)[None],
        in_grad.astype(BF)[None],
        gain_full[:rows],
        query_w_grad,
        key_w_grad,
        value_w_grad,
        gain_full[2 * rows : 2 * rows + head_rows],
        gain_full[2 * rows + head_rows : 2 * rows + 2 * head_rows],
        out_w_grad,
        gain_full[rows : 2 * rows],
        gate_w_grad,
        up_w_grad,
        down_w_grad,
    )


BLOCKS = 4
CHIPS = 4
ROWS = 128
SIZE = 256
HALF = SIZE // 2
Q_WIDTH = QUERY_HEADS // BLOCKS * HEAD_SIZE
KV_WIDTH = KEY_VALUE_HEADS // BLOCKS * HEAD_SIZE
ATTN_WIDTH = Q_WIDTH + 2 * KV_WIDTH
GROUPS = KV_WIDTH // HEAD_SIZE
GROUP_Q = GROUP * HEAD_SIZE
GROUP_WIDTH = GROUP_Q + 2 * HEAD_SIZE
FF_ROWS = 96
FF_PART = 768
OUT_ROWS = 64
PACKED = 3 * ROWS
TURN = HEAD_SIZE // 2
LENGTH = BLOCKS * SIZE
STORE_ROWS = 32768
RAW_WIDTH = GROUP_Q + HEAD_SIZE


def shape(dims, dtype):
    return jax.ShapeDtypeStruct(dims, dtype)


def on_core(body, name, outs, scalars, args, far=(), scratch=(), limit=16, far_outs=(), aliases=None):
    return pl.pallas_call(
        body,
        name=name,
        in_specs=[pl.BlockSpec(memory_space=pltpu.SMEM)] * len(scalars)
        + [pl.BlockSpec(memory_space=pltpu.VMEM)] * len(args)
        + [pl.BlockSpec(memory_space=pl.ANY)] * len(far),
        out_specs=[pl.BlockSpec(memory_space=pltpu.VMEM)] * len(outs)
        + [pl.BlockSpec(memory_space=pl.ANY)] * len(far_outs),
        out_shape=[*outs, *far_outs],
        scratch_shapes=list(scratch),
        input_output_aliases=aliases or {},
        compiler_params=pltpu.CompilerParams(vmem_limit_bytes=limit << 20),
    )(*scalars, *args, *far)


class Loads:
    def __init__(self, semaphores):
        self.semaphores, self.used = semaphores, 0

    def __call__(self, source, target):
        copy = pltpu.make_async_copy(source, target, self.semaphores.at[self.used])
        self.used += 1
        copy.start()
        return copy


def partial_shapes():
    return [
        shape((SIZE, MODEL_WIDTH), BF),
        shape((SIZE, MODEL_WIDTH), BF),
        shape((HALF, MODEL_WIDTH), F32),
        shape((HALF, MODEL_WIDTH), F32),
        shape((SIZE, MODEL_WIDTH), F32),
    ]


def put_partial(refs, j, part):
    by_one, by_two, keep_low, keep_high, keep = refs
    if j == 0:
        keep[...] = part
    if j == 1:
        by_one[:HALF] = part[:HALF].astype(BF)
        keep_high[...] = part[HALF:]
    if j == 2:
        by_two[:HALF] = part[HALF:].astype(BF)
        keep_low[...] = part[:HALF]
    if j == 3:
        by_one[HALF:] = part[:HALF].astype(BF)
        by_two[HALF:] = part[HALF:].astype(BF)


def move_partial(by_one, by_two, keep_low, keep_high, keep):
    one, two = flip(by_one, 1), flip(by_two, 2)
    low = flip((keep_low + one[HALF:].astype(F32)).astype(BF), 2)
    high = flip((keep_high + two[HALF:].astype(F32)).astype(BF), 1)
    return keep, one, two, low, high


def joined(keep, one, two, low, high):
    top = keep[:HALF] + one[:HALF].astype(F32) + low[...].astype(F32)
    bottom = keep[HALF:] + two[:HALF].astype(F32) + high[...].astype(F32)
    return jnp.concatenate([top, bottom], axis=0)


def spread(value):
    half = value.shape[0] // 2
    one, two = flip(value, 1), flip(value, 2)
    return value, one, two, flip(one[:half], 2), flip(two[half:], 1)


def spread_direct(value):
    return value, flip(value, 1), flip(value, 2), flip(value, 3)


def tie(values, *others):
    return lax.optimization_barrier((values, others))[0]


def block_of(refs, j):
    if j < 3 or len(refs) == 4:
        return refs[j][...]
    return jnp.concatenate([ref[...] for ref in refs[3:]], axis=0)


def head_places(store, near, g):
    places = []
    for n, (ref, rows) in enumerate(zip(near, (GROUP * SIZE, SIZE, SIZE))):
        columns = slice((n * GROUPS + g) * HEAD_SIZE, (n * GROUPS + g + 1) * HEAD_SIZE)
        for j in range(BLOCKS):
            at = 2 * LENGTH + j * rows
            places.append((store.at[at : at + rows, columns], ref.at[j]))
    return places


def load_paired(loads, refs, which, target):
    at = slice(which * HALF, (which + 1) * HALF)
    return [
        loads(refs[n].at[at, :], target.at[n * HALF : (n + 1) * HALF, :]) for n in range(2 * BLOCKS)
    ]


def part_shard(info, t):
    chip = lax.rem(info[1] + CHIPS - t % CHIPS, CHIPS)
    return 2 * chip + (info[2] if t < CHIPS else 1 - info[2])


def pack_kernel(info, wq, wk, wv, wo, *refs):
    gains, (out, *rows, semaphores) = refs[:4], refs[4:]
    loads = Loads(semaphores)
    gain_loads = [loads(gain, row) for gain, row in zip(gains, rows)]
    copies = []
    for g in range(GROUPS):
        at = g * GROUP_WIDTH
        head = info[0] * GROUPS + g
        columns = pl.ds(pl.multiple_of(head * GROUP_Q, GROUP_Q), GROUP_Q)
        copies.append(loads(wq.at[:, columns], out.at[:ROWS, at : at + GROUP_Q]))
        columns = pl.ds(pl.multiple_of(head * HEAD_SIZE, HEAD_SIZE), HEAD_SIZE)
        for weight, start in ((wk, at + GROUP_Q), (wv, at + GROUP_Q + HEAD_SIZE)):
            copies.append(loads(weight.at[:, columns], out.at[:ROWS, start : start + HEAD_SIZE]))
    own = pl.ds(pl.multiple_of(info[0] * OUT_ROWS, OUT_ROWS), OUT_ROWS)
    copies.append(loads(wo.at[own, :], out.at[ROWS + 16 :, :]))
    for copy in gain_loads:
        copy.wait()
    tile = slice(ROWS, ROWS + 16)
    out[tile, :] = jnp.zeros((16, ATTN_WIDTH), BF)
    for start, row in enumerate(rows):
        width = row.shape[1]
        out[tile, start * ROWS : start * ROWS + width] = jnp.broadcast_to(row[...], (16, width))
    for copy in copies:
        copy.wait()


def pack_feed_kernel(info, gate, up, down, out):
    for a in range(BLOCKS):

        @pl.when(info[0] == a)
        def _():
            for weight, first in ((gate, 0), (up, ROWS)):
                cut = []
                for s in range(2 * CHIPS):
                    start = (s * BLOCKS + a) * FF_ROWS
                    cut.append(weight[:, start : start + FF_ROWS])
                out[first : first + ROWS, :] = jnp.concatenate(cut, axis=1)
            rows = slice(a * FF_ROWS, (a + 1) * FF_ROWS)
            out[2 * ROWS : 2 * ROWS + FF_ROWS, :] = down[rows, :FF_PART]
            for i in range(3):
                rows = slice(a * FF_ROWS + i * 32, a * FF_ROWS + (i + 1) * 32)
                out[2 * ROWS + FF_ROWS :, i * 256 : (i + 1) * 256] = down[rows, FF_PART:]


def pick_kernel(info, *refs):
    parts, outs, semaphores = refs[:CHIPS], refs[CHIPS:-1], refs[-1]
    for j in range(BLOCKS):
        step = lax.rem(info[1] + CHIPS - (info[0] ^ j), CHIPS)
        for t in range(CHIPS):

            @pl.when(step == t)
            def _():
                pltpu.make_async_copy(
                    parts[t].at[ROWS + 16 :, :], outs[j], semaphores.at[j]
                ).start()

    for j in range(BLOCKS):
        pltpu.make_async_copy(parts[0].at[ROWS + 16 :, :], outs[j], semaphores.at[j]).wait()


def project_kernel(info, cos_ref, sin_ref, *refs):
    parts, tokens = refs[:8], refs[8:16]
    q_ref, k_ref, v_ref, gain_ref, low_store, wide_store = refs[16:22]
    normed_ref, raw_ref, w_ref, all_tokens, gain_rows, semaphores = refs[22:]
    loads = Loads(semaphores)
    gain_loads, part_loads = [], []
    shards = [part_shard(info, t) for t in range(2 * CHIPS)]
    for t in range(2 * CHIPS):
        gain_loads.append(loads(parts[t].at[ROWS : ROWS + 16, :], gain_rows.at[t]))
    token_loads = load_paired(loads, tokens, 0, all_tokens)
    for t in range(2 * CHIPS):
        at = pl.ds(pl.multiple_of(shards[t] * ROWS, ROWS), ROWS)
        part_loads.append(loads(parts[t].at[:ROWS, :], w_ref.at[at, :]))
    gain_ref[...] = jnp.zeros_like(gain_ref)
    low_lane = lax.broadcasted_iota(jnp.int32, (8, HEAD_SIZE), 1) < 16
    for t in range(2 * CHIPS):
        gain_loads[t].wait()
        columns = pl.ds(pl.multiple_of(shards[t] * ROWS, ROWS), ROWS)
        row = gain_rows[t, :, : 4 * ROWS].astype(F32)[:8]
        gain_ref[0:1, columns] = row[:1, :ROWS]
        gain_ref[1:2, columns] = row[:1, ROWS : 2 * ROWS]
        for start in (0, HEAD_SIZE):
            mine = jnp.where(low_lane, row[:, 2 * ROWS + start : 3 * ROWS + start], 0.0)
            gain_ref[2:3, start : start + HEAD_SIZE] += pltpu.roll(mine, shards[t] * 16, 1)[:1]
    for j in range(BLOCKS):
        here = slice(j * SIZE, (j + 1) * SIZE)
        for copy in token_loads[2 * j : 2 * j + 2]:
            copy.wait()
        wide = all_tokens[here, :].astype(F32)
        normed = (wide * inverse_root(wide) * gain_ref[0:1, :]).astype(BF)
        normed_ref[here, :] = normed
    stores = [loads(normed_ref, low_store.at[:LENGTH, :])]
    for n, table in enumerate((cos_ref, sin_ref)):
        at = GROUPS * RAW_WIDTH + n * HEAD_SIZE
        stores.append(loads(table, wide_store.at[:LENGTH, at : at + HEAD_SIZE]))
    for copy in part_loads:
        copy.wait()
    stores.append(loads(w_ref, low_store.at[LENGTH : 2 * LENGTH, :]))
    for j in range(BLOCKS):
        here = slice(j * SIZE, (j + 1) * SIZE)
        raw = mm(normed_ref[here, :], w_ref[...])
        cosine, sine = cos_ref[here, :], sin_ref[here, :]
        for g in range(GROUPS):
            for h in range(GROUP + 1):
                at = g * GROUP_WIDTH + h * HEAD_SIZE
                one = raw[:, at : at + HEAD_SIZE]
                raw_ref[g, here, h * HEAD_SIZE : (h + 1) * HEAD_SIZE] = one
                gain_at = HEAD_SIZE if h == GROUP else 0
                scaled = one * inverse_root(one) * gain_ref[2:3, gain_at : gain_at + HEAD_SIZE]
                rotated = (scaled * cosine + pltpu.roll(scaled, TURN, 1) * sine).astype(BF)
                if h == GROUP:
                    k_ref[g, j] = rotated
                else:
                    q_ref[g, j, h * SIZE : (h + 1) * SIZE, :] = rotated
            v_ref[g, j] = raw[:, (g + 1) * GROUP_WIDTH - HEAD_SIZE : (g + 1) * GROUP_WIDTH].astype(BF)
            at = slice(g * RAW_WIDTH, (g + 1) * RAW_WIDTH)
            stores.append(loads(raw_ref.at[g, here, :], wide_store.at[here, at]))
            places = head_places(low_store, (q_ref.at[g], k_ref.at[g], v_ref.at[g]), g)
            stores += [loads(near, far) for far, near in places[j::BLOCKS]]
    for copy in stores:
        copy.wait()


def attend_kernel(info, q_ref, k_ref, v_ref, store_in, mixed_ref, lse_ref, store, semaphores):
    own = info[0]
    loads = Loads(semaphores)
    stores = []
    for last in range(BLOCKS - 1, -1, -1):
        i = own ^ last
        for g in range(GROUPS):
            query = q_ref[g, i]
            total = jnp.zeros((1, GROUP * SIZE), F32)
            mixed = jnp.zeros((HEAD_SIZE, GROUP * SIZE), F32)
            for block in range(last + 1):
                j = own ^ block
                scores = mm(k_ref[g, j], query, ((1,), (1,)))
                weights = jnp.exp2(scores * (SCALE * LOG2E))
                if block == last:
                    weights = jnp.where(piece_mask(info[3 + i], SIZE, GROUP), weights, 0.0)
                total = total + jnp.sum(weights, axis=0, keepdims=True)
                mixed = mixed + mm(v_ref[g, j], weights.astype(BF), ((0,), (0,)))
            mixed = mixed * (1.0 / total)
            for h in range(GROUP):
                columns = slice(h * SIZE, (h + 1) * SIZE)
                at = (g * GROUP + h) * HEAD_SIZE
                mixed_ref[i, :, at : at + HEAD_SIZE] = mixed[:, columns].T.astype(BF)
            lse_ref[g, i] = jnp.log2(total)
        at = pl.ds(pl.multiple_of(4 * LENGTH + i * SIZE, SIZE), SIZE)
        stores.append(loads(mixed_ref.at[i], store.at[at, :Q_WIDTH]))
    for copy in stores:
        copy.wait()


def out_kernel(info, mixed_ref, *refs):
    own_pieces, other_pieces, out_ref, partial = refs[:4], refs[4:8], refs[8], refs[9:]
    own = info[0]
    for core, rows in ((info[2], own_pieces), (1 - info[2], other_pieces)):
        for q in range(BLOCKS):
            at = pl.multiple_of(core * SIZE + (own ^ q) * OUT_ROWS, OUT_ROWS)
            out_ref[pl.ds(at, OUT_ROWS), :] = rows[q][...]
    for j in (3, 1, 2, 0):
        put_partial(partial, j, mm(mixed_ref[j], out_ref[...]))


def after_kernel(tokens, gain_ref, *refs):
    after_ref, low_ref = refs[5:]
    after = tokens[...].astype(F32) + joined(*refs[:5])
    after_ref[...] = after
    low_ref[...] = (after * inverse_root(after) * gain_ref[1:2, :]).astype(BF)


def prepare_kernel(info, *refs):
    parts, pieces = refs[:8], refs[8:16]
    gate_up_ref, down_ref, cotangent = refs[16:19]
    grads, semaphores = refs[19:23], refs[23]
    loads = Loads(semaphores)
    down_loads, gate_loads = [], []
    cotangent_loads = load_paired(loads, pieces, 1, cotangent)
    for t in range(2 * CHIPS):
        s = part_shard(info, t)
        at = pl.ds(pl.multiple_of(s * FF_ROWS, 32), FF_ROWS)
        rows = slice(2 * ROWS, 2 * ROWS + FF_ROWS)
        down_loads.append(loads(parts[t].at[rows, :], down_ref.at[at, :FF_PART]))
        for i in range(3):
            at = pl.ds(pl.multiple_of(s * FF_ROWS + i * 32, 32), 32)
            rest = parts[t].at[2 * ROWS + FF_ROWS :, i * 256 : (i + 1) * 256]
            down_loads.append(loads(rest, down_ref.at[at, FF_PART:]))
    for t in range(2 * CHIPS):
        at = pl.ds(pl.multiple_of(part_shard(info, t) * ROWS, ROWS), ROWS)
        gate_loads.append(loads(parts[t].at[:ROWS, :], gate_up_ref.at[at, :FF_PART]))
        gate_loads.append(loads(parts[t].at[ROWS : 2 * ROWS, :], gate_up_ref.at[at, FF_PART:]))
    for copy in cotangent_loads + down_loads:
        copy.wait()
    for j in range(BLOCKS):
        here = slice(j * SIZE, (j + 1) * SIZE)
        grads[j][...] = mm(cotangent[here, :], down_ref[...], ((1,), (1,)))
    for copy in gate_loads:
        copy.wait()


def feed_kernel(blocks, *refs):
    count = len(blocks)
    last = blocks == (3,)
    extra = 2 if last else count
    inputs, hidden_grads = refs[:extra], refs[extra : extra + count]
    gate_up_ref = refs[extra + count]
    if last:
        first_a, second_b = refs[extra + count + 1 : extra + count + 3]
    outs = refs[extra + count + (3 if last else 1) :]
    for n, j in enumerate(blocks):
        tokens = jnp.concatenate([inputs[0][...], inputs[1][...]], axis=0) if last else inputs[n][...]
        hidden_ref, both_ref = outs[2 * n : 2 * n + 2]
        gate_up = mm(tokens, gate_up_ref[...])
        gate, up = gate_up[:, :FF_PART], gate_up[:, FF_PART:]
        sigmoid = 1.0 / (1.0 + jnp.exp(-gate))
        silu = gate * sigmoid
        hidden_ref[...] = (silu * up).astype(BF)
        grad = hidden_grads[n][...]
        both_ref[:, :FF_PART] = (grad * up * sigmoid * (1.0 + gate * (1.0 - sigmoid))).astype(BF)
        both_ref[:, FF_PART:] = (grad * silu).astype(BF)
        part = mm(both_ref[...], gate_up_ref[...], ((1,), (1,)))
        first, second = outs[2 * count + 2 * n : 2 * count + 2 * n + 2]
        if last:
            first[:HALF] = first_a[...]
            first[HALF:] = part[:HALF].astype(BF)
            second[:HALF] = second_b[...]
            second[HALF:] = part[HALF:].astype(BF)
        else:
            first[...] = part[:HALF].astype(first.dtype)
            second[...] = part[HALF:].astype(second.dtype)


FEED_TYPES = {0: (F32, F32), 1: (BF, F32), 2: (F32, BF), 3: (BF, BF)}


def feed(blocks, inputs, hidden_grads, gate_up, earlier=()):
    outs = []
    for _ in blocks:
        outs += [shape((SIZE, FF_PART), BF), shape((SIZE, 2 * FF_PART), BF)]
    for j in blocks:
        outs += [shape((SIZE if j == 3 else HALF, MODEL_WIDTH), dtype) for dtype in FEED_TYPES[j]]

    def body(*refs):
        feed_kernel(blocks, *refs)

    args = (*inputs, *hidden_grads, gate_up, *earlier)
    result = on_core(body, "feed", outs, (), args)
    count = len(blocks)
    hidden, both = result[0 : 2 * count : 2], result[1 : 2 * count : 2]
    return hidden, both, result[2 * count :]


def split_rows(info, kept, away, t, at, values):
    half = values.shape[0] // 2
    first, second = values[:half], values[half:]
    is_first = info[2] == 0
    kept[t, at : at + half, :] = jnp.where(is_first, first, second)
    away[t, at : at + half, :] = jnp.where(is_first, second, first).astype(BF)


def feed_weights_kernel(info, cotangent, *refs):
    hidden, both, mlp_in = refs[:4], refs[4:8], refs[8:13]
    kept, away, down_grad, stored, semaphores = refs[13:]
    loads = Loads(semaphores)
    copies = [loads(mlp_in[j], stored.at[j * SIZE : (j + 1) * SIZE, :]) for j in range(3)]
    copies += [
        loads(mlp_in[3 + n], stored.at[3 * SIZE + n * HALF : 3 * SIZE + (n + 1) * HALF, :])
        for n in range(2)
    ]
    both_all = jnp.concatenate([ref[...] for ref in both], axis=0)
    hidden_all = jnp.concatenate([ref[...] for ref in hidden], axis=0)
    down_grad[...] = mm(hidden_all, cotangent[...], ((0,), (0,)))
    for copy in copies:
        copy.wait()
    for t in range(CHIPS):
        chip = lax.rem(info[1] + 2 * CHIPS - (t + 1), CHIPS)
        columns = stored[:, pl.ds(pl.multiple_of(chip * 2 * ROWS, 2 * ROWS), 2 * ROWS)]
        product = mm(columns, both_all, ((0,), (0,)))
        split_rows(info, kept, away, t, 0, product[:, :FF_PART])
        split_rows(info, kept, away, t, ROWS, product[:, FF_PART:])
        for core, target in ((info[2], kept), (1 - info[2], away)):
            at = pl.multiple_of((2 * chip + core) * FF_ROWS, 32)
            rows = down_grad[pl.ds(at, FF_ROWS), :].astype(target.dtype)
            target[t, 2 * ROWS : 2 * ROWS + FF_ROWS, :] = rows[:, :FF_PART]
            for i in range(3):
                target[t, 2 * ROWS + FF_ROWS :, i * 256 : (i + 1) * 256] = rows[
                    i * 32 : (i + 1) * 32, FF_PART:
                ]


def down_kernel(down_ref, *refs):
    hidden, partial = refs[:4], refs[4:]
    for j in (3, 1, 2, 0):
        put_partial(partial, j, mm(hidden[j][...], down_ref[...]))


def residual_kernel(cotangent, after_ref, gain_ref, *refs):
    low_ref, gain_part = refs[-2:]
    keep_a, keep_b, one, two, low, high = refs[:6]
    top = keep_a[...] + one[:HALF].astype(F32) + low[...].astype(F32)
    bottom = keep_b[...] + two[:HALF].astype(F32) + high[...].astype(F32)
    mlp_in_grad = jnp.concatenate([top, bottom], axis=0)
    after = after_ref[...]
    inverse = inverse_root(after)
    gain_part[...] = jnp.sum(mlp_in_grad * (after * inverse), axis=0, keepdims=True)
    grad = cotangent[...].astype(F32) + norm_back(after, inverse, gain_ref[1:2, :], mlp_in_grad)
    low_ref[...] = grad.astype(BF)


def mixed_grad_kernel(info, out_ref, *refs):
    branch, store, (grad_ref, kept, away, scratch, mixed_ref, semaphores) = refs[:5], refs[5], refs[6:]
    mixed_load = Loads(semaphores)(store.at[4 * LENGTH : 5 * LENGTH, :Q_WIDTH], mixed_ref)
    own = info[0]
    for j in range(BLOCKS):
        grad_ref[j] = mm(block_of(branch, j), out_ref[...], ((1,), (1,))).astype(BF)
    branch_all = jnp.concatenate([block_of(branch, j) for j in range(BLOCKS)], axis=0)
    mixed_load.wait()
    scratch[...] = mm(mixed_ref[...], branch_all, ((0,), (0,)))
    for core, target in ((info[2], kept), (1 - info[2], away)):
        for q in range(BLOCKS):
            at = pl.multiple_of(core * SIZE + (own ^ q) * OUT_ROWS, OUT_ROWS)
            target[q] = scratch[pl.ds(at, OUT_ROWS), :].astype(target.dtype)


def pair_kernel(kept, crossed, *outs):
    for j, out in enumerate(outs):
        out[...] = (kept[j] + crossed[j].astype(F32)).astype(BF)


def head_back(grad, cosine, sine, raw, gain):
    dy = grad * cosine - pltpu.roll(grad, TURN, 1) * sine
    inverse = inverse_root(raw)
    gain_part = jnp.sum(dy * (raw * inverse), axis=0, keepdims=True)
    return norm_back(raw, inverse, gain, dy).astype(BF), gain_part


def attend_back_kernel(g, info, lse_ref, grad_ref, mlp_part, gain_ref, *refs):
    (store, wide_store), (out_ref, kept, away, dk_ref, dv_ref) = refs[:2], refs[2:7]
    q_ref, k_ref, v_ref, mixed_ref, raw_ref, cos_ref, sin_ref, normed_ref, w_ref, semaphores = refs[7:]
    loads = Loads(semaphores)
    first = [loads(far, near) for far, near in head_places(store, (q_ref, k_ref, v_ref), g)]
    at = slice(g * GROUP_Q, (g + 1) * GROUP_Q)
    first += [
        loads(store.at[4 * LENGTH + j * SIZE : 4 * LENGTH + (j + 1) * SIZE, at], mixed_ref.at[j])
        for j in range(BLOCKS)
    ]
    second = [loads(wide_store.at[:LENGTH, g * RAW_WIDTH : (g + 1) * RAW_WIDTH], raw_ref)]
    for n, table in enumerate((cos_ref, sin_ref)):
        at = GROUPS * RAW_WIDTH + n * HEAD_SIZE
        second.append(loads(wide_store.at[:LENGTH, at : at + HEAD_SIZE], table))
    at = slice(g * GROUP_WIDTH, (g + 1) * GROUP_WIDTH)
    third = [
        loads(store.at[:LENGTH, :], normed_ref),
        loads(store.at[LENGTH : 2 * LENGTH, at], w_ref),
    ]
    own = info[0]
    query_part = jnp.zeros((1, HEAD_SIZE), F32)
    key_part = jnp.zeros((1, HEAD_SIZE), F32)
    dk_ref[...] = jnp.zeros_like(dk_ref)
    dv_ref[...] = jnp.zeros_like(dv_ref)
    for copy in first:
        copy.wait()
    for last in range(BLOCKS):
        i = own ^ last
        rows = pl.ds(pl.multiple_of(i * SIZE, SIZE), SIZE)
        heads = [slice((g * GROUP + h) * HEAD_SIZE, (g * GROUP + h + 1) * HEAD_SIZE) for h in range(GROUP)]
        query = q_ref[i]
        grad = jnp.concatenate([grad_ref[i, :, h] for h in heads], axis=0)
        mixed = jnp.concatenate(
            [mixed_ref[i, :, h * HEAD_SIZE : (h + 1) * HEAD_SIZE] for h in range(GROUP)], axis=0
        )
        delta = jnp.sum((grad.astype(F32) * mixed.astype(F32)).T, axis=0, keepdims=True)
        log_sum = lse_ref[g, i]
        dquery = jnp.zeros((HEAD_SIZE, GROUP * SIZE), F32)
        for block in range(last + 1):
            j = own ^ block
            scores = mm(k_ref[j], query, ((1,), (1,)))
            dprobs = mm(v_ref[j], grad, ((1,), (1,)))
            probs = jnp.exp2(scores * (SCALE * LOG2E) - log_sum)
            if block == last:
                probs = jnp.where(piece_mask(info[3 + i], SIZE, GROUP), probs, 0.0)
            dscores = (probs * (dprobs - delta)).astype(BF)
            dv_ref[j] += mm(probs.astype(BF), grad)
            dk_ref[j] += mm(dscores, query)
            dquery = dquery + mm(k_ref[j], dscores, ((0,), (0,)))
        if last == 0:
            for copy in second:
                copy.wait()
        for h in range(GROUP):
            at = slice(h * HEAD_SIZE, (h + 1) * HEAD_SIZE)
            back, part = head_back(
                dquery[:, h * SIZE : (h + 1) * SIZE].T * SCALE,
                cos_ref[rows, :],
                sin_ref[rows, :],
                raw_ref[rows, at],
                gain_ref[2:3, :HEAD_SIZE],
            )
            out_ref[rows, at] = back
            query_part = query_part + part
    for j in range(BLOCKS):
        rows = slice(j * SIZE, (j + 1) * SIZE)
        at = slice(GROUP_Q, GROUP_Q + HEAD_SIZE)
        back, part = head_back(
            dk_ref[j] * SCALE,
            cos_ref[rows, :],
            sin_ref[rows, :],
            raw_ref[rows, at],
            gain_ref[2:3, HEAD_SIZE : 2 * HEAD_SIZE],
        )
        out_ref[rows, at] = back
        key_part = key_part + part
        out_ref[rows, GROUP_Q + HEAD_SIZE :] = dv_ref[j].astype(BF)
    for copy in third:
        copy.wait()
    row = lax.broadcasted_iota(jnp.int32, (16, GROUP_WIDTH), 0)
    for t in range(CHIPS):
        chip = lax.rem(info[1] + 2 * CHIPS - (t + 1), CHIPS)
        at = pl.ds(pl.multiple_of(chip * 2 * ROWS, 2 * ROWS), 2 * ROWS)
        product = mm(normed_ref[:, at], out_ref[...], ((0,), (0,)))
        split_rows(info, kept, away, t, 0, product)
        inner = jnp.sum(product * w_ref[at, :].astype(F32), axis=1, keepdims=True)
        inner = jnp.broadcast_to(inner, (2 * ROWS, ROWS)).T[0:1] / gain_ref[0:1, at]
        mlp = mlp_part[0:1, at] if g == 0 else jnp.zeros_like(inner)
        for is_first, half in ((True, slice(0, ROWS)), (False, slice(ROWS, 2 * ROWS))):
            values = jnp.concatenate([inner[:, half], mlp[:, half], query_part, key_part], axis=1)
            values = jnp.where(row == 0, values, 0.0)

            @pl.when((info[2] == 0) == is_first)
            def _():
                kept[t, ROWS:, :] = values

            @pl.when((info[2] == 0) != is_first)
            def _():
                away[t, ROWS:, :] = values.astype(BF)


def normed_grad_kernel(*refs):
    grads, store, partial, (w_ref, semaphores) = refs[:GROUPS], refs[GROUPS], refs[GROUPS + 1 : -2], refs[-2:]
    Loads(semaphores)(store.at[LENGTH : 2 * LENGTH, :], w_ref).wait()
    for j in (3, 1, 2, 0):
        here = slice(j * SIZE, (j + 1) * SIZE)
        grad = jnp.concatenate([ref[here, :] for ref in grads], axis=1)
        put_partial(partial, j, mm(grad, w_ref[...], ((1,), (1,))))


def final_kernel(tokens, gain_ref, residual, *refs):
    grad_ref = refs[5]
    wide = tokens[...].astype(F32)
    dy = joined(*refs[:5])
    back = norm_back(wide, inverse_root(wide), gain_ref[0:1, :], dy)
    grad_ref[...] = (residual[...].astype(F32) + back).astype(BF)


def output_kernel(after_ref, *refs):
    refs[5][...] = (after_ref[...] + joined(*refs[:5])).astype(BF)


def unpack_feed_kernel(info, *refs):
    pieces, (gate_ref, up_ref, down_ref, scratch) = refs[:5], refs[5:]
    for j in range(BLOCKS):
        scratch[info[0] ^ j] = block_of(pieces, j).astype(F32)
    for first, target in ((0, gate_ref), (ROWS, up_ref)):
        for s in range(0, 2 * CHIPS):
            columns = slice(s * FF_ROWS, (s + 1) * FF_ROWS)
            cut = [scratch[a, first : first + ROWS, columns] for a in range(BLOCKS)]
            target[:, s * BLOCKS * FF_ROWS : (s + 1) * BLOCKS * FF_ROWS] = jnp.concatenate(cut, axis=1)
    for a in range(BLOCKS):
        at = slice(a * FF_ROWS, (a + 1) * FF_ROWS)
        down_ref[at, :FF_PART] = scratch[a, 2 * ROWS : 2 * ROWS + FF_ROWS, :]
        for i in range(3):
            at = slice(a * FF_ROWS + i * 32, a * FF_ROWS + (i + 1) * 32)
            down_ref[at, FF_PART:] = scratch[a, 2 * ROWS + FF_ROWS :, i * 256 : (i + 1) * 256]


def unpack_attend_kernel(info, *refs):
    pieces, (query_ref, key_ref, value_ref, out_ref, gain_ref) = (refs[:4], refs[4:8]), refs[8:]
    gains = jnp.zeros((8, GROUP_WIDTH), F32)
    for g in range(GROUPS):
        for j in range(BLOCKS):
            piece = pieces[g][j]
            head = (info[0] ^ j) * GROUPS + g
            values = piece[:ROWS, :].astype(F32)
            wide = pl.ds(pl.multiple_of(head * GROUP_Q, GROUP_Q), GROUP_Q)
            thin = pl.ds(pl.multiple_of(head * HEAD_SIZE, HEAD_SIZE), HEAD_SIZE)
            query_ref[:, wide] = values[:, :GROUP_Q]
            key_ref[:, thin] = values[:, GROUP_Q : GROUP_Q + HEAD_SIZE]
            value_ref[:, thin] = values[:, GROUP_Q + HEAD_SIZE :]
            gains = gains + piece[ROWS : ROWS + 16, :].astype(F32)[:8]
            if g == 0:
                rows = pl.ds(pl.multiple_of((info[0] ^ j) * OUT_ROWS, OUT_ROWS), OUT_ROWS)
                top = piece[ROWS + 16 : ROWS + 16 + OUT_ROWS, :].astype(F32)
                out_ref[rows, :GROUP_WIDTH] = top
                out_ref[rows, GROUP_WIDTH:] = piece[ROWS + 16 + OUT_ROWS :, :].astype(F32)
    gain_ref[...] = gains


def ring_parts(value, swapped, then):
    own, other = [value], [swapped]
    for t in range(1, CHIPS):
        ready = then.get(t, ())
        if t > 1:
            ready = (ready, other[t - 2])
        own.append(ring_up(tie(own[-1], ready)))
        other.append(other_core(own[-1]))
    return own, other


def ring_term(kept, crossed, t, previous=None, beside=None, after=()):
    value = kept[t] + crossed[t].astype(F32)
    count = value.shape[0]
    if t:
        moved = tie(ring_up(previous), after)
        value = value + moved[:count].astype(F32)
    value = value.astype(BF)
    if beside is not None:
        extra = beside(t + 1)
        if t:
            extra = (moved[count:].astype(F32) + extra.astype(F32)).astype(BF)
        value = jnp.concatenate([value, extra], axis=0)
    return value


def ring_sum(kept, crossed, beside=None):
    running = [ring_term(kept, crossed, 0, None, beside)]
    for t in range(1, CHIPS):
        running.append(ring_term(kept, crossed, t, running[-1], beside))
    return running


def per_device(
    layer_in,
    out_grad,
    attn_norm,
    query_weight,
    key_projection,
    value_projection,
    query_norm,
    key_norm,
    out_weight,
    mlp_norm,
    gate_weight,
    up_weight,
    down_weight,
    picture_starts,
    picture_count,
):
    r, index = lax.axis_index("rep"), lax.axis_index("shard")
    chip, core = index // 2, index % 2
    length = BLOCKS * SIZE
    tokens, cotangent_own = layer_in[0], out_grad[0]

    block_ids = r ^ jnp.arange(BLOCKS, dtype=jnp.int32)
    starts = picture_starts[0]
    held = (starts[None, :] == block_ids[:, None] * PIECE) & (
        jnp.arange(starts.shape[0], dtype=jnp.int32)[None, :] < picture_count[0]
    )
    place = jnp.stack([r, chip, core]).astype(jnp.int32)
    info = jnp.concatenate([place, jnp.any(held, axis=1).astype(jnp.int32)])

    gains = tuple(gain.reshape(1, -1) for gain in (attn_norm, mlp_norm, query_norm, key_norm))
    (attn_rows,) = on_core(
        pack_kernel,
        "pack",
        [shape((ROWS + 16 + OUT_ROWS, ATTN_WIDTH), BF)],
        (place,),
        (),
        (query_weight, key_projection, value_projection, out_weight, *gains),
        [pltpu.VMEM(gain.shape, BF) for gain in gains] + [pltpu.SemaphoreType.DMA((11,))],
        62,
    )
    attn_swap = other_core(attn_rows)
    low_half, high_half = tie(
        tuple(jnp.concatenate([tokens[at], cotangent_own[at]]) for at in (slice(0, HALF), slice(HALF, SIZE))),
        attn_rows,
    )
    one = flip(low_half, 1), flip(high_half, 1)
    two = flip(low_half, 2), flip(high_half, 2)
    pieces = (low_half, high_half, *one, *two, flip(one[0], 2), flip(two[1], 1))
    (feed_rows,) = on_core(
        pack_feed_kernel,
        "pack_feed",
        [shape((PACKED, FF_PART), BF)],
        (place,),
        tie((gate_weight, up_weight, down_weight), attn_rows),
    )

    positions = (block_ids[:, None] * SIZE + jnp.arange(SIZE, dtype=jnp.int32)[None, :]).reshape(-1)
    inv_freq = ROPE_BASE ** (-2.0 * jnp.arange(TURN, dtype=F32) / HEAD_SIZE)
    angles = positions.astype(F32)[:, None] * inv_freq[None, :]
    cosine, sine = jnp.cos(angles), jnp.sin(angles)
    cos_rows = jnp.concatenate([cosine, cosine], axis=1)
    sin_rows = jnp.concatenate([-sine, sine], axis=1)

    attn_own, attn_other = ring_parts(
        attn_rows, attn_swap, {2: (feed_rows, info), 3: (one, two, cos_rows, sin_rows)}
    )

    picked = on_core(
        pick_kernel,
        "pick",
        [shape((OUT_ROWS, MODEL_WIDTH), BF)] * BLOCKS,
        (place,),
        (),
        attn_own,
        [pltpu.SemaphoreType.DMA((BLOCKS,))],
    )
    out_own = [picked[0]] + [flip(picked[j], j) for j in (1, 2, 3)]

    heads = [
        shape((GROUPS, BLOCKS, GROUP * SIZE, HEAD_SIZE), BF),
        shape((GROUPS, BLOCKS, SIZE, HEAD_SIZE), BF),
        shape((GROUPS, BLOCKS, SIZE, HEAD_SIZE), BF),
    ]
    store_shape = shape((STORE_ROWS, MODEL_WIDTH), BF)
    query, key, value, gain_rows, store, wide_store = on_core(
        project_kernel,
        "project",
        heads + [shape((8, MODEL_WIDTH), F32)],
        (info,),
        (cos_rows, sin_rows),
        (*attn_own, *attn_other, *pieces),
        [
            pltpu.VMEM((length, MODEL_WIDTH), BF),
            pltpu.VMEM((GROUPS, length, RAW_WIDTH), F32),
            pltpu.VMEM((MODEL_WIDTH, ATTN_WIDTH), BF),
            pltpu.VMEM((length, MODEL_WIDTH), BF),
            pltpu.VMEM((2 * CHIPS, 16, ATTN_WIDTH), BF),
            pltpu.SemaphoreType.DMA((14 * CHIPS + 4,)),
        ],
        24,
        [store_shape, shape((STORE_ROWS // 2, MODEL_WIDTH), F32)],
    )
    mixed, lse, store = on_core(
        attend_kernel,
        "attend",
        [
            shape((BLOCKS, SIZE, Q_WIDTH), BF),
            shape((GROUPS, BLOCKS, 1, GROUP * SIZE), F32),
        ],
        (info,),
        (query, key, value),
        (store,),
        [pltpu.SemaphoreType.DMA((BLOCKS,))],
        16,
        [store_shape],
        {4: 2},
    )
    out_own = tie(out_own, query)
    out_other = other_core(jnp.concatenate(out_own, axis=0))
    out_other = [out_other[j * OUT_ROWS : (j + 1) * OUT_ROWS] for j in range(BLOCKS)]
    out_matrix, *partial = on_core(
        out_kernel,
        "out",
        [shape((Q_WIDTH, MODEL_WIDTH), BF)] + partial_shapes(),
        (info,),
        (mixed, *out_own, *out_other),
    )
    feed_start = tie(feed_rows, attn_own[-1])
    feed_own, feed_other = ring_parts(feed_start, other_core(feed_start), {2: mixed, 3: partial[0]})
    partial = move_partial(*partial)
    after_attn, mlp_own = on_core(
        after_kernel,
        "after",
        [shape((SIZE, MODEL_WIDTH), F32), shape((SIZE, MODEL_WIDTH), BF)],
        (),
        (tokens, gain_rows, *partial),
    )
    mlp_in = spread(mlp_own)
    gate_up, down, cotangent, *hidden_grads = on_core(
        prepare_kernel,
        "prepare",
        [
            shape((MODEL_WIDTH, 2 * FF_PART), BF),
            shape((FF_PART, MODEL_WIDTH), BF),
            shape((length, MODEL_WIDTH), BF),
        ]
        + [shape((SIZE, FF_PART), F32)] * BLOCKS,
        (info,),
        (),
        (*tie((*feed_own, *feed_other), mlp_own), *pieces),
        [pltpu.SemaphoreType.DMA((14 * CHIPS,))],
    )
    hidden_0, both_0, keep = feed((0,), mlp_in[:1], hidden_grads[:1], gate_up)
    hidden_12, both_12, (one_a, keep_high, keep_low, two_a) = feed(
        (1, 2), tie(mlp_in[1:3], both_0), hidden_grads[1:3], gate_up
    )
    hidden_3, both_3, (one, two) = feed(
        (3,), tie(mlp_in[3:], both_12), hidden_grads[3:], gate_up, (one_a, two_a)
    )
    hidden = [*hidden_0, *hidden_12, *hidden_3]
    both = [*both_0, *both_12, *both_3]

    feed_kept, feed_away = on_core(
        feed_weights_kernel,
        "feed_weights",
        [
            shape((CHIPS, PACKED, FF_PART), F32),
            shape((CHIPS, PACKED, FF_PART), BF),
        ],
        (info,),
        (cotangent, *hidden, *both),
        mlp_in,
        [
            pltpu.VMEM((FF_PART, MODEL_WIDTH), F32),
            pltpu.VMEM((length, MODEL_WIDTH), BF),
            pltpu.SemaphoreType.DMA((5,)),
        ],
        24,
    )
    one, two = tie((flip(one, 1), flip(two, 2)), feed_kept)
    low = (keep_low + one[HALF:].astype(F32)).astype(BF)
    high = (keep_high + two[HALF:].astype(F32)).astype(BF)
    crossed = other_core(tie(feed_away, low, high))
    low, high = flip(low, 2), flip(high, 1)
    branch_own, mlp_gain_part = on_core(
        residual_kernel,
        "residual",
        [
            shape((SIZE, MODEL_WIDTH), BF),
            shape((1, MODEL_WIDTH), F32),
        ],
        (),
        (cotangent_own, after_attn, gain_rows, *tie((*keep, one, two, low, high), crossed)),
    )
    branch = spread(branch_own)
    feed_ring = [ring_term(feed_kept, crossed, 0)]
    feed_ring.append(ring_term(feed_kept, crossed, 1, feed_ring[0]))
    layer_partial = on_core(
        down_kernel, "down", partial_shapes(), (), tie((down, *hidden), branch_own, feed_ring[0])
    )

    mixed_grad, out_kept, out_away = on_core(
        mixed_grad_kernel,
        "mixed_grad",
        [
            shape((BLOCKS, SIZE, Q_WIDTH), BF),
            shape((BLOCKS, OUT_ROWS, MODEL_WIDTH), F32),
            shape((BLOCKS, OUT_ROWS, MODEL_WIDTH), BF),
        ],
        (info,),
        (out_matrix, *tie(branch, layer_partial, feed_ring[1])),
        (store,),
        [
            pltpu.VMEM((Q_WIDTH, MODEL_WIDTH), F32),
            pltpu.VMEM((length, Q_WIDTH), BF),
            pltpu.SemaphoreType.DMA((1,)),
        ],
    )
    out_pair = on_core(
        pair_kernel,
        "pair",
        [shape((OUT_ROWS, MODEL_WIDTH), BF)] * BLOCKS,
        (),
        (out_kept, other_core(out_away)),
    )
    out_moved = [out_pair[0]] + [flip(out_pair[j], j) for j in (1, 2, 3)]

    def back(g, grad):
        def body(*refs):
            attend_back_kernel(g, *refs)

        return on_core(
            body,
            "attend_back",
            [
                shape((length, GROUP_WIDTH), BF),
                shape((CHIPS, ROWS + 16, GROUP_WIDTH), F32),
                shape((CHIPS, ROWS + 16, GROUP_WIDTH), BF),
            ],
            (info,),
            (lse, grad, mlp_gain_part, gain_rows),
            (store, wide_store),
            [
                pltpu.VMEM((BLOCKS, SIZE, HEAD_SIZE), F32),
                pltpu.VMEM((BLOCKS, SIZE, HEAD_SIZE), F32),
                pltpu.VMEM((BLOCKS, GROUP * SIZE, HEAD_SIZE), BF),
                pltpu.VMEM((BLOCKS, SIZE, HEAD_SIZE), BF),
                pltpu.VMEM((BLOCKS, SIZE, HEAD_SIZE), BF),
                pltpu.VMEM((BLOCKS, SIZE, GROUP_Q), BF),
                pltpu.VMEM((length, RAW_WIDTH), F32),
                pltpu.VMEM((length, HEAD_SIZE), F32),
                pltpu.VMEM((length, HEAD_SIZE), F32),
                pltpu.VMEM((length, MODEL_WIDTH), BF),
                pltpu.VMEM((MODEL_WIDTH, GROUP_WIDTH), BF),
                pltpu.SemaphoreType.DMA((4 * BLOCKS + 5,)),
            ],
        )

    grad_0, kept_0, away_0 = back(0, tie(mixed_grad, out_pair))
    out_blocks = jnp.stack(tie(out_moved, grad_0))

    def out_step(t):
        block = lax.dynamic_index_in_dim(
            out_blocks, r ^ ((chip + 2 * CHIPS - t) % CHIPS), 0, keepdims=False
        )
        return jnp.concatenate([block[:, :GROUP_WIDTH], block[:, GROUP_WIDTH:]], axis=0)

    kept = (kept_0, other_core(away_0))
    attn_first = [ring_term(*kept, 0, None, out_step)]
    feed_ring.append(ring_term(feed_kept, crossed, 2, feed_ring[1], None, grad_0))
    layer_one, layer_two, layer_low, layer_high, layer_keep = tie(layer_partial, grad_0)
    layer_one, layer_two = flip(layer_one, 1), flip(layer_two, 2)
    grad_1, kept_1, away_1 = back(1, tie(mixed_grad, attn_first[0], feed_ring[2]))
    layer_one, layer_two = tie((layer_one, layer_two), grad_1)
    layer_low = flip((layer_low + layer_one[HALF:].astype(F32)).astype(BF), 2)
    layer_high = flip((layer_high + layer_two[HALF:].astype(F32)).astype(BF), 1)
    for t in range(1, CHIPS):
        attn_first.append(ring_term(*kept, t, attn_first[-1], out_step, grad_1))
    feed_ring.append(ring_term(feed_kept, crossed, 3, feed_ring[2], None, grad_1))
    attn_second = ring_sum(kept_1, other_core(away_1))
    partial = on_core(
        normed_grad_kernel,
        "normed_grad",
        partial_shapes(),
        (),
        tie((grad_0, grad_1), out_blocks, attn_second[0]),
        (store,),
        [pltpu.VMEM((MODEL_WIDTH, ATTN_WIDTH), BF), pltpu.SemaphoreType.DMA((1,))],
    )
    (layer_out,) = on_core(
        output_kernel,
        "output",
        [shape((SIZE, MODEL_WIDTH), BF)],
        (),
        (after_attn, layer_keep, layer_one, layer_two, layer_low, layer_high),
    )
    (in_grad,) = on_core(
        final_kernel,
        "final",
        [shape((SIZE, MODEL_WIDTH), BF)],
        (),
        (tokens, gain_rows, branch_own, *move_partial(*partial)),
    )

    gate_w_grad, up_w_grad, down_w_grad = on_core(
        unpack_feed_kernel,
        "unpack_feed",
        [
            shape((ROWS, 2 * CHIPS * BLOCKS * FF_ROWS), F32),
            shape((ROWS, 2 * CHIPS * BLOCKS * FF_ROWS), F32),
            shape((BLOCKS * FF_ROWS, MODEL_WIDTH), F32),
        ],
        (place,),
        spread(feed_ring[-1]),
        (),
        [pltpu.VMEM((BLOCKS, PACKED, FF_PART), F32)],
    )
    query_w_grad, key_w_grad, value_w_grad, out_w_grad, gain_full = on_core(
        unpack_attend_kernel,
        "unpack_attend",
        [
            shape((ROWS, QUERY_HEADS * HEAD_SIZE), F32),
            shape((ROWS, KEY_VALUE_HEADS * HEAD_SIZE), F32),
            shape((ROWS, KEY_VALUE_HEADS * HEAD_SIZE), F32),
            shape((SIZE, MODEL_WIDTH), F32),
            shape((8, GROUP_WIDTH), F32),
        ],
        (place,),
        (*spread_direct(attn_first[-1]), *spread_direct(attn_second[-1])),
    )
    gains = gain_full[0]
    head_rows = query_norm.shape[0]

    def slice_of(start, width):
        return lax.dynamic_slice_in_dim(gains, start + index * width, width, 0)

    return (
        layer_out[None],
        in_grad[None],
        gains[:ROWS],
        query_w_grad,
        key_w_grad,
        value_w_grad,
        slice_of(2 * ROWS, head_rows),
        slice_of(2 * ROWS + HEAD_SIZE, head_rows),
        out_w_grad,
        gains[ROWS : 2 * ROWS],
        gate_w_grad,
        up_w_grad,
        down_w_grad,
    )


def solution(mesh):
    tokens, matrix, vector = P("shard", "rep", None), P("shard", None), P("shard")
    return jax.shard_map(
        per_device if dict(mesh.shape) == {"rep": 4, "shard": 8} else per_device_any,
        mesh=mesh,
        in_specs=(tokens, tokens, vector, matrix, matrix, matrix, vector, vector, matrix, vector)
        + (matrix, matrix, matrix, matrix, vector),
        out_specs=(tokens, tokens, vector, matrix, matrix, matrix, vector, vector, matrix, vector)
        + (matrix, matrix, matrix),
        check_vma=False,
    )
```

```python
import jax
import jax.numpy as jnp
from jax import lax
from jax.experimental import pallas as pl
from jax.experimental.pallas import tpu as pltpu
from jax.sharding import PartitionSpec as P

MODEL_WIDTH = 1024
QUERY_HEADS = 16
KEY_VALUE_HEADS = 8
HEAD_SIZE = 128
GROUP = QUERY_HEADS // KEY_VALUE_HEADS
PIECE = 256

EPSILON = 1e-06
ROPE_BASE = 1000000.0
SCALE = HEAD_SIZE ** (-0.5)
LOG2E = 1.4426950408889634
BF = jnp.bfloat16
F32 = jnp.float32


def mm(a, b, dims=((1,), (0,))):
    return lax.dot_general(a, b, (dims, ((), ())), preferred_element_type=F32)


def flip(value, bit):
    count = lax.axis_size("rep")
    return lax.ppermute(value, "rep", [(i, i ^ bit) for i in range(count)])


def spread_blocks(value):
    count = lax.axis_size("rep")
    if count == 4:
        half = value.shape[0] // 2
        by_one, by_two = flip(value, 1), flip(value, 2)
        low, high = flip(by_one[:half], 2), flip(by_two[half:], 1)
        return jnp.stack([value, by_one, by_two, jnp.concatenate([low, high], axis=0)])
    blocks = value[None]
    bit = 1
    while bit < count:
        blocks = jnp.concatenate([blocks, flip(blocks, bit)], axis=0)
        bit *= 2
    return blocks


def sum_blocks(parts):
    count = lax.axis_size("rep")
    if count == 4:
        half = parts.shape[1] // 2
        a, b = parts[:, :half], parts[:, half:]
        a_in = flip(jnp.stack([a[1], a[3]]).astype(BF), 1).astype(F32)
        b_in = flip(jnp.stack([b[2], b[3]]).astype(BF), 2).astype(F32)
        a_last = flip((a[2] + a_in[1]).astype(BF), 2).astype(F32)
        b_last = flip((b[1] + b_in[1]).astype(BF), 1).astype(F32)
        return jnp.concatenate([a[0] + a_in[0] + a_last, b[0] + b_in[0] + b_last], axis=0)
    bit = count // 2
    while bit:
        parts = parts[:bit] + flip(parts[bit:].astype(BF), bit).astype(F32)
        bit //= 2
    return parts[0]


def ring_up(value):
    count = lax.axis_size("shard")
    return lax.ppermute(value, "shard", [(i, (i + 2) % count) for i in range(count)])


def other_core(value):
    count = lax.axis_size("shard")
    return lax.ppermute(value, "shard", [(i, i ^ 1) for i in range(count)])


def gather_rows(value):
    count = lax.axis_size("shard")
    chips = count // 2
    index = lax.axis_index("shard")
    chip, core = index // 2, index % 2
    full = jnp.zeros((count,) + value.shape, value.dtype)
    current = value
    for step in range(chips):
        if step:
            current = ring_up(current)
        place = 2 * ((chip + chips - step) % chips)
        full = lax.dynamic_update_index_in_dim(full, current, place + core, 0)
        full = lax.dynamic_update_index_in_dim(full, other_core(current), place + 1 - core, 0)
    return full, current


def scatter_rows(parts):
    count = lax.axis_size("shard")
    chips = count // 2
    index = lax.axis_index("shard")
    chip, core = index // 2, index % 2
    by_chip = parts.reshape((chips, 2) + parts.shape[1:])
    away = lax.dynamic_index_in_dim(by_chip, 1 - core, 1, keepdims=False).astype(BF)
    kept = lax.dynamic_index_in_dim(by_chip, core, 1, keepdims=False)
    paired = kept + other_core(away).astype(F32)

    def own(step):
        return lax.dynamic_index_in_dim(paired, (chip + 2 * chips - step) % chips, 0, keepdims=False)

    running = own(1)
    for step in range(1, chips):
        running = ring_up(running.astype(BF)).astype(F32) + own(step + 1)
    return running


def joint_move(value, pairs):
    shards = lax.axis_size("shard")
    joint = [
        (r0 * shards + 2 * z0 + c, r1 * shards + 2 * z1 + c)
        for (r0, z0), (r1, z1) in pairs
        for c in range(2)
    ]
    return lax.ppermute(value, ("rep", "shard"), joint)


def gather_heads(value):
    replicas, shards = lax.axis_size("rep"), lax.axis_size("shard")
    r, index = lax.axis_index("rep"), lax.axis_index("shard")
    if shards != 2 * replicas:
        full = lax.all_gather(value, "shard", axis=0, tiled=True)
        rows = full.shape[0] // replicas
        return lax.dynamic_slice_in_dim(full, r * rows, rows, 0)
    chip, core = index // 2, index % 2
    up = [((i, z), (i, z + 1)) for i in range(replicas) for z in range(i, replicas - 1)]
    down = [((i, z), (i, z - 1)) for i in range(replicas) for z in range(1, i + 1)]
    moved_up = joint_move(value, [p for p in up if p[0][1] == p[0][0]])
    moved_down = joint_move(value, [p for p in down if p[0][1] == p[0][0]])
    total = moved_up + moved_down
    result = jnp.where(chip == r, value, total)
    moved = total
    for hop in range(2, replicas):
        pairs = [p for p in up if p[0][1] - p[0][0] == hop - 1]
        pairs += [p for p in down if p[0][0] - p[0][1] == hop - 1]
        moved = joint_move(moved, pairs)
        result = result + moved
    other = other_core(result)
    first = jnp.where(core == 0, result, other)
    second = jnp.where(core == 0, other, result)
    return jnp.concatenate([first, second], axis=0)


def scatter_heads(parts):
    replicas, shards = lax.axis_size("rep"), lax.axis_size("shard")
    r, index = lax.axis_index("rep"), lax.axis_index("shard")
    if shards != 2 * replicas:
        rows = parts.shape[0]
        full = jnp.zeros((rows * replicas,) + parts.shape[1:], F32)
        full = lax.dynamic_update_slice_in_dim(full, parts, r * rows, 0)
        owned = lax.psum_scatter(full.astype(BF), "shard", scatter_dimension=0, tiled=True)
        return lax.psum(owned, "rep").astype(F32)
    chip, core = index // 2, index % 2
    halves = parts.reshape((2, -1) + parts.shape[1:])
    away = lax.dynamic_index_in_dim(halves, 1 - core, 0, keepdims=False).astype(BF)
    total = lax.dynamic_index_in_dim(halves, core, 0, keepdims=False) + other_core(away).astype(F32)
    low = total.astype(BF)
    for hop in range(1, replicas):
        pairs = [((i, (i + hop) % replicas), (i, i)) for i in range(replicas)]
        total = total + joint_move(low, pairs).astype(F32)
    low = total.astype(BF)
    if replicas == 4:
        half = low.shape[0] // 2
        one = joint_move(low, [((z, z), (z ^ 1, z)) for z in range(4)])
        two = joint_move(low, [((z, z), (z ^ 2, z)) for z in range(4)])
        top = joint_move(one[:half], [((z ^ 1, z), (z ^ 3, z)) for z in range(4)])
        bottom = joint_move(two[half:], [((z ^ 2, z), (z ^ 3, z)) for z in range(4)])
        rest = one + two + jnp.concatenate([top, bottom], axis=0)
    else:
        rest = jnp.zeros_like(low)
        for other in range(1, replicas):
            rest = rest + joint_move(low, [((z, z), ((z + other) % replicas, z)) for z in range(replicas)])
    return jnp.where(chip == r, low, rest).astype(F32)


def piece_mask(picture_flag, size, heads):
    key = lax.broadcasted_iota(jnp.int32, (size, size * heads), 0)
    query = lax.broadcasted_iota(jnp.int32, (size, size * heads), 1) % size
    return (key <= query) | (picture_flag > 0)


def attention_forward_kernel(info, q_ref, k_ref, v_ref, mixed_ref, lse_ref):
    blocks, size = k_ref.shape[0], k_ref.shape[1]
    own = info[0]
    for last in range(blocks):
        i = own ^ last
        query = jnp.concatenate(
            [q_ref[i, :, h * HEAD_SIZE : (h + 1) * HEAD_SIZE] for h in range(GROUP)], axis=0
        )
        total = jnp.zeros((1, GROUP * size), F32)
        mixed = jnp.zeros((HEAD_SIZE, GROUP * size), F32)
        for block in range(last + 1):
            j = own ^ block
            scores = mm(k_ref[j], query, ((1,), (1,)))
            weights = jnp.exp2(scores * (SCALE * LOG2E))
            if block == last:
                weights = jnp.where(piece_mask(info[1 + i], size, GROUP), weights, 0.0)
            total = total + jnp.sum(weights, axis=0, keepdims=True)
            mixed = mixed + mm(v_ref[j], weights.astype(BF), ((0,), (0,)))
        mixed = mixed * (1.0 / total)
        log_sum = jnp.log2(total)
        for h in range(GROUP):
            columns = slice(h * size, (h + 1) * size)
            mixed_ref[i, :, h * HEAD_SIZE : (h + 1) * HEAD_SIZE] = mixed[:, columns].T.astype(BF)
            lse_ref[i, h : h + 1, :] = log_sum[:, columns]


def attention_backward_kernel(
    info, q_ref, k_ref, v_ref, mixed_ref, lse_ref, grad_ref, dq_ref, dk_ref, dv_ref
):
    blocks, size = k_ref.shape[0], k_ref.shape[1]
    own = info[0]
    dk_ref[...] = jnp.zeros_like(dk_ref)
    dv_ref[...] = jnp.zeros_like(dv_ref)
    for last in range(blocks):
        i = own ^ last
        heads = [slice(h * HEAD_SIZE, (h + 1) * HEAD_SIZE) for h in range(GROUP)]
        query = jnp.concatenate([q_ref[i, :, h] for h in heads], axis=0)
        grad = jnp.concatenate([grad_ref[i, :, h] for h in heads], axis=0)
        mixed = jnp.concatenate([mixed_ref[i, :, h] for h in heads], axis=0)
        delta = jnp.sum((grad.astype(F32) * mixed.astype(F32)).T, axis=0, keepdims=True)
        log_sum = jnp.concatenate([lse_ref[i, h : h + 1, :] for h in range(GROUP)], axis=1)
        dquery = jnp.zeros((HEAD_SIZE, GROUP * size), F32)
        for block in range(last + 1):
            j = own ^ block
            scores = mm(k_ref[j], query, ((1,), (1,)))
            dprobs = mm(v_ref[j], grad, ((1,), (1,)))
            probs = jnp.exp2(scores * (SCALE * LOG2E) - log_sum)
            if block == last:
                probs = jnp.where(piece_mask(info[1 + i], size, GROUP), probs, 0.0)
            dscores = (probs * (dprobs - delta)).astype(BF)
            dv_ref[j] += mm(probs.astype(BF), grad)
            dk_ref[j] += mm(dscores, query)
            dquery = dquery + mm(k_ref[j], dscores, ((0,), (0,)))
        for h in range(GROUP):
            dq_ref[i, :, heads[h]] = dquery[:, h * size : (h + 1) * size].T * SCALE
    dk_ref[...] = dk_ref[...] * SCALE


def attention_specs(blocks, size):
    wide = pl.BlockSpec((blocks, size, GROUP * HEAD_SIZE), lambda g, info: (0, 0, g))
    thin = pl.BlockSpec((blocks, size, HEAD_SIZE), lambda g, info: (0, 0, g))
    rows = pl.BlockSpec((None, blocks, GROUP, size), lambda g, info: (g, 0, 0, 0))
    return wide, thin, rows


def attention_forward(info, query, key, value):
    blocks, size, width = key.shape
    groups = width // HEAD_SIZE
    wide, thin, rows = attention_specs(blocks, size)
    return pl.pallas_call(
        attention_forward_kernel,
        grid_spec=pltpu.PrefetchScalarGridSpec(
            num_scalar_prefetch=1,
            grid=(groups,),
            in_specs=[wide, thin, thin],
            out_specs=[wide, rows],
        ),
        out_shape=[
            jax.ShapeDtypeStruct(query.shape, BF),
            jax.ShapeDtypeStruct((groups, blocks, GROUP, size), F32),
        ],
        compiler_params=pltpu.CompilerParams(vmem_limit_bytes=48 << 20),
        name="attention_forward",
    )(info, query, key, value)


def attention_backward(info, query, key, value, mixed, lse, grad):
    blocks, size, width = key.shape
    groups = width // HEAD_SIZE
    wide, thin, rows = attention_specs(blocks, size)
    return pl.pallas_call(
        attention_backward_kernel,
        grid_spec=pltpu.PrefetchScalarGridSpec(
            num_scalar_prefetch=1,
            grid=(groups,),
            in_specs=[wide, thin, thin, wide, rows, wide],
            out_specs=[wide, thin, thin],
        ),
        out_shape=[
            jax.ShapeDtypeStruct(query.shape, F32),
            jax.ShapeDtypeStruct(key.shape, F32),
            jax.ShapeDtypeStruct(key.shape, F32),
        ],
        compiler_params=pltpu.CompilerParams(vmem_limit_bytes=48 << 20),
        name="attention_backward",
    )(info, query, key, value, mixed, lse, grad)


def inverse_root(values):
    return lax.rsqrt(jnp.mean(values * values, axis=-1, keepdims=True) + EPSILON)


def norm_back(values, inverse, gain, dy):
    weighted = dy * gain
    inner = jnp.mean(values * weighted, axis=-1, keepdims=True)
    return inverse * weighted - values * (inverse * inverse * inverse) * inner


def turn(values):
    return jnp.concatenate([values[..., HEAD_SIZE // 2 :], values[..., : HEAD_SIZE // 2]], axis=-1)


def per_device_any(
    layer_in,
    out_grad,
    attn_norm,
    query_weight,
    key_projection,
    value_projection,
    query_norm,
    key_norm,
    out_weight,
    mlp_norm,
    gate_weight,
    up_weight,
    down_weight,
    picture_starts,
    picture_count,
):
    replicas, shards = lax.axis_size("rep"), lax.axis_size("shard")
    r = lax.axis_index("rep")
    size = layer_in.shape[1]
    length = size * replicas
    rows = attn_norm.shape[0]
    q_width = QUERY_HEADS // replicas * HEAD_SIZE
    kv_width = KEY_VALUE_HEADS // replicas * HEAD_SIZE
    attn_width = q_width + 2 * kv_width
    ff_rows = down_weight.shape[0] // replicas
    ff = ff_rows * shards

    def columns_of(weight, width):
        return lax.dynamic_slice_in_dim(weight, r * width, width, 1)

    gains = jnp.concatenate([attn_norm, mlp_norm, query_norm, key_norm])
    head_rows = query_norm.shape[0]
    gain_rows = jnp.zeros((16, attn_width), BF).at[0, : gains.shape[0]].set(gains)
    attn_rows = jnp.concatenate(
        [
            jnp.concatenate(
                [
                    columns_of(query_weight, q_width),
                    columns_of(key_projection, kv_width),
                    columns_of(value_projection, kv_width),
                ],
                axis=1,
            ),
            gain_rows,
        ],
        axis=0,
    )

    def interleaved(weight):
        cut = weight.reshape(rows, shards, replicas, ff_rows)
        return lax.dynamic_index_in_dim(cut, r, 2, keepdims=False).reshape(rows, ff)

    gate_up_rows = jnp.concatenate([interleaved(gate_weight), interleaved(up_weight)], axis=1)
    down_rows = lax.dynamic_slice_in_dim(down_weight, r * ff_rows, ff_rows, 0)

    tokens = layer_in[0]
    all_tokens = spread_blocks(tokens)
    attn_all, attn_last = gather_rows(attn_rows)
    out_weight, _ = lax.optimization_barrier((out_weight, attn_last))
    out_matrix = gather_heads(out_weight)
    gate_up_rows, down_rows, _ = lax.optimization_barrier((gate_up_rows, down_rows, attn_last))
    gate_up_all, _ = gather_rows(gate_up_rows)
    down_all, _ = gather_rows(down_rows)
    cotangent_low, _ = lax.optimization_barrier((out_grad[0], all_tokens))
    all_cotangent = spread_blocks(cotangent_low).reshape(length, MODEL_WIDTH)

    attn_matrix = attn_all[:, :rows].reshape(MODEL_WIDTH, attn_width)
    gain_all = attn_all[:, rows].astype(F32)
    attn_gain = gain_all[:, :rows].reshape(MODEL_WIDTH)
    mlp_gain = gain_all[:, rows : 2 * rows].reshape(MODEL_WIDTH)
    query_gain = gain_all[:, 2 * rows : 2 * rows + head_rows].reshape(HEAD_SIZE)
    key_gain = gain_all[:, 2 * rows + head_rows : 2 * rows + 2 * head_rows].reshape(HEAD_SIZE)
    gate_up_matrix = gate_up_all.reshape(MODEL_WIDTH, 2 * ff)
    down_matrix = down_all.reshape(ff, MODEL_WIDTH)

    block_ids = r ^ jnp.arange(replicas, dtype=jnp.int32)
    positions = (block_ids[:, None] * size + jnp.arange(size, dtype=jnp.int32)[None, :]).reshape(-1)
    half = HEAD_SIZE // 2
    inv_freq = ROPE_BASE ** (-2.0 * jnp.arange(half, dtype=F32) / HEAD_SIZE)
    angles = positions.astype(F32)[:, None] * inv_freq[None, :]
    cosine, sine = jnp.cos(angles), jnp.sin(angles)
    cos_row = jnp.concatenate([cosine, cosine], axis=1)[:, None, :]
    sin_row = jnp.concatenate([-sine, sine], axis=1)[:, None, :]
    starts = picture_starts[0]
    held = (starts[None, :] == block_ids[:, None] * PIECE) & (
        jnp.arange(starts.shape[0], dtype=jnp.int32)[None, :] < picture_count[0]
    )
    info = jnp.concatenate([r[None].astype(jnp.int32), jnp.any(held, axis=1).astype(jnp.int32)])

    wide = all_tokens.reshape(length, MODEL_WIDTH).astype(F32)
    token_inverse = inverse_root(wide)
    normed = (wide * token_inverse * attn_gain).astype(BF)
    raw = mm(normed, attn_matrix)
    query_raw = raw[:, :q_width].reshape(length, -1, HEAD_SIZE)
    key_raw = raw[:, q_width : q_width + kv_width].reshape(length, -1, HEAD_SIZE)
    value = raw[:, q_width + kv_width :].astype(BF).reshape(replicas, size, kv_width)

    def rotated(values, gain):
        scaled = values * inverse_root(values) * gain
        return (scaled * cos_row + turn(scaled) * sin_row).astype(BF).reshape(replicas, size, -1)

    query, key = rotated(query_raw, query_gain), rotated(key_raw, key_gain)
    mixed, lse = attention_forward(info, query, key, value)
    mixed_rows = mixed.reshape(length, q_width)
    after_attn = tokens.astype(F32) + sum_blocks(
        mm(mixed_rows, out_matrix).reshape(replicas, size, MODEL_WIDTH)
    )
    after_inverse = inverse_root(after_attn)
    scaled_attn = after_attn * after_inverse
    mlp_in = spread_blocks((scaled_attn * mlp_gain).astype(BF)).reshape(length, MODEL_WIDTH)
    gate_up = mm(mlp_in, gate_up_matrix)
    gate_act, up_act = gate_up[:, :ff], gate_up[:, ff:]
    sigmoid = 1.0 / (1.0 + jnp.exp(-gate_act))
    silu = gate_act * sigmoid
    hidden = (silu * up_act).astype(BF)

    hidden_grad = mm(all_cotangent, down_matrix, ((1,), (1,)))
    gate_grad = (hidden_grad * up_act * sigmoid * (1.0 + gate_act * (1.0 - sigmoid))).astype(BF)
    up_grad = (hidden_grad * silu).astype(BF)
    gate_up_grad = jnp.concatenate([gate_grad, up_grad], axis=1)
    mlp_in_part = mm(gate_up_grad, gate_up_matrix, ((1,), (1,)))
    mlp_in_grad = sum_blocks(mlp_in_part.reshape(replicas, size, MODEL_WIDTH))
    residual_grad = out_grad[0].astype(F32) + norm_back(
        after_attn, after_inverse, mlp_gain, mlp_in_grad
    )
    mlp_gain_part = jnp.sum(mlp_in_grad * scaled_attn, axis=0)
    branch_grad = spread_blocks(residual_grad.astype(BF)).reshape(length, MODEL_WIDTH)

    layer_out = after_attn + sum_blocks(mm(hidden, down_matrix).reshape(replicas, size, MODEL_WIDTH))
    gate_up_w = scatter_rows(
        mm(mlp_in, gate_up_grad, ((0,), (0,))).reshape(shards, rows, 2 * ff)
    )
    down_w = scatter_rows(
        mm(hidden, all_cotangent, ((0,), (0,))).reshape(shards, ff_rows, MODEL_WIDTH)
    )

    out_w_grad = scatter_heads(mm(mixed_rows, branch_grad, ((0,), (0,))))
    mixed_grad = mm(branch_grad, out_matrix, ((1,), (1,))).astype(BF)
    dq, dk, dv = attention_backward(
        info, query, key, value, mixed, lse, mixed_grad.reshape(replicas, size, q_width)
    )

    def head_back(values, gain, dy):
        dy = dy.reshape(length, -1, HEAD_SIZE)
        dy = dy * cos_row - turn(dy) * sin_row
        inverse = inverse_root(values)
        gain_part = jnp.sum(dy * values * inverse, axis=(0, 1))
        return norm_back(values, inverse, gain, dy).astype(BF).reshape(length, -1), gain_part

    query_grad, query_gain_part = head_back(query_raw, query_gain, dq)
    key_grad, key_gain_part = head_back(key_raw, key_gain, dk)
    attn_grad = jnp.concatenate(
        [query_grad, key_grad, dv.reshape(length, kv_width).astype(BF)], axis=1
    )
    normed_part = mm(attn_grad, attn_matrix, ((1,), (1,)))
    normed_grad = sum_blocks(normed_part.reshape(replicas, size, MODEL_WIDTH))
    attn_gain_part = jnp.sum(normed_part * (wide * token_inverse), axis=0)
    own_tokens = tokens.astype(F32)
    in_grad = residual_grad + norm_back(own_tokens, inverse_root(own_tokens), attn_gain, normed_grad)

    gain_parts = jnp.concatenate(
        [
            attn_gain_part.reshape(shards, rows),
            mlp_gain_part.reshape(shards, rows),
            query_gain_part.reshape(shards, head_rows),
            key_gain_part.reshape(shards, head_rows),
        ],
        axis=1,
    )
    gain_block = jnp.zeros((shards, 16, attn_width), F32).at[:, 0, : gain_parts.shape[1]].set(gain_parts)
    attn_w_parts = mm(normed, attn_grad, ((0,), (0,))).reshape(shards, rows, attn_width)
    attn_w = scatter_rows(jnp.concatenate([attn_w_parts, gain_block], axis=1))

    def in_order(value):
        spread = spread_blocks(value.astype(BF))
        return jnp.stack(
            [lax.dynamic_index_in_dim(spread, r ^ a, 0, keepdims=False) for a in range(replicas)]
        ).astype(F32)

    attn_full = in_order(attn_w)
    gain_full = jnp.sum(attn_full[:, rows], axis=0)

    def beside(values):
        return jnp.concatenate([values[a] for a in range(replicas)], axis=1)

    query_w_grad = beside(attn_full[:, :rows, :q_width])
    key_w_grad = beside(attn_full[:, :rows, q_width : q_width + kv_width])
    value_w_grad = beside(attn_full[:, :rows, q_width + kv_width :])
    gate_up_full = in_order(gate_up_w)

    def woven(values):
        cut = values.reshape(replicas, rows, shards, ff_rows)
        return cut.transpose(1, 2, 0, 3).reshape(rows, shards * replicas * ff_rows)

    gate_w_grad = woven(gate_up_full[:, :, :ff])
    up_w_grad = woven(gate_up_full[:, :, ff:])
    down_w_grad = in_order(down_w).reshape(replicas * ff_rows, MODEL_WIDTH)

    return (
        layer_out.astype(BF)[None],
        in_grad.astype(BF)[None],
        gain_full[:rows],
        query_w_grad,
        key_w_grad,
        value_w_grad,
        gain_full[2 * rows : 2 * rows + head_rows],
        gain_full[2 * rows + head_rows : 2 * rows + 2 * head_rows],
        out_w_grad,
        gain_full[rows : 2 * rows],
        gate_w_grad,
        up_w_grad,
        down_w_grad,
    )


BLOCKS = 4
CHIPS = 4
ROWS = 128
SIZE = 256
HALF = SIZE // 2
Q_WIDTH = QUERY_HEADS // BLOCKS * HEAD_SIZE
KV_WIDTH = KEY_VALUE_HEADS // BLOCKS * HEAD_SIZE
ATTN_WIDTH = Q_WIDTH + 2 * KV_WIDTH
GROUPS = KV_WIDTH // HEAD_SIZE
GROUP_Q = GROUP * HEAD_SIZE
GROUP_WIDTH = GROUP_Q + 2 * HEAD_SIZE
FF_ROWS = 96
FF_PART = 768
OUT_ROWS = 64
PACKED = 3 * ROWS
TURN = HEAD_SIZE // 2
LENGTH = BLOCKS * SIZE
STORE_ROWS = 32768
RAW_WIDTH = GROUP_Q + HEAD_SIZE


def shape(dims, dtype):
    return jax.ShapeDtypeStruct(dims, dtype)


def on_core(body, name, outs, scalars, args, far=(), scratch=(), limit=16, far_outs=(), aliases=None):
    return pl.pallas_call(
        body,
        name=name,
        in_specs=[pl.BlockSpec(memory_space=pltpu.SMEM)] * len(scalars)
        + [pl.BlockSpec(memory_space=pltpu.VMEM)] * len(args)
        + [pl.BlockSpec(memory_space=pl.ANY)] * len(far),
        out_specs=[pl.BlockSpec(memory_space=pltpu.VMEM)] * len(outs)
        + [pl.BlockSpec(memory_space=pl.ANY)] * len(far_outs),
        out_shape=[*outs, *far_outs],
        scratch_shapes=list(scratch),
        input_output_aliases=aliases or {},
        compiler_params=pltpu.CompilerParams(vmem_limit_bytes=limit << 20),
    )(*scalars, *args, *far)


class Loads:
    def __init__(self, semaphores):
        self.semaphores, self.used = semaphores, 0

    def __call__(self, source, target):
        copy = pltpu.make_async_copy(source, target, self.semaphores.at[self.used])
        self.used += 1
        copy.start()
        return copy


def partial_shapes():
    return [
        shape((SIZE, MODEL_WIDTH), BF),
        shape((SIZE, MODEL_WIDTH), BF),
        shape((HALF, MODEL_WIDTH), F32),
        shape((HALF, MODEL_WIDTH), F32),
        shape((SIZE, MODEL_WIDTH), F32),
    ]


def put_partial(refs, j, part):
    by_one, by_two, keep_low, keep_high, keep = refs
    if j == 0:
        keep[...] = part
    if j == 1:
        by_one[:HALF] = part[:HALF].astype(BF)
        keep_high[...] = part[HALF:]
    if j == 2:
        by_two[:HALF] = part[HALF:].astype(BF)
        keep_low[...] = part[:HALF]
    if j == 3:
        by_one[HALF:] = part[:HALF].astype(BF)
        by_two[HALF:] = part[HALF:].astype(BF)


def move_partial(by_one, by_two, keep_low, keep_high, keep):
    one, two = flip(by_one, 1), flip(by_two, 2)
    low = flip((keep_low + one[HALF:].astype(F32)).astype(BF), 2)
    high = flip((keep_high + two[HALF:].astype(F32)).astype(BF), 1)
    return keep, one, two, low, high


def joined(keep, one, two, low, high):
    top = keep[:HALF] + one[:HALF].astype(F32) + low[...].astype(F32)
    bottom = keep[HALF:] + two[:HALF].astype(F32) + high[...].astype(F32)
    return jnp.concatenate([top, bottom], axis=0)


def spread(value):
    half = value.shape[0] // 2
    one, two = flip(value, 1), flip(value, 2)
    return value, one, two, flip(one[:half], 2), flip(two[half:], 1)


def spread_direct(value):
    return value, flip(value, 1), flip(value, 2), flip(value, 3)


def tie(values, *others):
    return lax.optimization_barrier((values, others))[0]


def block_of(refs, j):
    if j < 3 or len(refs) == 4:
        return refs[j][...]
    return jnp.concatenate([ref[...] for ref in refs[3:]], axis=0)


def head_places(store, near, g):
    places = []
    for n, (ref, rows) in enumerate(zip(near, (GROUP * SIZE, SIZE, SIZE))):
        columns = slice((n * GROUPS + g) * HEAD_SIZE, (n * GROUPS + g + 1) * HEAD_SIZE)
        for j in range(BLOCKS):
            at = 2 * LENGTH + j * rows
            places.append((store.at[at : at + rows, columns], ref.at[j]))
    return places


def load_paired(loads, refs, which, target):
    at = slice(which * HALF, (which + 1) * HALF)
    return [
        loads(refs[n].at[at, :], target.at[n * HALF : (n + 1) * HALF, :]) for n in range(2 * BLOCKS)
    ]


def part_shard(info, t):
    chip = lax.rem(info[1] + CHIPS - t % CHIPS, CHIPS)
    return 2 * chip + (info[2] if t < CHIPS else 1 - info[2])


def pack_kernel(info, wq, wk, wv, wo, *refs):
    gains, (out, *rows, semaphores) = refs[:4], refs[4:]
    loads = Loads(semaphores)
    gain_loads = [loads(gain, row) for gain, row in zip(gains, rows)]
    copies = []
    for g in range(GROUPS):
        at = g * GROUP_WIDTH
        head = info[0] * GROUPS + g
        columns = pl.ds(pl.multiple_of(head * GROUP_Q, GROUP_Q), GROUP_Q)
        copies.append(loads(wq.at[:, columns], out.at[:ROWS, at : at + GROUP_Q]))
        columns = pl.ds(pl.multiple_of(head * HEAD_SIZE, HEAD_SIZE), HEAD_SIZE)
        for weight, start in ((wk, at + GROUP_Q), (wv, at + GROUP_Q + HEAD_SIZE)):
            copies.append(loads(weight.at[:, columns], out.at[:ROWS, start : start + HEAD_SIZE]))
    own = pl.ds(pl.multiple_of(info[0] * OUT_ROWS, OUT_ROWS), OUT_ROWS)
    copies.append(loads(wo.at[own, :], out.at[ROWS + 16 :, :]))
    for copy in gain_loads:
        copy.wait()
    tile = slice(ROWS, ROWS + 16)
    out[tile, :] = jnp.zeros((16, ATTN_WIDTH), BF)
    for start, row in enumerate(rows):
        width = row.shape[1]
        out[tile, start * ROWS : start * ROWS + width] = jnp.broadcast_to(row[...], (16, width))
    for copy in copies:
        copy.wait()


def pack_feed_kernel(info, gate, up, down, out):
    for a in range(BLOCKS):

        @pl.when(info[0] == a)
        def _():
            for weight, first in ((gate, 0), (up, ROWS)):
                cut = []
                for s in range(2 * CHIPS):
                    start = (s * BLOCKS + a) * FF_ROWS
                    cut.append(weight[:, start : start + FF_ROWS])
                out[first : first + ROWS, :] = jnp.concatenate(cut, axis=1)
            rows = slice(a * FF_ROWS, (a + 1) * FF_ROWS)
            out[2 * ROWS : 2 * ROWS + FF_ROWS, :] = down[rows, :FF_PART]
            for i in range(3):
                rows = slice(a * FF_ROWS + i * 32, a * FF_ROWS + (i + 1) * 32)
                out[2 * ROWS + FF_ROWS :, i * 256 : (i + 1) * 256] = down[rows, FF_PART:]


def pick_kernel(info, *refs):
    parts, outs, semaphores = refs[:CHIPS], refs[CHIPS:-1], refs[-1]
    for j in range(BLOCKS):
        step = lax.rem(info[1] + CHIPS - (info[0] ^ j), CHIPS)
        for t in range(CHIPS):

            @pl.when(step == t)
            def _():
                pltpu.make_async_copy(
                    parts[t].at[ROWS + 16 :, :], outs[j], semaphores.at[j]
                ).start()

    for j in range(BLOCKS):
        pltpu.make_async_copy(parts[0].at[ROWS + 16 :, :], outs[j], semaphores.at[j]).wait()


def project_kernel(info, cos_ref, sin_ref, *refs):
    parts, tokens = refs[:8], refs[8:16]
    q_ref, k_ref, v_ref, gain_ref, low_store, wide_store = refs[16:22]
    normed_ref, raw_ref, w_ref, all_tokens, gain_rows, semaphores = refs[22:]
    loads = Loads(semaphores)
    gain_loads, part_loads = [], []
    shards = [part_shard(info, t) for t in range(2 * CHIPS)]
    for t in range(2 * CHIPS):
        gain_loads.append(loads(parts[t].at[ROWS : ROWS + 16, :], gain_rows.at[t]))
    token_loads = load_paired(loads, tokens, 0, all_tokens)
    for t in range(2 * CHIPS):
        at = pl.ds(pl.multiple_of(shards[t] * ROWS, ROWS), ROWS)
        part_loads.append(loads(parts[t].at[:ROWS, :], w_ref.at[at, :]))
    gain_ref[...] = jnp.zeros_like(gain_ref)
    low_lane = lax.broadcasted_iota(jnp.int32, (8, HEAD_SIZE), 1) < 16
    for t in range(2 * CHIPS):
        gain_loads[t].wait()
        columns = pl.ds(pl.multiple_of(shards[t] * ROWS, ROWS), ROWS)
        row = gain_rows[t, :, : 4 * ROWS].astype(F32)[:8]
        gain_ref[0:1, columns] = row[:1, :ROWS]
        gain_ref[1:2, columns] = row[:1, ROWS : 2 * ROWS]
        for start in (0, HEAD_SIZE):
            mine = jnp.where(low_lane, row[:, 2 * ROWS + start : 3 * ROWS + start], 0.0)
            gain_ref[2:3, start : start + HEAD_SIZE] += pltpu.roll(mine, shards[t] * 16, 1)[:1]
    for j in range(BLOCKS):
        here = slice(j * SIZE, (j + 1) * SIZE)
        for copy in token_loads[2 * j : 2 * j + 2]:
            copy.wait()
        wide = all_tokens[here, :].astype(F32)
        normed = (wide * inverse_root(wide) * gain_ref[0:1, :]).astype(BF)
        normed_ref[here, :] = normed
    stores = [loads(normed_ref, low_store.at[:LENGTH, :])]
    for n, table in enumerate((cos_ref, sin_ref)):
        at = GROUPS * RAW_WIDTH + n * HEAD_SIZE
        stores.append(loads(table, wide_store.at[:LENGTH, at : at + HEAD_SIZE]))
    for copy in part_loads:
        copy.wait()
    stores.append(loads(w_ref, low_store.at[LENGTH : 2 * LENGTH, :]))
    for j in range(BLOCKS):
        here = slice(j * SIZE, (j + 1) * SIZE)
        raw = mm(normed_ref[here, :], w_ref[...])
        cosine, sine = cos_ref[here, :], sin_ref[here, :]
        for g in range(GROUPS):
            for h in range(GROUP + 1):
                at = g * GROUP_WIDTH + h * HEAD_SIZE
                one = raw[:, at : at + HEAD_SIZE]
                raw_ref[g, here, h * HEAD_SIZE : (h + 1) * HEAD_SIZE] = one
                gain_at = HEAD_SIZE if h == GROUP else 0
                scaled = one * inverse_root(one) * gain_ref[2:3, gain_at : gain_at + HEAD_SIZE]
                rotated = (scaled * cosine + pltpu.roll(scaled, TURN, 1) * sine).astype(BF)
                if h == GROUP:
                    k_ref[g, j] = rotated
                else:
                    q_ref[g, j, h * SIZE : (h + 1) * SIZE, :] = rotated
            v_ref[g, j] = raw[:, (g + 1) * GROUP_WIDTH - HEAD_SIZE : (g + 1) * GROUP_WIDTH].astype(BF)
            at = slice(g * RAW_WIDTH, (g + 1) * RAW_WIDTH)
            stores.append(loads(raw_ref.at[g, here, :], wide_store.at[here, at]))
            places = head_places(low_store, (q_ref.at[g], k_ref.at[g], v_ref.at[g]), g)
            stores += [loads(near, far) for far, near in places[j::BLOCKS]]
    for copy in stores:
        copy.wait()


def attend_kernel(info, q_ref, k_ref, v_ref, store_in, mixed_ref, lse_ref, store, semaphores):
    own = info[0]
    loads = Loads(semaphores)
    stores = []
    for last in range(BLOCKS - 1, -1, -1):
        i = own ^ last
        for g in range(GROUPS):
            query = q_ref[g, i]
            total = jnp.zeros((1, GROUP * SIZE), F32)
            mixed = jnp.zeros((HEAD_SIZE, GROUP * SIZE), F32)
            for block in range(last + 1):
                j = own ^ block
                scores = mm(k_ref[g, j], query, ((1,), (1,)))
                weights = jnp.exp2(scores * (SCALE * LOG2E))
                if block == last:
                    weights = jnp.where(piece_mask(info[3 + i], SIZE, GROUP), weights, 0.0)
                total = total + jnp.sum(weights, axis=0, keepdims=True)
                mixed = mixed + mm(v_ref[g, j], weights.astype(BF), ((0,), (0,)))
            mixed = mixed * (1.0 / total)
            for h in range(GROUP):
                columns = slice(h * SIZE, (h + 1) * SIZE)
                at = (g * GROUP + h) * HEAD_SIZE
                mixed_ref[i, :, at : at + HEAD_SIZE] = mixed[:, columns].T.astype(BF)
            lse_ref[g, i] = jnp.log2(total)
        at = pl.ds(pl.multiple_of(4 * LENGTH + i * SIZE, SIZE), SIZE)
        stores.append(loads(mixed_ref.at[i], store.at[at, :Q_WIDTH]))
    for copy in stores:
        copy.wait()


def out_kernel(info, mixed_ref, *refs):
    own_pieces, other_pieces, out_ref, partial = refs[:4], refs[4:8], refs[8], refs[9:]
    own = info[0]
    for core, rows in ((info[2], own_pieces), (1 - info[2], other_pieces)):
        for q in range(BLOCKS):
            at = pl.multiple_of(core * SIZE + (own ^ q) * OUT_ROWS, OUT_ROWS)
            out_ref[pl.ds(at, OUT_ROWS), :] = rows[q][...]
    for j in (3, 1, 2, 0):
        put_partial(partial, j, mm(mixed_ref[j], out_ref[...]))


def after_kernel(tokens, gain_ref, *refs):
    after_ref, low_ref = refs[5:]
    after = tokens[...].astype(F32) + joined(*refs[:5])
    after_ref[...] = after
    low_ref[...] = (after * inverse_root(after) * gain_ref[1:2, :]).astype(BF)


def prepare_kernel(info, *refs):
    parts, pieces = refs[:8], refs[8:16]
    gate_up_ref, down_ref, cotangent = refs[16:19]
    grads, semaphores = refs[19:23], refs[23]
    loads = Loads(semaphores)
    down_loads, gate_loads = [], []
    cotangent_loads = load_paired(loads, pieces, 1, cotangent)
    for t in range(2 * CHIPS):
        s = part_shard(info, t)
        at = pl.ds(pl.multiple_of(s * FF_ROWS, 32), FF_ROWS)
        rows = slice(2 * ROWS, 2 * ROWS + FF_ROWS)
        down_loads.append(loads(parts[t].at[rows, :], down_ref.at[at, :FF_PART]))
        for i in range(3):
            at = pl.ds(pl.multiple_of(s * FF_ROWS + i * 32, 32), 32)
            rest = parts[t].at[2 * ROWS + FF_ROWS :, i * 256 : (i + 1) * 256]
            down_loads.append(loads(rest, down_ref.at[at, FF_PART:]))
    for t in range(2 * CHIPS):
        at = pl.ds(pl.multiple_of(part_shard(info, t) * ROWS, ROWS), ROWS)
        gate_loads.append(loads(parts[t].at[:ROWS, :], gate_up_ref.at[at, :FF_PART]))
        gate_loads.append(loads(parts[t].at[ROWS : 2 * ROWS, :], gate_up_ref.at[at, FF_PART:]))
    for copy in cotangent_loads + down_loads:
        copy.wait()
    for j in range(BLOCKS):
        here = slice(j * SIZE, (j + 1) * SIZE)
        grads[j][...] = mm(cotangent[here, :], down_ref[...], ((1,), (1,)))
    for copy in gate_loads:
        copy.wait()


def feed_kernel(blocks, *refs):
    count = len(blocks)
    last = blocks == (3,)
    extra = 2 if last else count
    inputs, hidden_grads = refs[:extra], refs[extra : extra + count]
    gate_up_ref = refs[extra + count]
    if last:
        first_a, second_b = refs[extra + count + 1 : extra + count + 3]
    outs = refs[extra + count + (3 if last else 1) :]
    for n, j in enumerate(blocks):
        tokens = jnp.concatenate([inputs[0][...], inputs[1][...]], axis=0) if last else inputs[n][...]
        hidden_ref, both_ref = outs[2 * n : 2 * n + 2]
        gate_up = mm(tokens, gate_up_ref[...])
        gate, up = gate_up[:, :FF_PART], gate_up[:, FF_PART:]
        sigmoid = 1.0 / (1.0 + jnp.exp(-gate))
        silu = gate * sigmoid
        hidden_ref[...] = (silu * up).astype(BF)
        grad = hidden_grads[n][...]
        both_ref[:, :FF_PART] = (grad * up * sigmoid * (1.0 + gate * (1.0 - sigmoid))).astype(BF)
        both_ref[:, FF_PART:] = (grad * silu).astype(BF)
        part = mm(both_ref[...], gate_up_ref[...], ((1,), (1,)))
        first, second = outs[2 * count + 2 * n : 2 * count + 2 * n + 2]
        if last:
            first[:HALF] = first_a[...]
            first[HALF:] = part[:HALF].astype(BF)
            second[:HALF] = second_b[...]
            second[HALF:] = part[HALF:].astype(BF)
        else:
            first[...] = part[:HALF].astype(first.dtype)
            second[...] = part[HALF:].astype(second.dtype)


FEED_TYPES = {0: (F32, F32), 1: (BF, F32), 2: (F32, BF), 3: (BF, BF)}


def feed(blocks, inputs, hidden_grads, gate_up, earlier=()):
    outs = []
    for _ in blocks:
        outs += [shape((SIZE, FF_PART), BF), shape((SIZE, 2 * FF_PART), BF)]
    for j in blocks:
        outs += [shape((SIZE if j == 3 else HALF, MODEL_WIDTH), dtype) for dtype in FEED_TYPES[j]]

    def body(*refs):
        feed_kernel(blocks, *refs)

    args = (*inputs, *hidden_grads, gate_up, *earlier)
    result = on_core(body, "feed", outs, (), args)
    count = len(blocks)
    hidden, both = result[0 : 2 * count : 2], result[1 : 2 * count : 2]
    return hidden, both, result[2 * count :]


def split_rows(info, kept, away, t, at, values):
    half = values.shape[0] // 2
    first, second = values[:half], values[half:]
    is_first = info[2] == 0
    kept[t, at : at + half, :] = jnp.where(is_first, first, second)
    away[t, at : at + half, :] = jnp.where(is_first, second, first).astype(BF)


def feed_weights_kernel(info, cotangent, *refs):
    hidden, both, mlp_in = refs[:4], refs[4:8], refs[8:13]
    kept, away, down_grad, stored, semaphores = refs[13:]
    loads = Loads(semaphores)
    copies = [loads(mlp_in[j], stored.at[j * SIZE : (j + 1) * SIZE, :]) for j in range(3)]
    copies += [
        loads(mlp_in[3 + n], stored.at[3 * SIZE + n * HALF : 3 * SIZE + (n + 1) * HALF, :])
        for n in range(2)
    ]
    both_all = jnp.concatenate([ref[...] for ref in both], axis=0)
    hidden_all = jnp.concatenate([ref[...] for ref in hidden], axis=0)
    down_grad[...] = mm(hidden_all, cotangent[...], ((0,), (0,)))
    for copy in copies:
        copy.wait()
    for t in range(CHIPS):
        chip = lax.rem(info[1] + 2 * CHIPS - (t + 1), CHIPS)
        columns = stored[:, pl.ds(pl.multiple_of(chip * 2 * ROWS, 2 * ROWS), 2 * ROWS)]
        product = mm(columns, both_all, ((0,), (0,)))
        split_rows(info, kept, away, t, 0, product[:, :FF_PART])
        split_rows(info, kept, away, t, ROWS, product[:, FF_PART:])
        for core, target in ((info[2], kept), (1 - info[2], away)):
            at = pl.multiple_of((2 * chip + core) * FF_ROWS, 32)
            rows = down_grad[pl.ds(at, FF_ROWS), :].astype(target.dtype)
            target[t, 2 * ROWS : 2 * ROWS + FF_ROWS, :] = rows[:, :FF_PART]
            for i in range(3):
                target[t, 2 * ROWS + FF_ROWS :, i * 256 : (i + 1) * 256] = rows[
                    i * 32 : (i + 1) * 32, FF_PART:
                ]


def down_kernel(down_ref, *refs):
    hidden, partial = refs[:4], refs[4:]
    for j in (3, 1, 2, 0):
        put_partial(partial, j, mm(hidden[j][...], down_ref[...]))


def residual_kernel(cotangent, after_ref, gain_ref, *refs):
    low_ref, gain_part = refs[-2:]
    keep_a, keep_b, one, two, low, high = refs[:6]
    top = keep_a[...] + one[:HALF].astype(F32) + low[...].astype(F32)
    bottom = keep_b[...] + two[:HALF].astype(F32) + high[...].astype(F32)
    mlp_in_grad = jnp.concatenate([top, bottom], axis=0)
    after = after_ref[...]
    inverse = inverse_root(after)
    gain_part[...] = jnp.sum(mlp_in_grad * (after * inverse), axis=0, keepdims=True)
    grad = cotangent[...].astype(F32) + norm_back(after, inverse, gain_ref[1:2, :], mlp_in_grad)
    low_ref[...] = grad.astype(BF)


def mixed_grad_kernel(info, out_ref, *refs):
    branch, store, (grad_ref, kept, away, scratch, mixed_ref, semaphores) = refs[:5], refs[5], refs[6:]
    mixed_load = Loads(semaphores)(store.at[4 * LENGTH : 5 * LENGTH, :Q_WIDTH], mixed_ref)
    own = info[0]
    for j in range(BLOCKS):
        grad_ref[j] = mm(block_of(branch, j), out_ref[...], ((1,), (1,))).astype(BF)
    branch_all = jnp.concatenate([block_of(branch, j) for j in range(BLOCKS)], axis=0)
    mixed_load.wait()
    scratch[...] = mm(mixed_ref[...], branch_all, ((0,), (0,)))
    for core, target in ((info[2], kept), (1 - info[2], away)):
        for q in range(BLOCKS):
            at = pl.multiple_of(core * SIZE + (own ^ q) * OUT_ROWS, OUT_ROWS)
            target[q] = scratch[pl.ds(at, OUT_ROWS), :].astype(target.dtype)


def pair_kernel(kept, crossed, *outs):
    for j, out in enumerate(outs):
        out[...] = (kept[j] + crossed[j].astype(F32)).astype(BF)


def head_back(grad, cosine, sine, raw, gain):
    dy = grad * cosine - pltpu.roll(grad, TURN, 1) * sine
    inverse = inverse_root(raw)
    gain_part = jnp.sum(dy * (raw * inverse), axis=0, keepdims=True)
    return norm_back(raw, inverse, gain, dy).astype(BF), gain_part


def attend_back_kernel(g, info, lse_ref, grad_ref, mlp_part, gain_ref, *refs):
    (store, wide_store), (out_ref, kept, away, dk_ref, dv_ref) = refs[:2], refs[2:7]
    q_ref, k_ref, v_ref, mixed_ref, raw_ref, cos_ref, sin_ref, normed_ref, w_ref, semaphores = refs[7:]
    loads = Loads(semaphores)
    first = [loads(far, near) for far, near in head_places(store, (q_ref, k_ref, v_ref), g)]
    at = slice(g * GROUP_Q, (g + 1) * GROUP_Q)
    first += [
        loads(store.at[4 * LENGTH + j * SIZE : 4 * LENGTH + (j + 1) * SIZE, at], mixed_ref.at[j])
        for j in range(BLOCKS)
    ]
    second = [loads(wide_store.at[:LENGTH, g * RAW_WIDTH : (g + 1) * RAW_WIDTH], raw_ref)]
    for n, table in enumerate((cos_ref, sin_ref)):
        at = GROUPS * RAW_WIDTH + n * HEAD_SIZE
        second.append(loads(wide_store.at[:LENGTH, at : at + HEAD_SIZE], table))
    at = slice(g * GROUP_WIDTH, (g + 1) * GROUP_WIDTH)
    third = [
        loads(store.at[:LENGTH, :], normed_ref),
        loads(store.at[LENGTH : 2 * LENGTH, at], w_ref),
    ]
    own = info[0]
    query_part = jnp.zeros((1, HEAD_SIZE), F32)
    key_part = jnp.zeros((1, HEAD_SIZE), F32)
    dk_ref[...] = jnp.zeros_like(dk_ref)
    dv_ref[...] = jnp.zeros_like(dv_ref)
    for copy in first:
        copy.wait()
    for last in range(BLOCKS):
        i = own ^ last
        rows = pl.ds(pl.multiple_of(i * SIZE, SIZE), SIZE)
        heads = [slice((g * GROUP + h) * HEAD_SIZE, (g * GROUP + h + 1) * HEAD_SIZE) for h in range(GROUP)]
        query = q_ref[i]
        grad = jnp.concatenate([grad_ref[i, :, h] for h in heads], axis=0)
        mixed = jnp.concatenate(
            [mixed_ref[i, :, h * HEAD_SIZE : (h + 1) * HEAD_SIZE] for h in range(GROUP)], axis=0
        )
        delta = jnp.sum((grad.astype(F32) * mixed.astype(F32)).T, axis=0, keepdims=True)
        log_sum = lse_ref[g, i]
        dquery = jnp.zeros((HEAD_SIZE, GROUP * SIZE), F32)
        for block in range(last + 1):
            j = own ^ block
            scores = mm(k_ref[j], query, ((1,), (1,)))
            dprobs = mm(v_ref[j], grad, ((1,), (1,)))
            probs = jnp.exp2(scores * (SCALE * LOG2E) - log_sum)
            if block == last:
                probs = jnp.where(piece_mask(info[3 + i], SIZE, GROUP), probs, 0.0)
            dscores = (probs * (dprobs - delta)).astype(BF)
            dv_ref[j] += mm(probs.astype(BF), grad)
            dk_ref[j] += mm(dscores, query)
            dquery = dquery + mm(k_ref[j], dscores, ((0,), (0,)))
        if last == 0:
            for copy in second:
                copy.wait()
        for h in range(GROUP):
            at = slice(h * HEAD_SIZE, (h + 1) * HEAD_SIZE)
            back, part = head_back(
                dquery[:, h * SIZE : (h + 1) * SIZE].T * SCALE,
                cos_ref[rows, :],
                sin_ref[rows, :],
                raw_ref[rows, at],
                gain_ref[2:3, :HEAD_SIZE],
            )
            out_ref[rows, at] = back
            query_part = query_part + part
    for j in range(BLOCKS):
        rows = slice(j * SIZE, (j + 1) * SIZE)
        at = slice(GROUP_Q, GROUP_Q + HEAD_SIZE)
        back, part = head_back(
            dk_ref[j] * SCALE,
            cos_ref[rows, :],
            sin_ref[rows, :],
            raw_ref[rows, at],
            gain_ref[2:3, HEAD_SIZE : 2 * HEAD_SIZE],
        )
        out_ref[rows, at] = back
        key_part = key_part + part
        out_ref[rows, GROUP_Q + HEAD_SIZE :] = dv_ref[j].astype(BF)
    for copy in third:
        copy.wait()
    row = lax.broadcasted_iota(jnp.int32, (16, GROUP_WIDTH), 0)
    for t in range(CHIPS):
        chip = lax.rem(info[1] + 2 * CHIPS - (t + 1), CHIPS)
        at = pl.ds(pl.multiple_of(chip * 2 * ROWS, 2 * ROWS), 2 * ROWS)
        product = mm(normed_ref[:, at], out_ref[...], ((0,), (0,)))
        split_rows(info, kept, away, t, 0, product)
        inner = jnp.sum(product * w_ref[at, :].astype(F32), axis=1, keepdims=True)
        inner = jnp.broadcast_to(inner, (2 * ROWS, ROWS)).T[0:1] / gain_ref[0:1, at]
        mlp = mlp_part[0:1, at] if g == 0 else jnp.zeros_like(inner)
        for is_first, half in ((True, slice(0, ROWS)), (False, slice(ROWS, 2 * ROWS))):
            values = jnp.concatenate([inner[:, half], mlp[:, half], query_part, key_part], axis=1)
            values = jnp.where(row == 0, values, 0.0)

            @pl.when((info[2] == 0) == is_first)
            def _():
                kept[t, ROWS:, :] = values

            @pl.when((info[2] == 0) != is_first)
            def _():
                away[t, ROWS:, :] = values.astype(BF)


def normed_grad_kernel(*refs):
    grads, store, partial, (w_ref, semaphores) = refs[:GROUPS], refs[GROUPS], refs[GROUPS + 1 : -2], refs[-2:]
    Loads(semaphores)(store.at[LENGTH : 2 * LENGTH, :], w_ref).wait()
    for j in (3, 1, 2, 0):
        here = slice(j * SIZE, (j + 1) * SIZE)
        grad = jnp.concatenate([ref[here, :] for ref in grads], axis=1)
        put_partial(partial, j, mm(grad, w_ref[...], ((1,), (1,))))


def final_kernel(tokens, gain_ref, residual, *refs):
    grad_ref = refs[5]
    wide = tokens[...].astype(F32)
    dy = joined(*refs[:5])
    back = norm_back(wide, inverse_root(wide), gain_ref[0:1, :], dy)
    grad_ref[...] = (residual[...].astype(F32) + back).astype(BF)


def output_kernel(after_ref, *refs):
    refs[5][...] = (after_ref[...] + joined(*refs[:5])).astype(BF)


def unpack_feed_kernel(info, *refs):
    pieces, (gate_ref, up_ref, down_ref, scratch) = refs[:5], refs[5:]
    for j in range(BLOCKS):
        scratch[info[0] ^ j] = block_of(pieces, j).astype(F32)
    for first, target in ((0, gate_ref), (ROWS, up_ref)):
        for s in range(0, 2 * CHIPS):
            columns = slice(s * FF_ROWS, (s + 1) * FF_ROWS)
            cut = [scratch[a, first : first + ROWS, columns] for a in range(BLOCKS)]
            target[:, s * BLOCKS * FF_ROWS : (s + 1) * BLOCKS * FF_ROWS] = jnp.concatenate(cut, axis=1)
    for a in range(BLOCKS):
        at = slice(a * FF_ROWS, (a + 1) * FF_ROWS)
        down_ref[at, :FF_PART] = scratch[a, 2 * ROWS : 2 * ROWS + FF_ROWS, :]
        for i in range(3):
            at = slice(a * FF_ROWS + i * 32, a * FF_ROWS + (i + 1) * 32)
            down_ref[at, FF_PART:] = scratch[a, 2 * ROWS + FF_ROWS :, i * 256 : (i + 1) * 256]


def unpack_attend_kernel(info, *refs):
    pieces, (query_ref, key_ref, value_ref, out_ref, *gain_refs) = (refs[:4], refs[4:8]), refs[8:]
    gains = jnp.zeros((8, GROUP_WIDTH), F32)
    for g in range(GROUPS):
        for j in range(BLOCKS):
            piece = pieces[g][j]
            head = (info[0] ^ j) * GROUPS + g
            values = piece[:ROWS, :].astype(F32)
            wide = pl.ds(pl.multiple_of(head * GROUP_Q, GROUP_Q), GROUP_Q)
            thin = pl.ds(pl.multiple_of(head * HEAD_SIZE, HEAD_SIZE), HEAD_SIZE)
            query_ref[:, wide] = values[:, :GROUP_Q]
            key_ref[:, thin] = values[:, GROUP_Q : GROUP_Q + HEAD_SIZE]
            value_ref[:, thin] = values[:, GROUP_Q + HEAD_SIZE :]
            gains = gains + piece[ROWS : ROWS + 16, :].astype(F32)[:8]
            if g == 0:
                rows = pl.ds(pl.multiple_of((info[0] ^ j) * OUT_ROWS, OUT_ROWS), OUT_ROWS)
                top = piece[ROWS + 16 : ROWS + 16 + OUT_ROWS, :].astype(F32)
                out_ref[rows, :GROUP_WIDTH] = top
                out_ref[rows, GROUP_WIDTH:] = piece[ROWS + 16 + OUT_ROWS :, :].astype(F32)
    gain_refs[0][...] = gains[:1, :ROWS]
    gain_refs[1][...] = gains[:1, ROWS : 2 * ROWS]
    shard = 2 * info[1] + info[2]
    for n, target in enumerate(gain_refs[2:]):
        width = target.shape[1]
        lanes = gains[:, 2 * ROWS + n * HEAD_SIZE : 2 * ROWS + (n + 1) * HEAD_SIZE]
        turned = pltpu.roll(lanes, lax.rem(HEAD_SIZE - shard * width, HEAD_SIZE), 1)
        target[...] = turned[:1, :width]


def ring_parts(value, swapped, then):
    own, other = [value], [swapped]
    for t in range(1, CHIPS):
        ready = then.get(t, ())
        if t > 1:
            ready = (ready, other[t - 2])
        own.append(ring_up(tie(own[-1], ready)))
        other.append(other_core(own[-1]))
    return own, other


def ring_term(kept, crossed, t, previous=None, beside=None, after=()):
    value = kept[t] + crossed[t].astype(F32)
    count = value.shape[0]
    if t:
        moved = tie(ring_up(previous), after)
        value = value + moved[:count].astype(F32)
    value = value.astype(BF)
    if beside is not None:
        extra = beside(t + 1)
        if t:
            extra = (moved[count:].astype(F32) + extra.astype(F32)).astype(BF)
        value = jnp.concatenate([value, extra], axis=0)
    return value


def ring_sum(kept, crossed, beside=None):
    running = [ring_term(kept, crossed, 0, None, beside)]
    for t in range(1, CHIPS):
        running.append(ring_term(kept, crossed, t, running[-1], beside))
    return running


def per_device(
    layer_in,
    out_grad,
    attn_norm,
    query_weight,
    key_projection,
    value_projection,
    query_norm,
    key_norm,
    out_weight,
    mlp_norm,
    gate_weight,
    up_weight,
    down_weight,
    picture_starts,
    picture_count,
):
    r, index = lax.axis_index("rep"), lax.axis_index("shard")
    chip, core = index // 2, index % 2
    length = BLOCKS * SIZE
    tokens, cotangent_own = layer_in[0], out_grad[0]

    block_ids = r ^ jnp.arange(BLOCKS, dtype=jnp.int32)
    starts = picture_starts[0]
    held = (starts[None, :] == block_ids[:, None] * PIECE) & (
        jnp.arange(starts.shape[0], dtype=jnp.int32)[None, :] < picture_count[0]
    )
    place = jnp.stack([r, chip, core]).astype(jnp.int32)
    info = jnp.concatenate([place, jnp.any(held, axis=1).astype(jnp.int32)])

    gains = tuple(gain.reshape(1, -1) for gain in (attn_norm, mlp_norm, query_norm, key_norm))
    (attn_rows,) = on_core(
        pack_kernel,
        "pack",
        [shape((ROWS + 16 + OUT_ROWS, ATTN_WIDTH), BF)],
        (place,),
        (),
        (query_weight, key_projection, value_projection, out_weight, *gains),
        [pltpu.VMEM(gain.shape, BF) for gain in gains] + [pltpu.SemaphoreType.DMA((11,))],
        62,
    )
    attn_swap = other_core(attn_rows)
    low_half, high_half = tie(
        tuple(jnp.concatenate([tokens[at], cotangent_own[at]]) for at in (slice(0, HALF), slice(HALF, SIZE))),
        attn_rows,
    )
    one = flip(low_half, 1), flip(high_half, 1)
    two = flip(low_half, 2), flip(high_half, 2)
    pieces = (low_half, high_half, *one, *two, flip(one[0], 2), flip(two[1], 1))
    (feed_rows,) = on_core(
        pack_feed_kernel,
        "pack_feed",
        [shape((PACKED, FF_PART), BF)],
        (place,),
        tie((gate_weight, up_weight, down_weight), attn_rows),
    )

    positions = (block_ids[:, None] * SIZE + jnp.arange(SIZE, dtype=jnp.int32)[None, :]).reshape(-1)
    inv_freq = ROPE_BASE ** (-2.0 * jnp.arange(TURN, dtype=F32) / HEAD_SIZE)
    angles = positions.astype(F32)[:, None] * inv_freq[None, :]
    cosine, sine = jnp.cos(angles), jnp.sin(angles)
    cos_rows = jnp.concatenate([cosine, cosine], axis=1)
    sin_rows = jnp.concatenate([-sine, sine], axis=1)

    attn_own, attn_other = ring_parts(
        attn_rows, attn_swap, {2: (feed_rows, info), 3: (one, two, cos_rows, sin_rows)}
    )

    picked = on_core(
        pick_kernel,
        "pick",
        [shape((OUT_ROWS, MODEL_WIDTH), BF)] * BLOCKS,
        (place,),
        (),
        attn_own,
        [pltpu.SemaphoreType.DMA((BLOCKS,))],
    )
    out_own = [picked[0]] + [flip(picked[j], j) for j in (1, 2, 3)]

    heads = [
        shape((GROUPS, BLOCKS, GROUP * SIZE, HEAD_SIZE), BF),
        shape((GROUPS, BLOCKS, SIZE, HEAD_SIZE), BF),
        shape((GROUPS, BLOCKS, SIZE, HEAD_SIZE), BF),
    ]
    store_shape = shape((STORE_ROWS, MODEL_WIDTH), BF)
    query, key, value, gain_rows, store, wide_store = on_core(
        project_kernel,
        "project",
        heads + [shape((8, MODEL_WIDTH), F32)],
        (info,),
        (cos_rows, sin_rows),
        (*attn_own, *attn_other, *pieces),
        [
            pltpu.VMEM((length, MODEL_WIDTH), BF),
            pltpu.VMEM((GROUPS, length, RAW_WIDTH), F32),
            pltpu.VMEM((MODEL_WIDTH, ATTN_WIDTH), BF),
            pltpu.VMEM((length, MODEL_WIDTH), BF),
            pltpu.VMEM((2 * CHIPS, 16, ATTN_WIDTH), BF),
            pltpu.SemaphoreType.DMA((14 * CHIPS + 4,)),
        ],
        24,
        [store_shape, shape((STORE_ROWS // 2, MODEL_WIDTH), F32)],
    )
    mixed, lse, store = on_core(
        attend_kernel,
        "attend",
        [
            shape((BLOCKS, SIZE, Q_WIDTH), BF),
            shape((GROUPS, BLOCKS, 1, GROUP * SIZE), F32),
        ],
        (info,),
        (query, key, value),
        (store,),
        [pltpu.SemaphoreType.DMA((BLOCKS,))],
        16,
        [store_shape],
        {4: 2},
    )
    out_own = tie(out_own, query)
    out_other = other_core(jnp.concatenate(out_own, axis=0))
    out_other = [out_other[j * OUT_ROWS : (j + 1) * OUT_ROWS] for j in range(BLOCKS)]
    out_matrix, *partial = on_core(
        out_kernel,
        "out",
        [shape((Q_WIDTH, MODEL_WIDTH), BF)] + partial_shapes(),
        (info,),
        (mixed, *out_own, *out_other),
    )
    feed_start = tie(feed_rows, attn_own[-1])
    feed_own, feed_other = ring_parts(feed_start, other_core(feed_start), {2: mixed, 3: partial[0]})
    partial = move_partial(*partial)
    after_attn, mlp_own = on_core(
        after_kernel,
        "after",
        [shape((SIZE, MODEL_WIDTH), F32), shape((SIZE, MODEL_WIDTH), BF)],
        (),
        (tokens, gain_rows, *partial),
    )
    mlp_in = spread(mlp_own)
    gate_up, down, cotangent, *hidden_grads = on_core(
        prepare_kernel,
        "prepare",
        [
            shape((MODEL_WIDTH, 2 * FF_PART), BF),
            shape((FF_PART, MODEL_WIDTH), BF),
            shape((length, MODEL_WIDTH), BF),
        ]
        + [shape((SIZE, FF_PART), F32)] * BLOCKS,
        (info,),
        (),
        (*tie((*feed_own, *feed_other), mlp_own), *pieces),
        [pltpu.SemaphoreType.DMA((14 * CHIPS,))],
    )
    hidden_0, both_0, keep = feed((0,), mlp_in[:1], hidden_grads[:1], gate_up)
    hidden_12, both_12, (one_a, keep_high, keep_low, two_a) = feed(
        (1, 2), tie(mlp_in[1:3], both_0), hidden_grads[1:3], gate_up
    )
    hidden_3, both_3, (one, two) = feed(
        (3,), tie(mlp_in[3:], both_12), hidden_grads[3:], gate_up, (one_a, two_a)
    )
    hidden = [*hidden_0, *hidden_12, *hidden_3]
    both = [*both_0, *both_12, *both_3]

    feed_kept, feed_away = on_core(
        feed_weights_kernel,
        "feed_weights",
        [
            shape((CHIPS, PACKED, FF_PART), F32),
            shape((CHIPS, PACKED, FF_PART), BF),
        ],
        (info,),
        (cotangent, *hidden, *both),
        mlp_in,
        [
            pltpu.VMEM((FF_PART, MODEL_WIDTH), F32),
            pltpu.VMEM((length, MODEL_WIDTH), BF),
            pltpu.SemaphoreType.DMA((5,)),
        ],
        24,
    )
    one, two = tie((flip(one, 1), flip(two, 2)), feed_kept)
    low = (keep_low + one[HALF:].astype(F32)).astype(BF)
    high = (keep_high + two[HALF:].astype(F32)).astype(BF)
    crossed = other_core(tie(feed_away, low, high))
    low, high = flip(low, 2), flip(high, 1)
    branch_own, mlp_gain_part = on_core(
        residual_kernel,
        "residual",
        [
            shape((SIZE, MODEL_WIDTH), BF),
            shape((1, MODEL_WIDTH), F32),
        ],
        (),
        (cotangent_own, after_attn, gain_rows, *tie((*keep, one, two, low, high), crossed)),
    )
    branch = spread(branch_own)
    feed_ring = [ring_term(feed_kept, crossed, 0)]
    feed_ring.append(ring_term(feed_kept, crossed, 1, feed_ring[0]))
    layer_partial = on_core(
        down_kernel, "down", partial_shapes(), (), tie((down, *hidden), branch_own, feed_ring[0])
    )

    mixed_grad, out_kept, out_away = on_core(
        mixed_grad_kernel,
        "mixed_grad",
        [
            shape((BLOCKS, SIZE, Q_WIDTH), BF),
            shape((BLOCKS, OUT_ROWS, MODEL_WIDTH), F32),
            shape((BLOCKS, OUT_ROWS, MODEL_WIDTH), BF),
        ],
        (info,),
        (out_matrix, *tie(branch, layer_partial, feed_ring[1])),
        (store,),
        [
            pltpu.VMEM((Q_WIDTH, MODEL_WIDTH), F32),
            pltpu.VMEM((length, Q_WIDTH), BF),
            pltpu.SemaphoreType.DMA((1,)),
        ],
    )
    out_pair = on_core(
        pair_kernel,
        "pair",
        [shape((OUT_ROWS, MODEL_WIDTH), BF)] * BLOCKS,
        (),
        (out_kept, other_core(out_away)),
    )
    out_moved = [out_pair[0]] + [flip(out_pair[j], j) for j in (1, 2, 3)]

    def back(g, grad):
        def body(*refs):
            attend_back_kernel(g, *refs)

        return on_core(
            body,
            "attend_back",
            [
                shape((length, GROUP_WIDTH), BF),
                shape((CHIPS, ROWS + 16, GROUP_WIDTH), F32),
                shape((CHIPS, ROWS + 16, GROUP_WIDTH), BF),
            ],
            (info,),
            (lse, grad, mlp_gain_part, gain_rows),
            (store, wide_store),
            [
                pltpu.VMEM((BLOCKS, SIZE, HEAD_SIZE), F32),
                pltpu.VMEM((BLOCKS, SIZE, HEAD_SIZE), F32),
                pltpu.VMEM((BLOCKS, GROUP * SIZE, HEAD_SIZE), BF),
                pltpu.VMEM((BLOCKS, SIZE, HEAD_SIZE), BF),
                pltpu.VMEM((BLOCKS, SIZE, HEAD_SIZE), BF),
                pltpu.VMEM((BLOCKS, SIZE, GROUP_Q), BF),
                pltpu.VMEM((length, RAW_WIDTH), F32),
                pltpu.VMEM((length, HEAD_SIZE), F32),
                pltpu.VMEM((length, HEAD_SIZE), F32),
                pltpu.VMEM((length, MODEL_WIDTH), BF),
                pltpu.VMEM((MODEL_WIDTH, GROUP_WIDTH), BF),
                pltpu.SemaphoreType.DMA((4 * BLOCKS + 5,)),
            ],
        )

    grad_0, kept_0, away_0 = back(0, tie(mixed_grad, out_pair))
    out_blocks = jnp.stack(tie(out_moved, grad_0))

    def out_step(t):
        block = lax.dynamic_index_in_dim(
            out_blocks, r ^ ((chip + 2 * CHIPS - t) % CHIPS), 0, keepdims=False
        )
        return jnp.concatenate([block[:, :GROUP_WIDTH], block[:, GROUP_WIDTH:]], axis=0)

    kept = (kept_0, other_core(away_0))
    attn_first = [ring_term(*kept, 0, None, out_step)]
    feed_ring.append(ring_term(feed_kept, crossed, 2, feed_ring[1], None, grad_0))
    layer_one, layer_two, layer_low, layer_high, layer_keep = tie(layer_partial, grad_0)
    layer_one, layer_two = flip(layer_one, 1), flip(layer_two, 2)
    grad_1, kept_1, away_1 = back(1, tie(mixed_grad, attn_first[0], feed_ring[2]))
    layer_one, layer_two = tie((layer_one, layer_two), grad_1)
    layer_low = flip((layer_low + layer_one[HALF:].astype(F32)).astype(BF), 2)
    layer_high = flip((layer_high + layer_two[HALF:].astype(F32)).astype(BF), 1)
    for t in range(1, CHIPS):
        attn_first.append(ring_term(*kept, t, attn_first[-1], out_step, grad_1))
    feed_ring.append(ring_term(feed_kept, crossed, 3, feed_ring[2], None, grad_1))
    attn_second = ring_sum(kept_1, other_core(away_1))
    partial = on_core(
        normed_grad_kernel,
        "normed_grad",
        partial_shapes(),
        (),
        tie((grad_0, grad_1), out_blocks, attn_second[0]),
        (store,),
        [pltpu.VMEM((MODEL_WIDTH, ATTN_WIDTH), BF), pltpu.SemaphoreType.DMA((1,))],
    )
    (layer_out,) = on_core(
        output_kernel,
        "output",
        [shape((SIZE, MODEL_WIDTH), BF)],
        (),
        (after_attn, layer_keep, layer_one, layer_two, layer_low, layer_high),
    )
    (in_grad,) = on_core(
        final_kernel,
        "final",
        [shape((SIZE, MODEL_WIDTH), BF)],
        (),
        (tokens, gain_rows, branch_own, *move_partial(*partial)),
    )

    gate_w_grad, up_w_grad, down_w_grad = on_core(
        unpack_feed_kernel,
        "unpack_feed",
        [
            shape((ROWS, 2 * CHIPS * BLOCKS * FF_ROWS), F32),
            shape((ROWS, 2 * CHIPS * BLOCKS * FF_ROWS), F32),
            shape((BLOCKS * FF_ROWS, MODEL_WIDTH), F32),
        ],
        (place,),
        spread(feed_ring[-1]),
        (),
        [pltpu.VMEM((BLOCKS, PACKED, FF_PART), F32)],
    )
    head_rows = query_norm.shape[0]
    query_w_grad, key_w_grad, value_w_grad, out_w_grad, *gains = on_core(
        unpack_attend_kernel,
        "unpack_attend",
        [
            shape((ROWS, QUERY_HEADS * HEAD_SIZE), F32),
            shape((ROWS, KEY_VALUE_HEADS * HEAD_SIZE), F32),
            shape((ROWS, KEY_VALUE_HEADS * HEAD_SIZE), F32),
            shape((SIZE, MODEL_WIDTH), F32),
            shape((1, ROWS), F32),
            shape((1, ROWS), F32),
            shape((1, head_rows), F32),
            shape((1, head_rows), F32),
        ],
        (place,),
        (*spread_direct(attn_first[-1]), *spread_direct(attn_second[-1])),
    )
    gains = [gain.reshape(-1) for gain in gains]

    return (
        layer_out[None],
        in_grad[None],
        gains[0],
        query_w_grad,
        key_w_grad,
        value_w_grad,
        gains[2],
        gains[3],
        out_w_grad,
        gains[1],
        gate_w_grad,
        up_w_grad,
        down_w_grad,
    )


def solution(mesh):
    tokens, matrix, vector = P("shard", "rep", None), P("shard", None), P("shard")
    return jax.shard_map(
        per_device if dict(mesh.shape) == {"rep": 4, "shard": 8} else per_device_any,
        mesh=mesh,
        in_specs=(tokens, tokens, vector, matrix, matrix, matrix, vector, vector, matrix, vector)
        + (matrix, matrix, matrix, matrix, vector),
        out_specs=(tokens, tokens, vector, matrix, matrix, matrix, vector, vector, matrix, vector)
        + (matrix, matrix, matrix),
        check_vma=False,
    )
```
